256 devices in a mesh: dp: 8 (over y, z_hi), expert: 32 (over x, z_lo, core).
Axes of the slice: x: 4, y: 4, z: 8 (z_hi: 2, z_lo: 4; z = z_hi * 4 + z_lo), core: 2. Of those that a mesh axis runs over, the one named last changes fastest.
Arguments:
- token_blocks: bfloat16 [256, 128, 6144], P('expert', 'dp'), may hold values from -6 to 6
- output_grads: bfloat16 [256, 128, 6144], P('expert', 'dp'), may hold values from -0.1875 to 0.1875
- replica_weights: bfloat16 [32, 3, 144, 6144], P('expert'), as said below
- replica_counts: int32 [8], replicated, may hold values from 1 to 8, as said below
- replica_column: int32 [32], replicated, may hold values from 0 to 31, as said below
- block_dest: int32 [32, 8], replicated, may hold values from 0 to 31, as said below
- block_counts: int32 [32], replicated, may hold values from 3 to 8, as said below
Outputs:
- expert_grads: bfloat16 [8, 3, 144, 6144], P(None, None, 'dp', 'expert')
The draws below stay inside these ranges and needn't reach their ends.
Inputs may be any that keep to these rules, and one draw needn't show every extreme that they name: `replica_counts`: the replica counts sum to 32. `replica_column`: A permutation of the expert-axis indices; replicas are numbered expert by expert: the first replica_counts[0] replicas belong to expert 0, the next replica_counts[1] to expert 1, and so on. `replica_weights`: replicas of one expert hold equal weights. `block_dest`: the slots of one expert-axis index go to different replicas, and for each k the 32 indices send their k-th slots to different replicas; so a replica receives at most 8 live slots, and some replica receives exactly that many. `block_counts`: slots k below the count are live; the others are ignored.
All inputs are finite; a program needn't handle non-finite values.
Results may differ from the reference program's by a relative error of at most 0.0049.
Values may be sent and summed in bfloat16 or wider, within the bound.
A program may use at most 128 MiB of HBM per device.

```python
import jax
import jax.numpy as jnp
from jax import lax

D = 6144
EXPERTS = 8
F_DEV = 144
BLOCK = 128
BLK_COL = 8
SLOTS = 256
N_EXPERT = 32


def replica_layout(key):
    layout_key = jax.random.fold_in(key, 11)
    order_key, fill_key, place_key = jax.random.split(layout_key, 3)
    surplus = N_EXPERT - EXPERTS
    highest = min(7, surplus)
    expert_order = jax.random.permutation(order_key, EXPERTS)
    expert_ids = jnp.arange(EXPERTS, dtype=jnp.int32)
    counts = jnp.full((EXPERTS,), 1, jnp.int32).at[expert_order[0]].add(highest)

    def add_one(count_step, current):
        scores = jax.random.randint(jax.random.fold_in(fill_key, count_step), (EXPERTS,), 0, 1 << 20) * EXPERTS + expert_ids
        eligible = (current < 8) & (expert_ids != expert_order[0]) & (expert_ids != expert_order[1])
        chosen = jnp.argmax(jnp.where(eligible, scores, -1))
        return current.at[chosen].add(1)
    counts = lax.fori_loop(0, surplus - highest, add_one, counts)
    placement = jax.random.permutation(place_key, N_EXPERT).astype(jnp.int32)
    cumulative = jnp.cumsum(counts)
    replica_ids = jnp.arange(N_EXPERT, dtype=jnp.int32)
    replica_expert = jnp.sum((cumulative[None, :] <= replica_ids[:, None]).astype(jnp.int32), axis=1)
    column_expert = jnp.zeros((N_EXPERT,), jnp.int32).at[placement].set(replica_expert)
    return (counts.astype(jnp.int32), placement, column_expert)


def block_routing(key):
    route_key = jax.random.fold_in(key, 23)
    perm_key, anchor_key, count_key = jax.random.split(route_key, 3)
    relabel = jax.random.permutation(perm_key, N_EXPERT).astype(jnp.int32)
    anchor = jax.random.randint(anchor_key, (), 0, N_EXPERT)
    column_ids = jnp.arange(N_EXPERT, dtype=jnp.int32)
    lowest = max(1, 3 * BLK_COL // 8)
    drawn = jax.random.randint(count_key, (N_EXPERT,), lowest, BLK_COL + 1)
    behind = (anchor - column_ids) % N_EXPERT
    raised = jnp.where(behind < BLK_COL, jnp.maximum(drawn, behind + 1), drawn)
    counts = jnp.where(behind == 0, lowest, raised)
    slot_ids = jnp.arange(BLK_COL, dtype=jnp.int32)
    targets = relabel[(column_ids[:, None] + slot_ids[None, :]) % N_EXPERT]
    return (counts.astype(jnp.int32), targets.astype(jnp.int32))


def draw_replica_weights(key, part):
    layout = replica_layout(key)
    key = jax.random.fold_in(key, 5)
    base = jax.random.normal(key, (EXPERTS, 3, F_DEV, D), jnp.float32)
    base = base * D ** (-0.5)
    return base[layout[2]].astype(jnp.bfloat16)


def draw_replica_counts(key, part):
    layout = replica_layout(key)
    return layout[0]


def draw_replica_column(key, part):
    layout = replica_layout(key)
    return layout[1]


def draw_block_dest(key, part):
    routing = block_routing(key)
    return routing[1]


def draw_block_counts(key, part):
    routing = block_routing(key)
    return routing[0]


def steps_of(own_key, extent, cuts, least, largest):
    level, own = 1.0, jax.random.fold_in(own_key, 6)
    for axis_at, shards_of in cuts:
        draws = jnp.exp(jax.random.uniform(jax.random.fold_in(own, axis_at), (shards_of,), jnp.float32, least / len(cuts), largest / len(cuts)))
        level = level * jnp.repeat(draws, extent[axis_at] // shards_of).reshape([-1 if axis == axis_at else 1 for axis in range(len(extent))])
    return level


def normal_values(key, shape, width, most, pieces=(), kind=jnp.bfloat16):
    loudness = steps_of(key, shape, pieces, -0.22, 0.18) if pieces else 1.0
    array = jax.random.normal(key, shape, jnp.float32) * width * loudness
    return jnp.minimum(jnp.maximum(array, -most), most).astype(kind)


def setup_inputs(seed: int = 0) -> dict:
    keys = jax.random.split(jax.random.key(seed), 8)
    return {
        "token_blocks": normal_values(keys[0], (SLOTS, BLOCK, D), 1.0, 6.0, ((0, 32), (1, 8))),
        "output_grads": normal_values(keys[1], (SLOTS, BLOCK, D), 0.03, 0.1875, ((0, 32), (1, 8))),
        "replica_weights": draw_replica_weights(jax.random.fold_in(keys[7], 71), 0),
        "replica_counts": draw_replica_counts(jax.random.fold_in(keys[7], 71), 0),
        "replica_column": draw_replica_column(jax.random.fold_in(keys[7], 71), 0),
        "block_dest": draw_block_dest(jax.random.fold_in(keys[7], 71), 0),
        "block_counts": draw_block_counts(jax.random.fold_in(keys[7], 71), 0),
    }


def swiglu_grads(inputs, cotangents, weights):
    gate_rows = jnp.dot(inputs, weights[0].T, preferred_element_type=jnp.float32)
    up_rows = jnp.dot(inputs, weights[1].T, preferred_element_type=jnp.float32)
    gate_sig = jax.nn.sigmoid(gate_rows)
    activated = gate_rows * gate_sig
    hidden = (activated * up_rows).astype(jnp.bfloat16)
    hidden_grad = jnp.dot(cotangents, weights[2].T, preferred_element_type=jnp.float32)
    gate_grad = (hidden_grad * up_rows * gate_sig * (1.0 + gate_rows * (1.0 - gate_sig))).astype(jnp.bfloat16)
    up_grad = (hidden_grad * activated).astype(jnp.bfloat16)
    first = jnp.dot(gate_grad.T, inputs, preferred_element_type=jnp.float32)
    second = jnp.dot(up_grad.T, inputs, preferred_element_type=jnp.float32)
    third = jnp.dot(hidden.T, cotangents, preferred_element_type=jnp.float32)
    return jnp.stack([first, second, third])


def reference(token_blocks, output_grads, replica_weights, replica_counts, replica_column, block_dest, block_counts):
    replicas = replica_column.shape[0]
    slot_count = block_dest.shape[1]
    cumulative = jnp.cumsum(replica_counts)
    replica_ids = jnp.arange(replicas, dtype=jnp.int32)
    replica_expert = jnp.sum((cumulative[None, :] <= replica_ids[:, None]).astype(jnp.int32), axis=1)
    dest_flat = block_dest.reshape(-1)
    slot_ids = jnp.arange(slot_count, dtype=jnp.int32)
    live_flat = (slot_ids[None, :] < block_counts[:, None]).reshape(-1).astype(jnp.float32)

    def accumulate(totals, element):
        inputs, cotangents, target, alive = element
        column = replica_column[target]
        expert = replica_expert[target]
        weights = replica_weights[column]
        grads = swiglu_grads(inputs, cotangents, weights) * alive
        return totals.at[expert].add(grads), None

    start = jnp.zeros((EXPERTS, 3, replica_weights.shape[2], replica_weights.shape[3]), jnp.float32)
    totals, unused = lax.scan(accumulate, start, (token_blocks, output_grads, dest_flat, live_flat))
    return totals.astype(jnp.bfloat16)
```

```python
import jax
import jax.numpy as jnp
from jax import lax
from jax.experimental import pallas as pl
from jax.experimental.pallas import tpu as pltpu
from jax.sharding import PartitionSpec as P

MESH = pl.DeviceIdType.MESH
EXPERTS = 8
X, Y, Z = 4, 4, 8
GROUP = X * Y
D = 6144
DC = D // GROUP
SLOT = 8
ROWS = 16
MAIN = 128
TAIL = 16
LANES = 512
GROWS = 448
HALF = GROWS // 2
GRAN = Y * ROWS
NGRAN = X * SLOT
TILE = 256
PER_TILE = TILE // GRAN
MAX_TILES = NGRAN // PER_TILE + EXPERTS - 1
VMEM_LIMIT = 56 * 1024 * 1024


def coords():
    d = lax.axis_index("dp")
    c = lax.axis_index("expert")
    return c // 8, d // 2, (d % 2) * 4 + (c // 2) % 4, c % 2


def device(x, y, z, k):
    return (y * 2 + z // 4, (x * 4 + z % 4) * 2 + k)


def plane_peer(x, y, step):
    peer = (x * Y + y + step) % GROUP
    return peer // Y, peer % Y


def signal(sem, target):
    pl.semaphore_signal(sem, inc=1, device_id=target, device_id_type=MESH)


def remote(src, dst, send, recv, target):
    return pltpu.make_async_remote_copy(
        src_ref=src, dst_ref=dst, send_sem=send, recv_sem=recv, device_id=target, device_id_type=MESH
    )


def wait_bytes(ref, sem):
    pltpu.make_async_copy(ref, ref, sem).wait()


def spread_kernel(
    first_col, tok, cot, wts, xg, qg, wg, wr, sel, xs_sem, xr_sem, qs_sem, qr_sem, ws_sem, wr_sem, own_sem,
    rs_sem, rr_sem, ls_sem, lr_sem, ss_sem, sr_sem,
):
    x, y, z, k = coords()
    zh, zl = z // 4, z % 4
    me_col = (x * 4 + zl) * 2 + k
    barrier = pltpu.get_barrier_semaphore()

    def greet_plane(step, carry):
        px, py = plane_peer(x, y, step)
        signal(barrier, device(px, py, z, k))
        return carry

    def greet_column(step, carry):
        signal(barrier, (y * 2 + zh, (me_col + step) % 32))
        return carry

    lax.fori_loop(1, GROUP, greet_plane, 0)
    lax.fori_loop(1, 32, greet_column, 0)
    right, left = device(x, y, (z + 1) % Z, k), device(x, y, (z + Z - 1) % Z, k)
    sibling = device(x, y, z, 1 - k)
    signal(barrier, right)
    signal(barrier, left)
    pl.semaphore_wait(barrier, GROUP - 1 + 31 + 2)

    def weight_piece(col, part):
        cx, cz, ck = col // 8, zh * 4 + (col // 2) % 4, col % 2
        t = jnp.minimum((cz * 2 + ck) * 2 + part, 26)
        tail = t // 24
        m = (t // 8) * (1 - tail) + (t - 24) * tail
        row = (t % 8) * 16 * (1 - tail) + 128 * tail
        return wts.at[
            0,
            m,
            pl.ds(pl.multiple_of(row, 16), 16),
            pl.ds(pl.multiple_of((cx * Y + y) * DC, 128), DC),
        ]

    def send_weights(step, carry):
        col = (me_col + step) % 32
        for part in range(2):
            remote(
                weight_piece(col, part), wr.at[me_col, pl.ds(part * 16, 16), :], ws_sem, wr_sem, (y * 2 + zh, col)
            ).start()
        return carry

    lax.fori_loop(1, 32, send_weights, 0)
    for part in range(2):
        pltpu.make_async_copy(
            weight_piece(me_col, part), wr.at[me_col, pl.ds(part * 16, 16), :], wr_sem
        ).start()

    def columns(ref, px, py):
        return ref.at[:, :, pl.ds(pl.multiple_of((px * Y + py) * DC, 128), DC)]

    def send_rows(step, carry):
        px, py = plane_peer(x, y, step)
        target = device(px, py, z, k)
        remote(columns(tok, px, py), xg.at[x, :, y], xs_sem.at[step], xr_sem.at[step], target).start()
        remote(columns(cot, px, py), qg.at[x, :, y], qs_sem.at[step], qr_sem.at[step], target).start()
        return carry

    lax.fori_loop(1, GROUP, send_rows, 0)
    own_x = pltpu.make_async_copy(columns(tok, x, y), xg.at[x, :, y], own_sem.at[0])
    own_q = pltpu.make_async_copy(columns(cot, x, y), qg.at[x, :, y], own_sem.at[1])
    own_x.start()
    own_q.start()

    wait_bytes(wr, wr_sem)
    for e in range(EXPERTS):
        sel[e] = wr[first_col[e]]

    def chunk(pz):
        return wg.at[:, pl.ds(pl.multiple_of((pz * 2 + k) * 32, 32), 32), :]

    mine = chunk(z)
    own_w = pltpu.make_async_copy(sel, mine, own_sem.at[2])
    own_w.start()
    rights = [remote(sel, mine, rs_sem.at[0], rr_sem.at[0], right)]
    lefts = [remote(sel, mine, ls_sem.at[0], lr_sem.at[0], left)]
    sibs = [remote(sel, mine, ss_sem.at[0], sr_sem.at[0], sibling)]
    rights[0].start()
    lefts[0].start()
    sibs[0].start()
    for t in range(1, 5):
        rights[t - 1].wait_recv()
        piece = chunk((z + Z - t) % Z)
        if t < 4:
            go = remote(piece, piece, rs_sem.at[t], rr_sem.at[t], right)
            go.start()
            rights.append(go)
        go = remote(piece, piece, ss_sem.at[2 * t - 1], sr_sem.at[2 * t - 1], sibling)
        go.start()
        sibs.append(go)
        if t < 4:
            lefts[t - 1].wait_recv()
            piece = chunk((z + t) % Z)
            if t < 3:
                go = remote(piece, piece, ls_sem.at[t], lr_sem.at[t], left)
                go.start()
                lefts.append(go)
            go = remote(piece, piece, ss_sem.at[2 * t], sr_sem.at[2 * t], sibling)
            go.start()
            sibs.append(go)
    for go in sibs:
        go.wait_recv()
    for go in rights + lefts + sibs:
        go.wait_send()
    own_w.wait()
    wait_bytes(wr.at[pl.ds(0, 31)], ws_sem)

    def finish(step, carry):
        px, py = plane_peer(x, y, step)
        target = device(px, py, z, k)
        remote(columns(tok, px, py), xg.at[x, :, y], xs_sem.at[step], xr_sem.at[step], target).wait()
        remote(columns(cot, px, py), qg.at[x, :, y], qs_sem.at[step], qr_sem.at[step], target).wait()
        return carry

    lax.fori_loop(1, GROUP, finish, 0)
    own_x.wait()
    own_q.wait()


def spread(first_col, tok, cot, wts):
    hbm = pl.BlockSpec(memory_space=pl.ANY)
    dma = pltpu.SemaphoreType.DMA
    return pl.pallas_call(
        spread_kernel,
        out_shape=(
            jax.ShapeDtypeStruct((X, SLOT, Y, ROWS, DC), jnp.bfloat16),
            jax.ShapeDtypeStruct((X, SLOT, Y, ROWS, DC), jnp.bfloat16),
            jax.ShapeDtypeStruct((EXPERTS, LANES, DC), jnp.bfloat16),
        ),
        in_specs=[pl.BlockSpec(memory_space=pltpu.SMEM), hbm, hbm, hbm],
        out_specs=(hbm, hbm, hbm),
        scratch_shapes=[
            pltpu.VMEM((32, 32, DC), jnp.bfloat16),
            pltpu.VMEM((EXPERTS, 32, DC), jnp.bfloat16),
            dma((GROUP,)),
            dma((GROUP,)),
            dma((GROUP,)),
            dma((GROUP,)),
            dma,
            dma,
            dma((3,)),
            dma((4,)),
            dma((4,)),
            dma((3,)),
            dma((3,)),
            dma((8,)),
            dma((8,)),
        ],
        compiler_params=pltpu.CompilerParams(
            collective_id=0, has_side_effects=True, vmem_limit_bytes=VMEM_LIMIT
        ),
        name="spread",
    )(first_col, tok, cot, wts)


def place_granules(gexp, pos, owner):
    def clear(t, carry):
        owner[t] = 0
        return carry

    lax.fori_loop(0, MAX_TILES + 1, clear, 0)

    def one_expert(e, tile):
        def one_granule(g, count):
            hit = gexp[g] == e

            @pl.when(hit)
            def _():
                pos[g] = tile * PER_TILE + count

            return count + hit.astype(jnp.int32)

        count = lax.fori_loop(0, NGRAN, one_granule, 0)
        tiles = (count + PER_TILE - 1) // PER_TILE

        def name_tile(t, carry):
            owner[t] = e
            return carry

        lax.fori_loop(tile, tile + tiles, name_tile, 0)
        return tile + tiles

    used = lax.fori_loop(0, EXPERTS, one_expert, 0)

    def dead(g, carry):
        @pl.when(gexp[g] >= EXPERTS)
        def _():
            pos[g] = MAX_TILES * PER_TILE

        return carry

    lax.fori_loop(0, NGRAN, dead, 0)
    return used


def dot_nt(a, b):
    return lax.dot_general(a, b, (((1,), (1,)), ((), ())), preferred_element_type=jnp.float32)


def dot_tn(a, b):
    return lax.dot_general(a, b, (((0,), (0,)), ((), ())), preferred_element_type=jnp.float32)


def sort_rows(pos, pairs):
    for _, packed in pairs:
        packed[...] = jnp.zeros_like(packed)

    def move(g, carry):
        at = pl.ds(pl.multiple_of(pos[g] * GRAN, GRAN), GRAN)
        for source, packed in pairs:
            packed[at] = source[g]
        return carry

    lax.fori_loop(0, NGRAN, move, 0)


def project_kernel(gexp, xg, qg, wg, part, xs, qs, ps, pos, owner):
    used = place_granules(gexp, pos, owner)
    sort_rows(pos, [(xg, xs), (qg, qs)])
    in_tail = lax.broadcasted_iota(jnp.int32, (TILE, MAIN), 1) < 2 * TAIL

    def tile_step(t, carry):
        at = pl.ds(pl.multiple_of(t * TILE, TILE), TILE)
        e = owner[t]
        xt, qt = xs[at], qs[at]
        ps[at, 0 : 2 * MAIN] = dot_nt(xt, wg[e, 0 : 2 * MAIN]).astype(jnp.bfloat16)
        x_tail = dot_nt(xt, wg[e, 3 * MAIN : LANES])
        q_all = dot_nt(qt, wg[e, 2 * MAIN : LANES])
        ps[at, 2 * MAIN : 3 * MAIN] = q_all[:, :MAIN].astype(jnp.bfloat16)
        ps[at, 3 * MAIN : LANES] = jnp.where(in_tail, x_tail, q_all[:, MAIN:]).astype(jnp.bfloat16)
        return carry

    lax.fori_loop(0, used, tile_step, 0)

    def put_back(g, carry):
        rows = ps[pl.ds(pl.multiple_of(pos[g] * GRAN, GRAN), GRAN)]
        for py in range(Y):
            part[g // SLOT, py, g % SLOT] = rows[py * ROWS : (py + 1) * ROWS]
        return carry

    lax.fori_loop(0, NGRAN, put_back, 0)


def project(gexp, xg, qg, wg):
    vmem = pl.BlockSpec(memory_space=pltpu.VMEM)
    packed = (MAX_TILES + 1) * TILE
    return pl.pallas_call(
        project_kernel,
        out_shape=jax.ShapeDtypeStruct((X, Y, SLOT, ROWS, LANES), jnp.bfloat16),
        in_specs=[pl.BlockSpec(memory_space=pltpu.SMEM), vmem, vmem, vmem],
        out_specs=vmem,
        scratch_shapes=[
            pltpu.VMEM((packed, DC), jnp.bfloat16),
            pltpu.VMEM((packed, DC), jnp.bfloat16),
            pltpu.VMEM((packed, LANES), jnp.bfloat16),
            pltpu.SMEM((NGRAN,), jnp.int32),
            pltpu.SMEM((MAX_TILES + 1,), jnp.int32),
        ],
        compiler_params=pltpu.CompilerParams(vmem_limit_bytes=VMEM_LIMIT),
        name="project",
    )(gexp, xg, qg, wg)


def swiglu_rows(gate, up, grad):
    sig = jax.nn.sigmoid(gate)
    act = gate * sig
    return grad * up * sig * (1.0 + gate * (1.0 - sig)), grad * act, act * up


def hidden_kernel(part, hg, got, hid, ps_sem, pr_sem, hs_sem, hr_sem, own_sem):
    x, y, z, k = coords()
    me = x * Y + y
    barrier = pltpu.get_barrier_semaphore()

    def greet(step, carry):
        px, py = plane_peer(x, y, step)
        signal(barrier, device(px, py, z, k))
        return carry

    lax.fori_loop(1, GROUP, greet, 0)
    pl.semaphore_wait(barrier, GROUP - 1)

    def partial_copy(step):
        px, py = plane_peer(x, y, step)
        return remote(
            part.at[px * Y + py], got.at[me], ps_sem.at[step], pr_sem.at[step], device(px, py, z, k)
        )

    def send_partial(step, carry):
        partial_copy(step).start()
        return carry

    lax.fori_loop(1, GROUP, send_partial, 0)
    own = pltpu.make_async_copy(part.at[me], got.at[me], own_sem.at[0])
    own.start()
    own.wait()

    def wait_partial(step, carry):
        partial_copy(step).wait()
        return carry

    lax.fori_loop(1, GROUP, wait_partial, 0)

    lane = lax.broadcasted_iota(jnp.int32, (SLOT * ROWS, MAIN), 1)

    def total(lo):
        out = got[0, :, lo : lo + MAIN].astype(jnp.float32)
        for s in range(1, GROUP):
            out += got[s, :, lo : lo + MAIN].astype(jnp.float32)
        return out

    def shift(v, amount):
        return pltpu.roll(v, amount % MAIN, 1)

    def put(lo, value):
        hid[:, :, lo : lo + MAIN] = value.astype(jnp.bfloat16).reshape(SLOT, ROWS, MAIN)

    for at, value in enumerate(swiglu_rows(total(0), total(MAIN), total(2 * MAIN))):
        put(at * MAIN, value)
    tail = total(3 * MAIN)
    first, second, third = swiglu_rows(tail, shift(tail, -TAIL), shift(tail, -2 * TAIL))
    packed = jnp.where(
        lane < TAIL, first, jnp.where(lane < 2 * TAIL, shift(second, TAIL), shift(third, 2 * TAIL))
    )
    put(3 * MAIN, jnp.where(lane < 3 * TAIL, packed, 0.0))

    def hidden_copy(step):
        px, py = plane_peer(x, y, step)
        return remote(hid, hg.at[x, :, y], hs_sem.at[step], hr_sem.at[step], device(px, py, z, k))

    def send_hidden(step, carry):
        hidden_copy(step).start()
        return carry

    lax.fori_loop(1, GROUP, send_hidden, 0)
    keep = pltpu.make_async_copy(hid, hg.at[x, :, y], own_sem.at[1])
    keep.start()
    keep.wait()

    def wait_hidden(step, carry):
        hidden_copy(step).wait()
        return carry

    lax.fori_loop(1, GROUP, wait_hidden, 0)


def hidden(part):
    hbm = pl.BlockSpec(memory_space=pl.ANY)
    dma = pltpu.SemaphoreType.DMA
    return pl.pallas_call(
        hidden_kernel,
        out_shape=jax.ShapeDtypeStruct((X, SLOT, Y, ROWS, LANES), jnp.bfloat16),
        in_specs=[hbm],
        out_specs=hbm,
        scratch_shapes=[
            pltpu.VMEM((GROUP, SLOT * ROWS, LANES), jnp.bfloat16),
            pltpu.VMEM((SLOT, ROWS, LANES), jnp.bfloat16),
            dma((GROUP,)),
            dma((GROUP,)),
            dma((GROUP,)),
            dma((GROUP,)),
            dma((2,)),
        ],
        compiler_params=pltpu.CompilerParams(
            collective_id=1, has_side_effects=True, vmem_limit_bytes=VMEM_LIMIT
        ),
        name="hidden",
    )(part)


def grads_kernel(gexp, xg, qg, hg, acc, xs, qs, hs, pos, owner):
    used = place_granules(gexp, pos, owner)
    sort_rows(pos, [(xg, xs), (qg, qs), (hg, hs)])
    acc[...] = jnp.zeros_like(acc)
    tail_rows = GROWS - 3 * MAIN
    from_x = lax.broadcasted_iota(jnp.int32, (tail_rows, DC), 0) < 2 * TAIL

    def tile_step(t, carry):
        at = pl.ds(pl.multiple_of(t * TILE, TILE), TILE)
        e = owner[t]
        xt, qt = xs[at], qs[at]
        acc[e, 0 : 2 * MAIN] += dot_tn(hs[at, 0 : 2 * MAIN], xt)
        acc[e, 2 * MAIN : 3 * MAIN] += dot_tn(hs[at, 2 * MAIN : 3 * MAIN], qt)
        tail = hs[at, 3 * MAIN : LANES]
        x_tail, q_tail = dot_tn(tail, xt), dot_tn(tail, qt)
        acc[e, 3 * MAIN : GROWS] += jnp.where(from_x, x_tail[:tail_rows], q_tail[:tail_rows])
        return carry

    lax.fori_loop(0, used, tile_step, 0)


def gradients(gexp, xg, qg, hg):
    vmem = pl.BlockSpec(memory_space=pltpu.VMEM)
    packed = (MAX_TILES + 1) * TILE
    return pl.pallas_call(
        grads_kernel,
        out_shape=jax.ShapeDtypeStruct((EXPERTS, GROWS, DC), jnp.float32),
        in_specs=[pl.BlockSpec(memory_space=pltpu.SMEM), vmem, vmem, vmem],
        out_specs=vmem,
        scratch_shapes=[
            pltpu.VMEM((packed, DC), jnp.bfloat16),
            pltpu.VMEM((packed, DC), jnp.bfloat16),
            pltpu.VMEM((packed, LANES), jnp.bfloat16),
            pltpu.SMEM((NGRAN,), jnp.int32),
            pltpu.SMEM((MAX_TILES + 1,), jnp.int32),
        ],
        compiler_params=pltpu.CompilerParams(vmem_limit_bytes=VMEM_LIMIT),
        name="gradients",
    )(gexp, xg, qg, hg)


def reduce_kernel(grads, out, sib, own, mix, got, send, recv, own_sem, rs_sem, rr_sem):
    x, y, z, k = coords()
    sibling = device(x, y, z, 1 - k)
    barrier = pltpu.get_barrier_semaphore()
    signal(barrier, sibling)

    def greet(step, carry):
        signal(barrier, device(x, y, (z + step) % Z, k))
        return carry

    lax.fori_loop(1, Z, greet, 0)
    pl.semaphore_wait(barrier, Z)

    def half(ref, which):
        return ref.at[:, pl.ds(pl.multiple_of(which * HALF, HALF), HALF), :]

    trade = remote(half(grads, 1 - k), sib, send.at[0], recv.at[0], sibling)
    trade.start()
    keep = pltpu.make_async_copy(half(grads, k), own, own_sem)
    keep.start()
    keep.wait()
    trade.wait()

    def spread_copy(step):
        pz = (z + step) % Z
        return remote(mix.at[pz], got.at[z], rs_sem.at[step], rr_sem.at[step], device(x, y, pz, k))

    def send_sum(step, carry):
        pz = (z + step) % Z
        mix[pz] = (own[pz] + sib[pz]).astype(jnp.bfloat16)
        spread_copy(step).start()
        return carry

    lax.fori_loop(1, Z, send_sum, 0)
    got[z] = (own[z] + sib[z]).astype(jnp.bfloat16)

    def wait_sum(step, carry):
        spread_copy(step).wait()
        return carry

    lax.fori_loop(1, Z, wait_sum, 0)
    value = got[0].astype(jnp.float32)
    for s in range(1, Z):
        value += got[s].astype(jnp.float32)
    mine = out.at[pl.ds(pl.multiple_of(k * HALF, HALF), HALF), :]
    mine[...] = value.astype(jnp.bfloat16)
    swap = remote(mine, mine, send.at[1], recv.at[1], sibling)
    swap.start()
    swap.wait()


def reduce_grads(grads):
    dma = pltpu.SemaphoreType.DMA
    half = pltpu.VMEM((EXPERTS, HALF, DC), jnp.bfloat16)
    wide = pltpu.VMEM((EXPERTS, HALF, DC), jnp.float32)
    return pl.pallas_call(
        reduce_kernel,
        out_shape=jax.ShapeDtypeStruct((GROWS, DC), jnp.bfloat16),
        in_specs=[pl.BlockSpec(memory_space=pl.ANY)],
        out_specs=pl.BlockSpec(memory_space=pltpu.VMEM),
        scratch_shapes=[wide, wide, half, half, dma((2,)), dma((2,)), dma, dma((Z,)), dma((Z,))],
        compiler_params=pltpu.CompilerParams(
            collective_id=2, has_side_effects=True, vmem_limit_bytes=VMEM_LIMIT
        ),
        name="reduce_grads",
    )(grads)


PACK = 96


def deal_kernel(pieces, out, send, recv, own_sem):
    x, y, z, k = coords()
    zh, zl = z // 4, z % 4
    barrier = pltpu.get_barrier_semaphore()

    def target(share):
        return share // 2, (share % 2) * 4 + y

    def source(pz):
        return zl, pz

    def greet_share(share, carry):
        ty, tz = target(share)

        @pl.when((ty != y) | (tz != z))
        def _():
            signal(barrier, device(x, ty, tz, k))

        return carry

    def greet_source(pz, carry):
        @pl.when((zl != y) | (pz != z))
        def _():
            signal(barrier, device(x, zl, pz, k))

        return carry

    lax.fori_loop(0, 8, greet_share, 0)
    lax.fori_loop(0, 8, greet_source, 0)
    self_here = jnp.where(zl == y, 1, 0)
    pl.semaphore_wait(barrier, 16 - 2 * self_here)
    mine = y * 2 + zh

    def start(share, carry):
        ty, tz = target(share)

        @pl.when((ty != y) | (tz != z))
        def _():
            remote(pieces.at[share], out.at[z], send.at[share], recv.at[z], device(x, ty, tz, k)).start()

        @pl.when((ty == y) & (tz == z))
        def _():
            pltpu.make_async_copy(pieces.at[share], out.at[z], own_sem).start()

        return carry

    def finish_send(share, carry):
        ty, tz = target(share)

        @pl.when((ty != y) | (tz != z))
        def _():
            remote(
                pieces.at[share], out.at[z], send.at[share], recv.at[z], device(x, ty, tz, k)
            ).wait_send()

        @pl.when((ty == y) & (tz == z))
        def _():
            pltpu.make_async_copy(pieces.at[share], out.at[z], own_sem).wait()

        return carry

    def finish_recv(pz, carry):
        @pl.when((zl != y) | (pz != z))
        def _():
            pltpu.make_async_copy(out.at[pz], out.at[pz], recv.at[pz]).wait()

        return carry

    lax.fori_loop(0, 8, start, 0)
    lax.fori_loop(0, 8, finish_send, 0)
    lax.fori_loop(0, 8, finish_recv, 0)


def deal(pieces):
    dma = pltpu.SemaphoreType.DMA
    vmem = pl.BlockSpec(memory_space=pltpu.VMEM)
    return pl.pallas_call(
        deal_kernel,
        out_shape=jax.ShapeDtypeStruct((EXPERTS, PACK, 128), jnp.bfloat16),
        in_specs=[vmem],
        out_specs=vmem,
        scratch_shapes=[dma((8,)), dma((8,)), dma],
        compiler_params=pltpu.CompilerParams(
            collective_id=3, has_side_effects=True, vmem_limit_bytes=VMEM_LIMIT
        ),
        name="deal",
    )(pieces)


def on_device(tok, cot, wts, counts, column, dest, live):
    c = lax.axis_index("expert")
    in_plane = c % 8
    ids = jnp.arange(EXPERTS, dtype=jnp.int32)
    cumulative = jnp.sum(jnp.where(ids[None, :] <= ids[:, None], counts[None, :], 0), axis=1)
    first = cumulative - counts
    replicas = jnp.arange(32, dtype=jnp.int32)
    first_col = jnp.sum(jnp.where(replicas[None, :] == first[:, None], column[None, :], 0), axis=1)
    my_dest = lax.dynamic_index_in_dim(dest.reshape(X, 8, SLOT), in_plane, 1, keepdims=False)
    my_live = lax.dynamic_index_in_dim(live.reshape(X, 8), in_plane, 1, keepdims=False)
    expert = jnp.sum((cumulative[None, None, :] <= my_dest[:, :, None]).astype(jnp.int32), axis=2)
    slots = jnp.arange(SLOT, dtype=jnp.int32)
    gexp = jnp.where(slots[None, :] < my_live[:, None], expert, EXPERTS).reshape(NGRAN)

    xg, qg, wg = spread(first_col, tok, cot, wts)
    xg = xg.reshape(NGRAN, GRAN, DC)
    qg = qg.reshape(NGRAN, GRAN, DC)
    part = project(gexp, xg, qg, wg)
    hg = hidden(part.reshape(GROUP, SLOT * ROWS, LANES)).reshape(NGRAN, GRAN, LANES)
    grads = reduce_grads(gradients(gexp, xg, qg, hg))

    main = grads[: 3 * MAIN].reshape(3, MAIN, DC)
    rest = grads[3 * MAIN : 3 * MAIN + 3 * TAIL].reshape(3, TAIL, DC)
    whole = jnp.concatenate([main, rest], axis=1)
    ours = lax.dynamic_slice_in_dim(whole, (c % 2) * (DC // 2), DC // 2, 2)
    shares = ours.reshape(3, 8, 18, DC // 2).transpose(1, 0, 2, 3).reshape(8, 81, 128)
    pieces = jnp.pad(shares, ((0, 0), (0, PACK - 81), (0, 0)))
    return deal(pieces)[:, :81].reshape(EXPERTS, 3, 18, DC // 2)


def solution(mesh):
    placed = (
        P("expert", "dp", None),
        P("expert", "dp", None),
        P("expert", None, None, None),
        P(),
        P(),
        P(),
        P(),
    )
    return jax.shard_map(
        on_device,
        mesh=mesh,
        in_specs=placed,
        out_specs=P(None, None, "dp", "expert"),
        check_vma=False,
    )
```

```python
import jax
import jax.numpy as jnp
from jax import lax
from jax.experimental import pallas as pl
from jax.experimental.pallas import tpu as pltpu
from jax.sharding import PartitionSpec as P

MESH = pl.DeviceIdType.MESH
EXPERTS = 8
X, Y, Z = 4, 4, 8
GROUP = X * Y
D = 6144
DC = D // GROUP
SLOT = 8
ROWS = 16
MAIN = 128
TAIL = 16
LANES = 512
GROWS = 448
HALF = GROWS // 2
GRAN = Y * ROWS
NGRAN = X * SLOT
TILE = 256
PER_TILE = TILE // GRAN
MAX_TILES = NGRAN // PER_TILE + EXPERTS - 1
VMEM_LIMIT = 56 * 1024 * 1024


def coords():
    d = lax.axis_index("dp")
    c = lax.axis_index("expert")
    return c // 8, d // 2, (d % 2) * 4 + (c // 2) % 4, c % 2


def device(x, y, z, k):
    return (y * 2 + z // 4, (x * 4 + z % 4) * 2 + k)


def plane_peer(x, y, step):
    peer = (x * Y + y + step) % GROUP
    return peer // Y, peer % Y


def signal(sem, target):
    pl.semaphore_signal(sem, inc=1, device_id=target, device_id_type=MESH)


def remote(src, dst, send, recv, target):
    return pltpu.make_async_remote_copy(
        src_ref=src, dst_ref=dst, send_sem=send, recv_sem=recv, device_id=target, device_id_type=MESH
    )


def wait_bytes(ref, sem):
    pltpu.make_async_copy(ref, ref, sem).wait()


def swiglu_rows(gate, up, grad):
    sig = jax.nn.sigmoid(gate)
    act = gate * sig
    return grad * up * sig * (1.0 + gate * (1.0 - sig)), grad * act, act * up


def place_granules(gexp, pos, owner, packed):
    def one_expert(e, tile):
        def one_granule(g, count):
            hit = gexp[g] == e

            @pl.when(hit)
            def _():
                pos[g] = tile * PER_TILE + count

            return count + hit.astype(jnp.int32)

        count = lax.fori_loop(0, NGRAN, one_granule, 0)
        tiles = (count + PER_TILE - 1) // PER_TILE

        def name_tile(t, carry):
            owner[t] = e
            return carry

        lax.fori_loop(tile, tile + tiles, name_tile, 0)

        def pad(g, carry):
            at = pl.ds(pl.multiple_of(g * GRAN, GRAN), GRAN)
            for ref in packed:
                ref[at] = jnp.zeros((GRAN, ref.shape[1]), ref.dtype)
            return carry

        lax.fori_loop(tile * PER_TILE + count, (tile + tiles) * PER_TILE, pad, 0)
        return tile + tiles

    used = lax.fori_loop(0, EXPERTS, one_expert, 0)

    def dead(g, carry):
        @pl.when(gexp[g] >= EXPERTS)
        def _():
            pos[g] = MAX_TILES * PER_TILE

        return carry

    lax.fori_loop(0, NGRAN, dead, 0)
    return used


def dot_nt(a, b):
    return lax.dot_general(a, b, (((1,), (1,)), ((), ())), preferred_element_type=jnp.float32)


def dot_tn(a, b):
    return lax.dot_general(a, b, (((0,), (0,)), ((), ())), preferred_element_type=jnp.float32)


def sort_rows(pos, pairs):
    def move(g, carry):
        at = pl.ds(pl.multiple_of(pos[g] * GRAN, GRAN), GRAN)
        for source, packed in pairs:
            packed[at] = source[g]
        return carry

    lax.fori_loop(0, NGRAN, move, 0)


CHUNKS = 2
PART = SLOT // CHUNKS
SUM_TYPE = jnp.float32


def rows_kernel(
    first_col, gexp, tok, cot, wts, xg, qg, hg, wr, sel, wg, xv, qv, p1, r1, s2, r2, hid, xs_sem, xr_sem, qs_sem, qr_sem,
    ws_sem, wr_sem, own_sem, rs_sem, rr_sem, ls_sem, lr_sem, ss_sem, sr_sem, p1s_sem, p1r_sem, p2s_sem, p2r_sem,
    has_sem, har_sem, hbs_sem, hbr_sem, keep_sem,
):
    x, y, z, k = coords()
    zh, zl = z // 4, z % 4
    me_col = (x * 4 + zl) * 2 + k
    barrier = pltpu.get_barrier_semaphore()

    def greet_plane(step, carry):
        px, py = plane_peer(x, y, step)
        signal(barrier, device(px, py, z, k))
        return carry

    def greet_column(step, carry):
        signal(barrier, (y * 2 + zh, (me_col + step) % 32))
        return carry

    lax.fori_loop(1, GROUP, greet_plane, 0)
    lax.fori_loop(1, 32, greet_column, 0)
    right, left = device(x, y, (z + 1) % Z, k), device(x, y, (z + Z - 1) % Z, k)
    sibling = device(x, y, z, 1 - k)
    signal(barrier, right)
    signal(barrier, left)
    pl.semaphore_wait(barrier, GROUP - 1 + 31 + 2)

    def weight_piece(col, part):
        cx, cz, ck = col // 8, zh * 4 + (col // 2) % 4, col % 2
        t = jnp.minimum((cz * 2 + ck) * 2 + part, 26)
        tail = t // 24
        m = (t // 8) * (1 - tail) + (t - 24) * tail
        row = (t % 8) * 16 * (1 - tail) + 128 * tail
        return wts.at[
            0,
            m,
            pl.ds(pl.multiple_of(row, 16), 16),
            pl.ds(pl.multiple_of((cx * Y + y) * DC, 128), DC),
        ]

    def send_weights(step, carry):
        col = (me_col + step) % 32
        for part in range(2):
            remote(
                weight_piece(col, part), wr.at[me_col, pl.ds(part * 16, 16), :], ws_sem, wr_sem, (y * 2 + zh, col)
            ).start()
        return carry

    lax.fori_loop(1, 32, send_weights, 0)
    for part in range(2):
        pltpu.make_async_copy(
            weight_piece(me_col, part), wr.at[me_col, pl.ds(part * 16, 16), :], wr_sem
        ).start()

    def columns(ref, px, py):
        return ref.at[:, :, pl.ds(pl.multiple_of((px * Y + py) * DC, 128), DC)]

    def x_copy(step):
        px, py = plane_peer(x, y, step)
        return remote(
            columns(tok, px, py), xv.at[x, :, y], xs_sem.at[step], xr_sem.at[step], device(px, py, z, k)
        )

    def q_copy(step):
        px, py = plane_peer(x, y, step)
        return remote(
            columns(cot, px, py), qv.at[x, :, y], qs_sem.at[step], qr_sem.at[step], device(px, py, z, k)
        )

    def start_x(step, carry):
        x_copy(step).start()
        return carry

    def start_q(step, carry):
        q_copy(step).start()
        return carry

    lax.fori_loop(1, GROUP, start_x, 0)
    own_x = pltpu.make_async_copy(columns(tok, x, y), xv.at[x, :, y], own_sem.at[0])
    own_q = pltpu.make_async_copy(columns(cot, x, y), qv.at[x, :, y], own_sem.at[1])
    own_x.start()
    own_q.start()

    wait_bytes(wr, wr_sem)
    for e in range(EXPERTS):
        sel[e] = wr[first_col[e]]

    def chunk(pz):
        return wg.at[:, pl.ds(pl.multiple_of((pz * 2 + k) * 32, 32), 32), :]

    mine = chunk(z)
    own_w = pltpu.make_async_copy(sel, mine, own_sem.at[2])
    own_w.start()
    rights = [remote(sel, mine, rs_sem.at[0], rr_sem.at[0], right)]
    lefts = [remote(sel, mine, ls_sem.at[0], lr_sem.at[0], left)]
    sibs = [remote(sel, mine, ss_sem.at[0], sr_sem.at[0], sibling)]
    rights[0].start()
    lefts[0].start()
    sibs[0].start()
    lax.fori_loop(1, GROUP, start_q, 0)
    for t in range(1, 5):
        rights[t - 1].wait_recv()
        piece = chunk((z + Z - t) % Z)
        if t < 4:
            go = remote(piece, piece, rs_sem.at[t], rr_sem.at[t], right)
            go.start()
            rights.append(go)
        go = remote(piece, piece, ss_sem.at[2 * t - 1], sr_sem.at[2 * t - 1], sibling)
        go.start()
        sibs.append(go)
        if t < 4:
            lefts[t - 1].wait_recv()
            piece = chunk((z + t) % Z)
            if t < 3:
                go = remote(piece, piece, ls_sem.at[t], lr_sem.at[t], left)
                go.start()
                lefts.append(go)
            go = remote(piece, piece, ss_sem.at[2 * t], sr_sem.at[2 * t], sibling)
            go.start()
            sibs.append(go)
    for go in sibs:
        go.wait_recv()
    own_w.wait()

    def wait_rows(step, carry):
        x_copy(step).wait()
        q_copy(step).wait()
        return carry

    lax.fori_loop(1, GROUP, wait_rows, 0)
    own_x.wait()
    own_q.wait()
    keep_x = pltpu.make_async_copy(xv, xg, keep_sem.at[0])
    keep_q = pltpu.make_async_copy(qv, qg, keep_sem.at[1])
    keep_x.start()
    keep_q.start()

    a_here, b_here = x * (1 - k) + y * k, x * k + y * (1 - k)

    def place(a, b):
        return a * (1 - k) + b * k, a * k + b * (1 - k)

    def plane_device(a, b):
        px, py = place(a, b)
        return device(px, py, z, k)

    def slots(h):
        return pl.ds(h * PART, PART)

    in_tail = lax.broadcasted_iota(jnp.int32, (GRAN, MAIN), 1) < 2 * TAIL

    def first_copy(h, j):
        a = (a_here + j) % 4
        at = h * 3 + j - 1
        return remote(
            p1.at[a, :, slots(h)], r1.at[a_here, :, slots(h)], p1s_sem.at[at], p1r_sem.at[at], plane_device(a, b_here)
        )

    def second_copy(h, j):
        b = (b_here + j) % 4
        at = h * 3 + j - 1
        return remote(
            s2.at[b, slots(h)], r2.at[b_here, slots(h)], p2s_sem.at[at], p2r_sem.at[at], plane_device(a_here, b)
        )

    def hidden_place(a, b, h):
        px, py = place(a, b)
        return hg.at[px, slots(h), py]

    def hidden_first(h, j):
        at = h * 3 + j - 1
        return remote(
            hid.at[slots(h)], hidden_place(a_here, b_here, h), has_sem.at[at], har_sem.at[at],
            plane_device((a_here + j) % 4, b_here),
        )

    def hidden_second(h, j, i):
        at = (h * 4 + j) * 3 + i - 1
        here = hidden_place((a_here + 4 - j) % 4, b_here, h)
        return remote(
            hid.at[slots(h)] if j == 0 else here, here, hbs_sem.at[at], hbr_sem.at[at],
            plane_device(a_here, (b_here + i) % 4),
        )

    for h in range(CHUNKS):

        def granule(i, carry):
            px, s = i // PART, h * PART + i % PART
            e = jnp.minimum(gexp[px * SLOT + s], EXPERTS - 1)
            xt = xv[px, s].reshape(GRAN, DC)
            qt = qv[px, s].reshape(GRAN, DC)
            x_main = dot_nt(xt, wg[e, 0 : 2 * MAIN]).astype(SUM_TYPE)
            x_tail = dot_nt(xt, wg[e, 3 * MAIN : LANES])
            q_all = dot_nt(qt, wg[e, 2 * MAIN : LANES])
            q_main = q_all[:, :MAIN].astype(SUM_TYPE)
            tail = jnp.where(in_tail, x_tail, q_all[:, MAIN:]).astype(SUM_TYPE)
            for py in range(Y):
                pa, pb = px * (1 - k) + py * k, px * k + py * (1 - k)
                cut = slice(py * ROWS, (py + 1) * ROWS)
                p1[pa, pb, s, :, 0 : 2 * MAIN] = x_main[cut]
                p1[pa, pb, s, :, 2 * MAIN : 3 * MAIN] = q_main[cut]
                p1[pa, pb, s, :, 3 * MAIN : LANES] = tail[cut]
            return carry

        lax.fori_loop(0, X * PART, granule, 0)
        for j in (2, 1, 3):
            first_copy(h, j).start()

    for h in range(CHUNKS):
        for j in (1, 2, 3):
            first_copy(h, j).wait_recv()

        def sum_first(b, carry):
            value = p1[a_here, b, h * PART : (h + 1) * PART].astype(jnp.float32)
            for j in (1, 2, 3):
                value += r1[(a_here + j) % 4, b, h * PART : (h + 1) * PART].astype(jnp.float32)
            s2[b, h * PART : (h + 1) * PART] = value
            return carry

        lax.fori_loop(0, 4, sum_first, 0)
        for j in (2, 1, 3):
            second_copy(h, j).start()

    lane = lax.broadcasted_iota(jnp.int32, (PART * ROWS, MAIN), 1)

    def shift(v, amount):
        return pltpu.roll(v, amount % MAIN, 1)

    for h in range(CHUNKS):
        for j in (1, 2, 3):
            second_copy(h, j).wait_recv()
        cut = slice(h * PART, (h + 1) * PART)

        def total(lo):
            value = s2[b_here, cut, :, lo : lo + MAIN]
            for j in (1, 2, 3):
                value += r2[(b_here + j) % 4, cut, :, lo : lo + MAIN]
            return value.reshape(PART * ROWS, MAIN)

        def put(lo, value):
            hid[cut, :, lo : lo + MAIN] = value.astype(jnp.bfloat16).reshape(PART, ROWS, MAIN)

        for at, value in enumerate(swiglu_rows(total(0), total(MAIN), total(2 * MAIN))):
            put(at * MAIN, value)
        tail = total(3 * MAIN)
        first, second, third = swiglu_rows(tail, shift(tail, -TAIL), shift(tail, -2 * TAIL))
        packed = jnp.where(
            lane < TAIL, first, jnp.where(lane < 2 * TAIL, shift(second, TAIL), shift(third, 2 * TAIL))
        )
        put(3 * MAIN, jnp.where(lane < 3 * TAIL, packed, 0.0))
        for j in (2, 1, 3):
            hidden_first(h, j).start()
        for i in (2, 1, 3):
            hidden_second(h, 0, i).start()
        pltpu.make_async_copy(hid.at[slots(h)], hidden_place(a_here, b_here, h), keep_sem.at[2 + h]).start()

    for h in range(CHUNKS):
        for j in (1, 3, 2):
            hidden_first(h, j).wait_recv()
            for i in (2, 1, 3):
                hidden_second(h, j, i).start()
    for h in range(CHUNKS):
        for j in range(4):
            for i in (1, 2, 3):
                hidden_second(h, j, i).wait()
        for j in (1, 2, 3):
            hidden_first(h, j).wait_send()
            first_copy(h, j).wait_send()
            second_copy(h, j).wait_send()
        pltpu.make_async_copy(hid.at[slots(h)], hidden_place(a_here, b_here, h), keep_sem.at[2 + h]).wait()
    for go in rights + lefts + sibs:
        go.wait_send()
    wait_bytes(wr.at[pl.ds(0, 31)], ws_sem)
    keep_x.wait()
    keep_q.wait()


def rows_and_hidden(first_col, gexp, tok, cot, wts):
    hbm = pl.BlockSpec(memory_space=pl.ANY)
    smem = pl.BlockSpec(memory_space=pltpu.SMEM)
    dma = pltpu.SemaphoreType.DMA
    spread = pltpu.VMEM((X, SLOT, Y, ROWS, DC), jnp.bfloat16)
    sums = pltpu.VMEM((4, 4, SLOT, ROWS, LANES), SUM_TYPE)
    halfway = pltpu.VMEM((4, SLOT, ROWS, LANES), jnp.float32)
    return pl.pallas_call(
        rows_kernel,
        out_shape=(
            jax.ShapeDtypeStruct((X, SLOT, Y, ROWS, DC), jnp.bfloat16),
            jax.ShapeDtypeStruct((X, SLOT, Y, ROWS, DC), jnp.bfloat16),
            jax.ShapeDtypeStruct((X, SLOT, Y, ROWS, LANES), jnp.bfloat16),
        ),
        in_specs=[smem, smem, hbm, hbm, hbm],
        out_specs=(hbm, hbm, hbm),
        scratch_shapes=[
            pltpu.VMEM((32, 32, DC), jnp.bfloat16),
            pltpu.VMEM((EXPERTS, 32, DC), jnp.bfloat16),
            pltpu.VMEM((EXPERTS, LANES, DC), jnp.bfloat16),
            spread,
            spread,
            sums,
            sums,
            halfway,
            halfway,
            pltpu.VMEM((SLOT, ROWS, LANES), jnp.bfloat16),
            dma((GROUP,)),
            dma((GROUP,)),
            dma((GROUP,)),
            dma((GROUP,)),
            dma,
            dma,
            dma((3,)),
            dma((4,)),
            dma((4,)),
            dma((3,)),
            dma((3,)),
            dma((8,)),
            dma((8,)),
            dma((3 * CHUNKS,)),
            dma((3 * CHUNKS,)),
            dma((3 * CHUNKS,)),
            dma((3 * CHUNKS,)),
            dma((3 * CHUNKS,)),
            dma((3 * CHUNKS,)),
            dma((12 * CHUNKS,)),
            dma((12 * CHUNKS,)),
            dma((2 + CHUNKS,)),
        ],
        compiler_params=pltpu.CompilerParams(
            collective_id=0, has_side_effects=True, vmem_limit_bytes=VMEM_LIMIT
        ),
        name="rows_and_hidden",
    )(first_col, gexp, tok, cot, wts)


def grads_kernel(gexp, xg, qg, hg, acc, xs, qs, hs, pos, owner):
    used = place_granules(gexp, pos, owner, [xs, qs, hs])
    sort_rows(pos, [(xg, xs), (qg, qs), (hg, hs)])
    acc[...] = jnp.zeros_like(acc)
    tail_rows = GROWS - 3 * MAIN
    from_x = lax.broadcasted_iota(jnp.int32, (tail_rows, DC), 0) < 2 * TAIL

    def tile_step(t, carry):
        at = pl.ds(pl.multiple_of(t * TILE, TILE), TILE)
        e = owner[t]
        xt, qt = xs[at], qs[at]
        acc[e, 0 : 2 * MAIN] += dot_tn(hs[at, 0 : 2 * MAIN], xt)
        acc[e, 2 * MAIN : 3 * MAIN] += dot_tn(hs[at, 2 * MAIN : 3 * MAIN], qt)
        tail = hs[at, 3 * MAIN : LANES]
        x_tail, q_tail = dot_tn(tail, xt), dot_tn(tail, qt)
        acc[e, 3 * MAIN : GROWS] += jnp.where(from_x, x_tail[:tail_rows], q_tail[:tail_rows])
        return carry

    lax.fori_loop(0, used, tile_step, 0)


def gradients(gexp, xg, qg, hg):
    vmem = pl.BlockSpec(memory_space=pltpu.VMEM)
    packed = (MAX_TILES + 1) * TILE
    return pl.pallas_call(
        grads_kernel,
        out_shape=jax.ShapeDtypeStruct((EXPERTS, GROWS, DC), jnp.float32),
        in_specs=[pl.BlockSpec(memory_space=pltpu.SMEM), vmem, vmem, vmem],
        out_specs=vmem,
        scratch_shapes=[
            pltpu.VMEM((packed, DC), jnp.bfloat16),
            pltpu.VMEM((packed, DC), jnp.bfloat16),
            pltpu.VMEM((packed, LANES), jnp.bfloat16),
            pltpu.SMEM((NGRAN,), jnp.int32),
            pltpu.SMEM((MAX_TILES + 1,), jnp.int32),
        ],
        compiler_params=pltpu.CompilerParams(vmem_limit_bytes=VMEM_LIMIT),
        name="gradients",
    )(gexp, xg, qg, hg)


QUART = HALF // 2
PACK = 64
WINDOW = 256
OFFSETS = (4, 3, -3, 2, -2, 1, -1, 0)


def reduce_kernel(
    grads, out, own, sib, sbuf, rbuf, fin, win, wide, pack, os_sem, ts_sem, tr_sem, cs_sem, cr_sem, swap_sem, send, recv,
    keep_sem,
):
    x, y, z, k = coords()
    zh, zl = z // 4, z % 4
    sibling = device(x, y, z, 1 - k)
    barrier = pltpu.get_barrier_semaphore()

    def target(share):
        return share // 2, (share % 2) * 4 + y

    def greet_share(share, carry):
        ty, tz = target(share)

        @pl.when((ty != y) | (tz != z))
        def _():
            signal(barrier, device(x, ty, tz, k))

        return carry

    def greet_source(pz, carry):
        @pl.when((zl != y) | (pz != z))
        def _():
            signal(barrier, device(x, zl, pz, k))

        return carry

    ahead = (device(x, y, (z + 1) % Z, k), device(x, y, (z + Z - 1) % Z, k))
    signal(barrier, sibling)
    signal(barrier, ahead[0])
    signal(barrier, ahead[1])
    lax.fori_loop(0, 8, greet_share, 0)
    lax.fori_loop(0, 8, greet_source, 0)
    self_here = jnp.where(zl == y, 1, 0)
    pl.semaphore_wait(barrier, 19 - 2 * self_here)

    def half(e, which):
        return grads.at[e, pl.ds(pl.multiple_of(which * HALF, HALF), HALF), :]

    trades, keeps = {}, {}
    for i, off in enumerate(OFFSETS):
        e = (z + off + Z) % Z
        trades[off] = remote(half(e, 1 - k), sib.at[e], ts_sem.at[i], tr_sem.at[i], sibling)
        keeps[off] = pltpu.make_async_copy(half(e, k), own.at[e], os_sem.at[i])
        trades[off].start()
        keeps[off].start()
    trades[-4], keeps[-4] = trades[4], keeps[4]
    ready = set()

    def ours(off, j):
        if abs(off) % 8 == 4:
            off = 4
        if off not in ready:
            trades[off].wait_recv()
            keeps[off].wait()
            ready.add(off)
        e = (z + off + Z) % Z
        cut = slice(j * QUART, (j + 1) * QUART)
        return own[e, cut] + sib[e, cut]

    chain = {}
    for dist in (4, 3, 2, 1):
        for way in range(2):
            for j in range(2):
                longest = 4 if way == j else 3
                if dist > longest:
                    continue
                value = ours(dist if way == 0 else -dist, j)
                if dist < longest:
                    chain[way, j, dist + 1].wait_recv()
                    value += rbuf[way, j, dist].astype(jnp.float32)
                sbuf[way, j, dist - 1] = value.astype(jnp.bfloat16)
                at = (way * 2 + j) * 4 + dist - 1
                go = remote(
                    sbuf.at[way, j, dist - 1], rbuf.at[way, j, dist - 1], cs_sem.at[at], cr_sem.at[at], ahead[way]
                )
                go.start()
                chain[way, j, dist] = go
    for j in range(2):
        value = ours(0, j)
        for way in range(2):
            chain[way, j, 1].wait_recv()
            value += rbuf[way, j, 0].astype(jnp.float32)
        fin[pl.ds(pl.multiple_of(k * HALF + j * QUART, 16), QUART)] = value
    mine = fin.at[pl.ds(pl.multiple_of(k * HALF, HALF), HALF)]
    swap = remote(mine, mine, swap_sem.at[0], swap_sem.at[1], sibling)
    swap.start()
    swap.wait()

    low = fin[:, 0:WINDOW]
    high = pltpu.roll(fin[:, DC - WINDOW : DC], DC // 2, 1)
    win[...] = jnp.where(k == 0, low, high)
    for share in range(8):
        wide[share, 48:PACK] = jnp.zeros((PACK - 48, WINDOW), jnp.float32)
        for m in range(3):
            if share < 7:
                lo = m * MAIN + 18 * share
                wide[share, 18 * m : 18 * m + 18] = win[lo : lo + 18]
            else:
                lo = m * MAIN + 126
                wide[share, 18 * m : 18 * m + 2] = win[lo : lo + 2]
                lo = 3 * MAIN + m * TAIL
                wide[share, 18 * m + 2 : 18 * m + 18] = win[lo : lo + TAIL]
        pack[share] = wide[share].astype(jnp.bfloat16)

    def share_copy(share):
        ty, tz = target(share)
        return remote(pack.at[share], out.at[z], send.at[share], recv.at[z], device(x, ty, tz, k))

    def start(share, carry):
        ty, tz = target(share)

        @pl.when((ty != y) | (tz != z))
        def _():
            share_copy(share).start()

        @pl.when((ty == y) & (tz == z))
        def _():
            pltpu.make_async_copy(pack.at[share], out.at[z], keep_sem).start()

        return carry

    def finish_send(share, carry):
        ty, tz = target(share)

        @pl.when((ty != y) | (tz != z))
        def _():
            share_copy(share).wait_send()

        @pl.when((ty == y) & (tz == z))
        def _():
            pltpu.make_async_copy(pack.at[share], out.at[z], keep_sem).wait()

        return carry

    def finish_recv(pz, carry):
        @pl.when((zl != y) | (pz != z))
        def _():
            pltpu.make_async_copy(out.at[pz], out.at[pz], recv.at[pz]).wait()

        return carry

    lax.fori_loop(0, 8, start, 0)
    lax.fori_loop(0, 8, finish_send, 0)
    lax.fori_loop(0, 8, finish_recv, 0)
    for off in OFFSETS:
        trades[off].wait_send()
    for go in chain.values():
        go.wait_send()


def reduce_grads(grads):
    dma = pltpu.SemaphoreType.DMA
    wide = pltpu.VMEM((EXPERTS, HALF, DC), jnp.float32)
    steps = pltpu.VMEM((2, 2, 4, QUART, DC), jnp.bfloat16)
    return pl.pallas_call(
        reduce_kernel,
        out_shape=jax.ShapeDtypeStruct((EXPERTS, PACK, WINDOW), jnp.bfloat16),
        in_specs=[pl.BlockSpec(memory_space=pl.ANY)],
        out_specs=pl.BlockSpec(memory_space=pltpu.VMEM),
        scratch_shapes=[
            wide,
            wide,
            steps,
            steps,
            pltpu.VMEM((GROWS, DC), jnp.float32),
            pltpu.VMEM((GROWS, WINDOW), jnp.float32),
            pltpu.VMEM((8, PACK, WINDOW), jnp.float32),
            pltpu.VMEM((8, PACK, WINDOW), jnp.bfloat16),
            dma((8,)),
            dma((8,)),
            dma((8,)),
            dma((16,)),
            dma((16,)),
            dma((2,)),
            dma((8,)),
            dma((8,)),
            dma,
        ],
        compiler_params=pltpu.CompilerParams(
            collective_id=1, has_side_effects=True, vmem_limit_bytes=VMEM_LIMIT
        ),
        name="reduce_grads",
    )(grads)


def on_device(tok, cot, wts, counts, column, dest, live):
    c = lax.axis_index("expert")
    in_plane = c % 8
    ids = jnp.arange(EXPERTS, dtype=jnp.int32)
    cumulative = jnp.sum(jnp.where(ids[None, :] <= ids[:, None], counts[None, :], 0), axis=1)
    first = cumulative - counts
    replicas = jnp.arange(32, dtype=jnp.int32)
    first_col = jnp.sum(jnp.where(replicas[None, :] == first[:, None], column[None, :], 0), axis=1)
    my_dest = lax.dynamic_index_in_dim(dest.reshape(X, 8, SLOT), in_plane, 1, keepdims=False)
    my_live = lax.dynamic_index_in_dim(live.reshape(X, 8), in_plane, 1, keepdims=False)
    expert = jnp.sum((cumulative[None, None, :] <= my_dest[:, :, None]).astype(jnp.int32), axis=2)
    slots = jnp.arange(SLOT, dtype=jnp.int32)
    gexp = jnp.where(slots[None, :] < my_live[:, None], expert, EXPERTS).reshape(NGRAN)

    xg, qg, hg = rows_and_hidden(first_col, gexp, tok, cot, wts)
    xg = xg.reshape(NGRAN, GRAN, DC)
    qg = qg.reshape(NGRAN, GRAN, DC)
    hg = hg.reshape(NGRAN, GRAN, LANES)
    shares = reduce_grads(gradients(gexp, xg, qg, hg))
    return shares[:, :54, : DC // 2].reshape(EXPERTS, 3, 18, DC // 2)


def solution(mesh):
    placed = (
        P("expert", "dp", None),
        P("expert", "dp", None),
        P("expert", None, None, None),
        P(),
        P(),
        P(),
        P(),
    )
    return jax.shard_map(
        on_device,
        mesh=mesh,
        in_specs=placed,
        out_specs=P(None, None, "dp", "expert"),
        check_vma=False,
    )
```

```python
import jax
import jax.numpy as jnp
from jax import lax
from jax.experimental import pallas as pl
from jax.experimental.pallas import tpu as pltpu
from jax.sharding import PartitionSpec as P

MESH = pl.DeviceIdType.MESH
EXPERTS = 8
X, Y, Z = 4, 4, 8
GROUP = X * Y
D = 6144
DC = D // GROUP
SLOT = 8
ROWS = 16
MAIN = 128
TAIL = 16
LANES = 512
GROWS = 448
HALF = GROWS // 2
GRAN = Y * ROWS
NGRAN = X * SLOT
TILE = 256
PER_TILE = TILE // GRAN
MAX_TILES = NGRAN // PER_TILE + EXPERTS - 1
VMEM_LIMIT = 56 * 1024 * 1024


def coords():
    d = lax.axis_index("dp")
    c = lax.axis_index("expert")
    return c // 8, d // 2, (d % 2) * 4 + (c // 2) % 4, c % 2


def device(x, y, z, k):
    return (y * 2 + z // 4, (x * 4 + z % 4) * 2 + k)


MOVES = (
    (1, 0), (0, 1), (3, 0), (0, 3), (2, 0), (0, 2), (1, 1), (3, 3), (1, 3), (3, 1), (2, 1), (1, 2), (2, 3), (3, 2), (2, 2),
)


def plane_peer(x, y, step):
    dx, dy = MOVES[step]
    return (x + dx) % X, (y + dy) % Y


def signal(sem, target):
    pl.semaphore_signal(sem, inc=1, device_id=target, device_id_type=MESH)


def remote(src, dst, send, recv, target):
    return pltpu.make_async_remote_copy(
        src_ref=src, dst_ref=dst, send_sem=send, recv_sem=recv, device_id=target, device_id_type=MESH
    )


def wait_bytes(ref, sem):
    pltpu.make_async_copy(ref, ref, sem).wait()


def swiglu_rows(gate, up, grad):
    sig = jax.nn.sigmoid(gate)
    act = gate * sig
    return grad * up * sig * (1.0 + gate * (1.0 - sig)), grad * act, act * up


def dot_nt(a, b):
    return lax.dot_general(a, b, (((1,), (1,)), ((), ())), preferred_element_type=jnp.float32)


def dot_tn(a, b):
    return lax.dot_general(a, b, (((0,), (0,)), ((), ())), preferred_element_type=jnp.float32)


CHUNKS = 2
PART = SLOT // CHUNKS
SUM_TYPE = jnp.float32


def rows_kernel(
    counts, column, dest, live, tok, cot, wts, xg, qg, hg, gexp, wr, sel, wg, xv, qv, p1, r1, s2, r2, hid, xs_sem, xr_sem, qs_sem, qr_sem,
    ws_sem, wr_sem, own_sem, rs_sem, rr_sem, ls_sem, lr_sem, ss_sem, sr_sem, p1s_sem, p1r_sem, p2s_sem, p2r_sem,
    has_sem, har_sem, hbs_sem, hbr_sem, keep_sem,
):
    x, y, z, k = coords()
    zh, zl = z // 4, z % 4
    me_col = (x * 4 + zl) * 2 + k
    barrier = pltpu.get_barrier_semaphore()

    def greet_column(step, carry):
        signal(barrier, (y * 2 + zh, (me_col + step) % 32))
        return carry

    for step in range(GROUP - 1):
        px, py = plane_peer(x, y, step)
        signal(barrier, device(px, py, z, k))
    lax.fori_loop(1, 32, greet_column, 0)
    right, left = device(x, y, (z + 1) % Z, k), device(x, y, (z + Z - 1) % Z, k)
    sibling = device(x, y, z, 1 - k)
    signal(barrier, right)
    signal(barrier, left)
    pl.semaphore_wait(barrier, GROUP - 1 + 31 + 2)

    def weight_piece(col, part):
        cx, cz, ck = col // 8, zh * 4 + (col // 2) % 4, col % 2
        t = jnp.minimum((cz * 2 + ck) * 2 + part, 26)
        tail = t // 24
        m = (t // 8) * (1 - tail) + (t - 24) * tail
        row = (t % 8) * 16 * (1 - tail) + 128 * tail
        return wts.at[
            0,
            m,
            pl.ds(pl.multiple_of(row, 16), 16),
            pl.ds(pl.multiple_of((cx * Y + y) * DC, 128), DC),
        ]

    def send_weights(step, carry):
        col = (me_col + step) % 32
        for part in range(2):
            remote(
                weight_piece(col, part), wr.at[me_col, pl.ds(part * 16, 16), :], ws_sem, wr_sem, (y * 2 + zh, col)
            ).start()
        return carry

    lax.fori_loop(1, 32, send_weights, 0)
    for part in range(2):
        pltpu.make_async_copy(
            weight_piece(me_col, part), wr.at[me_col, pl.ds(part * 16, 16), :], wr_sem
        ).start()

    def columns(ref, px, py):
        return ref.at[:, :, pl.ds(pl.multiple_of((px * Y + py) * DC, 128), DC)]

    def x_copy(step):
        px, py = plane_peer(x, y, step)
        return remote(
            columns(tok, px, py), xv.at[x, :, y], xs_sem.at[step], xr_sem.at[step], device(px, py, z, k)
        )

    def q_copy(step):
        px, py = plane_peer(x, y, step)
        return remote(
            columns(cot, px, py), qv.at[x, :, y], qs_sem.at[step], qr_sem.at[step], device(px, py, z, k)
        )

    for step in range(GROUP - 1):
        x_copy(step).start()
    own_x = pltpu.make_async_copy(columns(tok, x, y), xv.at[x, :, y], own_sem.at[0])
    own_q = pltpu.make_async_copy(columns(cot, x, y), qv.at[x, :, y], own_sem.at[1])
    own_x.start()
    own_q.start()

    firsts, lasts = [], []
    for e in range(EXPERTS):
        firsts.append(lasts[-1] if e else 0)
        lasts.append(firsts[-1] + counts[e])

    def place_experts():
        def one(g, carry):
            col = ((g // SLOT) * 4 + zl) * 2 + k
            replica = dest[col, g % SLOT]
            expert = 0
            for e in range(EXPERTS - 1):
                expert += (lasts[e] <= replica).astype(jnp.int32)
            gexp[g] = jnp.where(g % SLOT < live[col], expert, EXPERTS)
            return carry

        lax.fori_loop(0, NGRAN, one, 0)

    wait_bytes(wr, wr_sem)
    for e in range(EXPERTS):
        sel[e] = wr[column[firsts[e]]]

    def chunk(pz):
        return wg.at[:, pl.ds(pl.multiple_of((pz * 2 + k) * 32, 32), 32), :]

    mine = chunk(z)
    own_w = pltpu.make_async_copy(sel, mine, own_sem.at[2])
    own_w.start()
    rights = [remote(sel, mine, rs_sem.at[0], rr_sem.at[0], right)]
    lefts = [remote(sel, mine, ls_sem.at[0], lr_sem.at[0], left)]
    sibs = [remote(sel, mine, ss_sem.at[0], sr_sem.at[0], sibling)]
    rights[0].start()
    lefts[0].start()
    sibs[0].start()
    for step in range(GROUP - 1):
        q_copy(step).start()
    place_experts()
    for t in range(1, 5):
        rights[t - 1].wait_recv()
        piece = chunk((z + Z - t) % Z)
        if t < 4:
            go = remote(piece, piece, rs_sem.at[t], rr_sem.at[t], right)
            go.start()
            rights.append(go)
        go = remote(piece, piece, ss_sem.at[2 * t - 1], sr_sem.at[2 * t - 1], sibling)
        go.start()
        sibs.append(go)
        if t < 4:
            lefts[t - 1].wait_recv()
            piece = chunk((z + t) % Z)
            if t < 3:
                go = remote(piece, piece, ls_sem.at[t], lr_sem.at[t], left)
                go.start()
                lefts.append(go)
            go = remote(piece, piece, ss_sem.at[2 * t], sr_sem.at[2 * t], sibling)
            go.start()
            sibs.append(go)
    for go in sibs:
        go.wait_recv()
    own_w.wait()

    for step in range(GROUP - 1):
        x_copy(step).wait_recv()
    own_x.wait()
    keep_x = pltpu.make_async_copy(xv, xg, keep_sem.at[0])
    keep_x.start()

    a_here, b_here = x * (1 - k) + y * k, x * k + y * (1 - k)

    def place(a, b):
        return a * (1 - k) + b * k, a * k + b * (1 - k)

    def plane_device(a, b):
        px, py = place(a, b)
        return device(px, py, z, k)

    def slots(h):
        return pl.ds(h * PART, PART)

    in_tail = lax.broadcasted_iota(jnp.int32, (ROWS, MAIN), 1) < 2 * TAIL

    def first_copy(h, j):
        a = (a_here + j) % 4
        at = h * 3 + j - 1
        return remote(
            p1.at[a, :, slots(h)], r1.at[a_here, :, slots(h)], p1s_sem.at[at], p1r_sem.at[at], plane_device(a, b_here)
        )

    def second_copy(h, j):
        b = (b_here + j) % 4
        at = h * 3 + j - 1
        return remote(
            s2.at[b, slots(h)], r2.at[b_here, slots(h)], p2s_sem.at[at], p2r_sem.at[at], plane_device(a_here, b)
        )

    def hidden_place(a, b, h):
        px, py = place(a, b)
        return hg.at[px, slots(h), py]

    def hidden_first(h, j):
        at = h * 3 + j - 1
        return remote(
            hid.at[slots(h)], hidden_place(a_here, b_here, h), has_sem.at[at], har_sem.at[at],
            plane_device((a_here + j) % 4, b_here),
        )

    def hidden_second(h, j, i):
        at = (h * 4 + j) * 3 + i - 1
        here = hidden_place((a_here + 4 - j) % 4, b_here, h)
        return remote(
            hid.at[slots(h)] if j == 0 else here, here, hbs_sem.at[at], hbr_sem.at[at],
            plane_device(a_here, (b_here + i) % 4),
        )

    def weights_of(px, s):
        return jnp.minimum(gexp[px * SLOT + s], EXPERTS - 1)

    def put_rows(px, s, lo, value):
        for py in range(Y):
            pa, pb = px * (1 - k) + py * k, px * k + py * (1 - k)
            p1[pa, pb, s, :, lo : lo + value.shape[1]] = value[py * ROWS : (py + 1) * ROWS]

    def project_x(g, carry):
        px, s = g // SLOT, g % SLOT
        e = weights_of(px, s)
        xt = xv[px, s].reshape(GRAN, DC)
        put_rows(px, s, 0, dot_nt(xt, wg[e, 0 : 2 * MAIN]).astype(SUM_TYPE))
        put_rows(px, s, 3 * MAIN, dot_nt(xt, wg[e, 3 * MAIN : LANES]).astype(SUM_TYPE))
        return carry

    lax.fori_loop(0, NGRAN, project_x, 0)
    for step in range(GROUP - 1):
        q_copy(step).wait_recv()
    own_q.wait()
    keep_q = pltpu.make_async_copy(qv, qg, keep_sem.at[1])
    keep_q.start()
    for h in range(CHUNKS):

        def project_q(i, carry):
            px, s = i // PART, h * PART + i % PART
            e = weights_of(px, s)
            rows = dot_nt(qv[px, s].reshape(GRAN, DC), wg[e, 2 * MAIN : LANES]).astype(SUM_TYPE)
            put_rows(px, s, 2 * MAIN, rows[:, :MAIN])
            for py in range(Y):
                pa, pb = px * (1 - k) + py * k, px * k + py * (1 - k)
                at = (pa, pb, s, slice(None), slice(3 * MAIN, LANES))
                p1[at] = jnp.where(in_tail, p1[at], rows[py * ROWS : (py + 1) * ROWS, MAIN:])
            return carry

        lax.fori_loop(0, X * PART, project_q, 0)
        for j in (2, 1, 3):
            first_copy(h, j).start()

    for h in range(CHUNKS):
        for j in (1, 2, 3):
            first_copy(h, j).wait_recv()

        def sum_first(b, carry):
            value = p1[a_here, b, h * PART : (h + 1) * PART].astype(jnp.float32)
            for j in (1, 2, 3):
                value += r1[(a_here + j) % 4, b, h * PART : (h + 1) * PART].astype(jnp.float32)
            s2[b, h * PART : (h + 1) * PART] = value
            return carry

        lax.fori_loop(0, 4, sum_first, 0)
        for j in (2, 1, 3):
            second_copy(h, j).start()

    lane = lax.broadcasted_iota(jnp.int32, (PART * ROWS, MAIN), 1)

    def shift(v, amount):
        return pltpu.roll(v, amount % MAIN, 1)

    for h in range(CHUNKS):
        for j in (1, 2, 3):
            second_copy(h, j).wait_recv()
        cut = slice(h * PART, (h + 1) * PART)

        def total(lo):
            value = s2[b_here, cut, :, lo : lo + MAIN]
            for j in (1, 2, 3):
                value += r2[(b_here + j) % 4, cut, :, lo : lo + MAIN]
            return value.reshape(PART * ROWS, MAIN)

        def put(lo, value):
            hid[cut, :, lo : lo + MAIN] = value.astype(jnp.bfloat16).reshape(PART, ROWS, MAIN)

        for at, value in enumerate(swiglu_rows(total(0), total(MAIN), total(2 * MAIN))):
            put(at * MAIN, value)
        tail = total(3 * MAIN)
        first, second, third = swiglu_rows(tail, shift(tail, -TAIL), shift(tail, -2 * TAIL))
        packed = jnp.where(
            lane < TAIL, first, jnp.where(lane < 2 * TAIL, shift(second, TAIL), shift(third, 2 * TAIL))
        )
        put(3 * MAIN, jnp.where(lane < 3 * TAIL, packed, 0.0))
        for j in (2, 1, 3):
            hidden_first(h, j).start()
        for i in (2, 1, 3):
            hidden_second(h, 0, i).start()
        pltpu.make_async_copy(hid.at[slots(h)], hidden_place(a_here, b_here, h), keep_sem.at[2 + h]).start()

    for h in range(CHUNKS):
        for j in (1, 3, 2):
            hidden_first(h, j).wait_recv()
            for i in (2, 1, 3):
                hidden_second(h, j, i).start()
    for h in range(CHUNKS):
        for j in range(4):
            for i in (1, 2, 3):
                hidden_second(h, j, i).wait()
        for j in (1, 2, 3):
            hidden_first(h, j).wait_send()
            first_copy(h, j).wait_send()
            second_copy(h, j).wait_send()
        pltpu.make_async_copy(hid.at[slots(h)], hidden_place(a_here, b_here, h), keep_sem.at[2 + h]).wait()
    for step in range(GROUP - 1):
        x_copy(step).wait_send()
        q_copy(step).wait_send()
    for go in rights + lefts + sibs:
        go.wait_send()
    wait_bytes(wr.at[pl.ds(0, 31)], ws_sem)
    keep_x.wait()
    keep_q.wait()


def rows_and_hidden(counts, column, dest, live, tok, cot, wts):
    hbm = pl.BlockSpec(memory_space=pl.ANY)
    smem = pl.BlockSpec(memory_space=pltpu.SMEM)
    dma = pltpu.SemaphoreType.DMA
    spread = pltpu.VMEM((X, SLOT, Y, ROWS, DC), jnp.bfloat16)
    sums = pltpu.VMEM((4, 4, SLOT, ROWS, LANES), SUM_TYPE)
    halfway = pltpu.VMEM((4, SLOT, ROWS, LANES), jnp.float32)
    return pl.pallas_call(
        rows_kernel,
        out_shape=(
            jax.ShapeDtypeStruct((X, SLOT, Y, ROWS, DC), jnp.bfloat16),
            jax.ShapeDtypeStruct((X, SLOT, Y, ROWS, DC), jnp.bfloat16),
            jax.ShapeDtypeStruct((X, SLOT, Y, ROWS, LANES), jnp.bfloat16),
            jax.ShapeDtypeStruct((NGRAN,), jnp.int32),
        ),
        in_specs=[smem, smem, smem, smem, hbm, hbm, hbm],
        out_specs=(hbm, hbm, hbm, smem),
        scratch_shapes=[
            pltpu.VMEM((32, 32, DC), jnp.bfloat16),
            pltpu.VMEM((EXPERTS, 32, DC), jnp.bfloat16),
            pltpu.VMEM((EXPERTS, LANES, DC), jnp.bfloat16),
            spread,
            spread,
            sums,
            sums,
            halfway,
            halfway,
            pltpu.VMEM((SLOT, ROWS, LANES), jnp.bfloat16),
            dma((GROUP,)),
            dma((GROUP,)),
            dma((GROUP,)),
            dma((GROUP,)),
            dma,
            dma,
            dma((3,)),
            dma((4,)),
            dma((4,)),
            dma((3,)),
            dma((3,)),
            dma((8,)),
            dma((8,)),
            dma((3 * CHUNKS,)),
            dma((3 * CHUNKS,)),
            dma((3 * CHUNKS,)),
            dma((3 * CHUNKS,)),
            dma((3 * CHUNKS,)),
            dma((3 * CHUNKS,)),
            dma((12 * CHUNKS,)),
            dma((12 * CHUNKS,)),
            dma((2 + CHUNKS,)),
        ],
        compiler_params=pltpu.CompilerParams(
            collective_id=0, has_side_effects=True, vmem_limit_bytes=VMEM_LIMIT
        ),
        name="rows_and_hidden",
    )(counts, column, dest, live, tok, cot, wts)


def grads_kernel(gexp, xg, qg, hg, out, xs, qs, hs, acc, order, ends, in_sem, out_sem):
    pairs = ((xg, xs), (qg, qs), (hg, hs))

    def at(place):
        return pl.ds(pl.multiple_of(place * GRAN, GRAN), GRAN)

    def one_expert(e, tile):
        def one_granule(g, count):
            hit = gexp[g] == e

            @pl.when(hit)
            def _():
                place = tile * PER_TILE + count
                order[place] = 1
                for i, (source, packed) in enumerate(pairs):
                    pltpu.make_async_copy(source.at[g], packed.at[at(place)], in_sem.at[i, place]).start()

            return count + hit.astype(jnp.int32)

        count = lax.fori_loop(0, NGRAN, one_granule, 0)
        tiles = (count + PER_TILE - 1) // PER_TILE

        def pad(place, carry):
            order[place] = 0
            for _, packed in pairs:
                packed[at(place)] = jnp.zeros((GRAN, packed.shape[1]), packed.dtype)
            return carry

        lax.fori_loop(tile * PER_TILE + count, (tile + tiles) * PER_TILE, pad, 0)
        ends[e] = tile + tiles
        return tile + tiles

    lax.fori_loop(0, EXPERTS, one_expert, 0)
    acc[...] = jnp.zeros_like(acc)
    tail_rows = GROWS - 3 * MAIN
    from_x = lax.broadcasted_iota(jnp.int32, (tail_rows, DC), 0) < 2 * TAIL

    def expert_step(e, start):
        def tile_step(t, carry):
            for j in range(PER_TILE):
                place = t * PER_TILE + j

                @pl.when(order[place] == 1)
                def _():
                    for i, (source, packed) in enumerate(pairs):
                        pltpu.make_async_copy(source.at[0], packed.at[at(place)], in_sem.at[i, place]).wait()

            rows = pl.ds(pl.multiple_of(t * TILE, TILE), TILE)
            xt, qt = xs[rows], qs[rows]
            acc[e, 0 : 2 * MAIN] += dot_tn(hs[rows, 0 : 2 * MAIN], xt)
            acc[e, 2 * MAIN : 3 * MAIN] += dot_tn(hs[rows, 2 * MAIN : 3 * MAIN], qt)
            tail = hs[rows, 3 * MAIN : LANES]
            x_tail, q_tail = dot_tn(tail, xt), dot_tn(tail, qt)
            acc[e, 3 * MAIN : GROWS] += jnp.where(from_x, x_tail[:tail_rows], q_tail[:tail_rows])
            return carry

        lax.fori_loop(start, ends[e], tile_step, 0)
        pltpu.make_async_copy(acc.at[e], out.at[e], out_sem.at[e]).start()
        return ends[e]

    lax.fori_loop(0, EXPERTS, expert_step, 0)

    def finish(e, carry):
        pltpu.make_async_copy(acc.at[e], out.at[e], out_sem.at[e]).wait()
        return carry

    lax.fori_loop(0, EXPERTS, finish, 0)


def gradients(gexp, xg, qg, hg):
    hbm = pl.BlockSpec(memory_space=pl.ANY)
    packed = MAX_TILES * TILE
    return pl.pallas_call(
        grads_kernel,
        out_shape=jax.ShapeDtypeStruct((EXPERTS, GROWS, DC), jnp.float32),
        in_specs=[pl.BlockSpec(memory_space=pltpu.SMEM), hbm, hbm, hbm],
        out_specs=hbm,
        scratch_shapes=[
            pltpu.VMEM((packed, DC), jnp.bfloat16),
            pltpu.VMEM((packed, DC), jnp.bfloat16),
            pltpu.VMEM((packed, LANES), jnp.bfloat16),
            pltpu.VMEM((EXPERTS, GROWS, DC), jnp.float32),
            pltpu.SMEM((MAX_TILES * PER_TILE,), jnp.int32),
            pltpu.SMEM((EXPERTS,), jnp.int32),
            pltpu.SemaphoreType.DMA((3, MAX_TILES * PER_TILE)),
            pltpu.SemaphoreType.DMA((EXPERTS,)),
        ],
        compiler_params=pltpu.CompilerParams(vmem_limit_bytes=VMEM_LIMIT),
        name="gradients",
    )(gexp, xg, qg, hg)


QUART = HALF // 2
PACK = 64
WINDOW = 256
OFFSETS = (4, 3, -3, 2, -2, 1, -1, 0)


def reduce_kernel(
    grads, out, own, sib, sbuf, rbuf, fin, win, wide, pack, os_sem, ts_sem, tr_sem, cs_sem, cr_sem, swap_sem, send, recv,
    keep_sem,
):
    x, y, z, k = coords()
    zh, zl = z // 4, z % 4
    sibling = device(x, y, z, 1 - k)
    barrier = pltpu.get_barrier_semaphore()

    def target(share):
        return share // 2, (share % 2) * 4 + y

    def greet_share(share, carry):
        ty, tz = target(share)

        @pl.when((ty != y) | (tz != z))
        def _():
            signal(barrier, device(x, ty, tz, k))

        return carry

    def greet_source(pz, carry):
        @pl.when((zl != y) | (pz != z))
        def _():
            signal(barrier, device(x, zl, pz, k))

        return carry

    ahead = (device(x, y, (z + 1) % Z, k), device(x, y, (z + Z - 1) % Z, k))
    signal(barrier, sibling)
    signal(barrier, ahead[0])
    signal(barrier, ahead[1])
    lax.fori_loop(0, 8, greet_share, 0)
    lax.fori_loop(0, 8, greet_source, 0)
    self_here = jnp.where(zl == y, 1, 0)
    pl.semaphore_wait(barrier, 19 - 2 * self_here)

    def half(e, which):
        return grads.at[e, pl.ds(pl.multiple_of(which * HALF, HALF), HALF), :]

    trades, keeps = {}, {}
    for i, off in enumerate(OFFSETS):
        e = (z + off + Z) % Z
        trades[off] = remote(half(e, 1 - k), sib.at[e], ts_sem.at[i], tr_sem.at[i], sibling)
        keeps[off] = pltpu.make_async_copy(half(e, k), own.at[e], os_sem.at[i])
        trades[off].start()
        keeps[off].start()
    trades[-4], keeps[-4] = trades[4], keeps[4]
    ready = set()

    def ours(off, j):
        if abs(off) % 8 == 4:
            off = 4
        if off not in ready:
            trades[off].wait_recv()
            keeps[off].wait()
            ready.add(off)
        e = (z + off + Z) % Z
        cut = slice(j * QUART, (j + 1) * QUART)
        return own[e, cut] + sib[e, cut]

    chain = {}
    for dist in (4, 3, 2, 1):
        for way in range(2):
            for j in range(2):
                longest = 4 if way == j else 3
                if dist > longest:
                    continue
                value = ours(dist if way == 0 else -dist, j)
                if dist < longest:
                    chain[way, j, dist + 1].wait_recv()
                    value += rbuf[way, j, dist].astype(jnp.float32)
                sbuf[way, j, dist - 1] = value.astype(jnp.bfloat16)
                at = (way * 2 + j) * 4 + dist - 1
                go = remote(
                    sbuf.at[way, j, dist - 1], rbuf.at[way, j, dist - 1], cs_sem.at[at], cr_sem.at[at], ahead[way]
                )
                go.start()
                chain[way, j, dist] = go
    for j in range(2):
        value = ours(0, j)
        for way in range(2):
            chain[way, j, 1].wait_recv()
            value += rbuf[way, j, 0].astype(jnp.float32)
        fin[pl.ds(pl.multiple_of(k * HALF + j * QUART, 16), QUART)] = value
    mine = fin.at[pl.ds(pl.multiple_of(k * HALF, HALF), HALF)]
    swap = remote(mine, mine, swap_sem.at[0], swap_sem.at[1], sibling)
    swap.start()
    swap.wait()

    low = fin[:, 0:WINDOW]
    high = pltpu.roll(fin[:, DC - WINDOW : DC], DC // 2, 1)
    win[...] = jnp.where(k == 0, low, high)
    for share in range(8):
        wide[share, 48:PACK] = jnp.zeros((PACK - 48, WINDOW), jnp.float32)
        for m in range(3):
            if share < 7:
                lo = m * MAIN + 18 * share
                wide[share, 18 * m : 18 * m + 18] = win[lo : lo + 18]
            else:
                lo = m * MAIN + 126
                wide[share, 18 * m : 18 * m + 2] = win[lo : lo + 2]
                lo = 3 * MAIN + m * TAIL
                wide[share, 18 * m + 2 : 18 * m + 18] = win[lo : lo + TAIL]
        pack[share] = wide[share].astype(jnp.bfloat16)

    def share_copy(share):
        ty, tz = target(share)
        return remote(pack.at[share], out.at[z], send.at[share], recv.at[z], device(x, ty, tz, k))

    def start(share, carry):
        ty, tz = target(share)

        @pl.when((ty != y) | (tz != z))
        def _():
            share_copy(share).start()

        @pl.when((ty == y) & (tz == z))
        def _():
            pltpu.make_async_copy(pack.at[share], out.at[z], keep_sem).start()

        return carry

    def finish_send(share, carry):
        ty, tz = target(share)

        @pl.when((ty != y) | (tz != z))
        def _():
            share_copy(share).wait_send()

        @pl.when((ty == y) & (tz == z))
        def _():
            pltpu.make_async_copy(pack.at[share], out.at[z], keep_sem).wait()

        return carry

    def finish_recv(pz, carry):
        @pl.when((zl != y) | (pz != z))
        def _():
            pltpu.make_async_copy(out.at[pz], out.at[pz], recv.at[pz]).wait()

        return carry

    lax.fori_loop(0, 8, start, 0)
    lax.fori_loop(0, 8, finish_send, 0)
    lax.fori_loop(0, 8, finish_recv, 0)
    for off in OFFSETS:
        trades[off].wait_send()
    for go in chain.values():
        go.wait_send()


def reduce_grads(grads):
    dma = pltpu.SemaphoreType.DMA
    wide = pltpu.VMEM((EXPERTS, HALF, DC), jnp.float32)
    steps = pltpu.VMEM((2, 2, 4, QUART, DC), jnp.bfloat16)
    return pl.pallas_call(
        reduce_kernel,
        out_shape=jax.ShapeDtypeStruct((EXPERTS, PACK, WINDOW), jnp.bfloat16),
        in_specs=[pl.BlockSpec(memory_space=pl.ANY)],
        out_specs=pl.BlockSpec(memory_space=pltpu.VMEM),
        scratch_shapes=[
            wide,
            wide,
            steps,
            steps,
            pltpu.VMEM((GROWS, DC), jnp.float32),
            pltpu.VMEM((GROWS, WINDOW), jnp.float32),
            pltpu.VMEM((8, PACK, WINDOW), jnp.float32),
            pltpu.VMEM((8, PACK, WINDOW), jnp.bfloat16),
            dma((8,)),
            dma((8,)),
            dma((8,)),
            dma((16,)),
            dma((16,)),
            dma((2,)),
            dma((8,)),
            dma((8,)),
            dma,
        ],
        compiler_params=pltpu.CompilerParams(
            collective_id=1, has_side_effects=True, vmem_limit_bytes=VMEM_LIMIT
        ),
        name="reduce_grads",
    )(grads)


def on_device(tok, cot, wts, counts, column, dest, live):
    xg, qg, hg, gexp = rows_and_hidden(counts, column, dest, live, tok, cot, wts)
    xg = xg.reshape(NGRAN, GRAN, DC)
    qg = qg.reshape(NGRAN, GRAN, DC)
    hg = hg.reshape(NGRAN, GRAN, LANES)
    shares = reduce_grads(gradients(gexp, xg, qg, hg))
    return shares[:, :54, : DC // 2].reshape(EXPERTS, 3, 18, DC // 2)


def solution(mesh):
    placed = (
        P("expert", "dp", None),
        P("expert", "dp", None),
        P("expert", None, None, None),
        P(),
        P(),
        P(),
        P(),
    )
    return jax.shard_map(
        on_device,
        mesh=mesh,
        in_specs=placed,
        out_specs=P(None, None, "dp", "expert"),
        check_vma=False,
    )
```

```python
import jax
import jax.numpy as jnp
from jax import lax
from jax.experimental import pallas as pl
from jax.experimental.pallas import tpu as pltpu
from jax.sharding import PartitionSpec as P

MESH = pl.DeviceIdType.MESH
EXPERTS = 8
X, Y, Z = 4, 4, 8
GROUP = X * Y
D = 6144
DC = D // GROUP
SLOT = 8
ROWS = 16
MAIN = 128
TAIL = 16
LANES = 512
GROWS = 448
HALF = GROWS // 2
GRAN = Y * ROWS
NGRAN = X * SLOT
TILE = 256
PER_TILE = TILE // GRAN
MAX_TILES = NGRAN // PER_TILE + EXPERTS - 1
VMEM_LIMIT = 56 * 1024 * 1024


def coords():
    d = lax.axis_index("dp")
    c = lax.axis_index("expert")
    return c // 8, d // 2, (d % 2) * 4 + (c // 2) % 4, c % 2


def device(x, y, z, k):
    return (y * 2 + z // 4, (x * 4 + z % 4) * 2 + k)


MOVES = (
    (1, 0), (0, 1), (3, 0), (0, 3), (2, 0), (0, 2), (1, 1), (3, 3), (1, 3), (3, 1), (2, 1), (1, 2), (2, 3), (3, 2), (2, 2),
)


def plane_peer(x, y, step):
    dx, dy = MOVES[step]
    return (x + dx) % X, (y + dy) % Y


def signal(sem, target):
    pl.semaphore_signal(sem, inc=1, device_id=target, device_id_type=MESH)


def remote(src, dst, send, recv, target):
    return pltpu.make_async_remote_copy(
        src_ref=src, dst_ref=dst, send_sem=send, recv_sem=recv, device_id=target, device_id_type=MESH
    )


def wait_bytes(ref, sem):
    pltpu.make_async_copy(ref, ref, sem).wait()


def swiglu_rows(gate, up, grad):
    sig = jax.nn.sigmoid(gate)
    act = gate * sig
    return grad * up * sig * (1.0 + gate * (1.0 - sig)), grad * act, act * up


def dot_nt(a, b):
    return lax.dot_general(a, b, (((1,), (1,)), ((), ())), preferred_element_type=jnp.float32)


def dot_tn(a, b):
    return lax.dot_general(a, b, (((0,), (0,)), ((), ())), preferred_element_type=jnp.float32)


CHUNKS = 2
PART = SLOT // CHUNKS
PAIRS = PART // 2
BLOCKS = 3 * PART + PAIRS
SIDE = 64
SUM_TYPE = jnp.float32


def rows_kernel(
    counts, column, dest, live, tok, cot, wts, xg, qg, hg, gexp, wr, sel, wg, xv, qv, p1, m1, r1, s2, r2, hid, xs_sem, xr_sem, qs_sem, qr_sem,
    ws_sem, wr_sem, own_sem, rs_sem, rr_sem, ls_sem, lr_sem, ss_sem, sr_sem, p1s_sem, p1r_sem, p2s_sem, p2r_sem,
    has_sem, har_sem, hbs_sem, hbr_sem, keep_sem,
):
    x, y, z, k = coords()
    zh, zl = z // 4, z % 4
    me_col = (x * 4 + zl) * 2 + k
    barrier = pltpu.get_barrier_semaphore()

    def greet_column(step, carry):
        signal(barrier, (y * 2 + zh, (me_col + step) % 32))
        return carry

    for step in range(GROUP - 1):
        px, py = plane_peer(x, y, step)
        signal(barrier, device(px, py, z, k))
    lax.fori_loop(1, 32, greet_column, 0)
    right, left = device(x, y, (z + 1) % Z, k), device(x, y, (z + Z - 1) % Z, k)
    sibling = device(x, y, z, 1 - k)
    signal(barrier, right)
    signal(barrier, left)
    pl.semaphore_wait(barrier, GROUP - 1 + 31 + 2)

    def weight_piece(col, part):
        cx, cz, ck = col // 8, zh * 4 + (col // 2) % 4, col % 2
        t = jnp.minimum((cz * 2 + ck) * 2 + part, 26)
        tail = t // 24
        m = (t // 8) * (1 - tail) + (t - 24) * tail
        row = (t % 8) * 16 * (1 - tail) + 128 * tail
        return wts.at[
            0,
            m,
            pl.ds(pl.multiple_of(row, 16), 16),
            pl.ds(pl.multiple_of((cx * Y + y) * DC, 128), DC),
        ]

    def send_weights(step, carry):
        col = (me_col + step) % 32
        for part in range(2):
            remote(
                weight_piece(col, part), wr.at[me_col, pl.ds(part * 16, 16), :], ws_sem, wr_sem, (y * 2 + zh, col)
            ).start()
        return carry

    lax.fori_loop(1, 32, send_weights, 0)
    for part in range(2):
        pltpu.make_async_copy(
            weight_piece(me_col, part), wr.at[me_col, pl.ds(part * 16, 16), :], wr_sem
        ).start()

    def columns(ref, px, py):
        return ref.at[:, :, pl.ds(pl.multiple_of((px * Y + py) * DC, 128), DC)]

    def x_copy(step):
        px, py = plane_peer(x, y, step)
        return remote(
            columns(tok, px, py), xv.at[x, :, y], xs_sem.at[step], xr_sem.at[step], device(px, py, z, k)
        )

    def q_copy(step):
        px, py = plane_peer(x, y, step)
        return remote(
            columns(cot, px, py), qv.at[x, :, y], qs_sem.at[step], qr_sem.at[step], device(px, py, z, k)
        )

    for step in range(GROUP - 1):
        x_copy(step).start()
    own_x = pltpu.make_async_copy(columns(tok, x, y), xv.at[x, :, y], own_sem.at[0])
    own_q = pltpu.make_async_copy(columns(cot, x, y), qv.at[x, :, y], own_sem.at[1])
    own_x.start()
    own_q.start()

    firsts, lasts = [], []
    for e in range(EXPERTS):
        firsts.append(lasts[-1] if e else 0)
        lasts.append(firsts[-1] + counts[e])

    def place_experts():
        def one(g, carry):
            col = ((g // SLOT) * 4 + zl) * 2 + k
            replica = dest[col, g % SLOT]
            expert = 0
            for e in range(EXPERTS - 1):
                expert += (lasts[e] <= replica).astype(jnp.int32)
            gexp[g] = jnp.where(g % SLOT < live[col], expert, EXPERTS)
            return carry

        lax.fori_loop(0, NGRAN, one, 0)

    wait_bytes(wr, wr_sem)
    for e in range(EXPERTS):
        sel[e] = wr[column[firsts[e]]]

    def chunk(pz):
        return wg.at[:, pl.ds(pl.multiple_of((pz * 2 + k) * 32, 32), 32), :]

    mine = chunk(z)
    own_w = pltpu.make_async_copy(sel, mine, own_sem.at[2])
    own_w.start()
    rights = [remote(sel, mine, rs_sem.at[0], rr_sem.at[0], right)]
    lefts = [remote(sel, mine, ls_sem.at[0], lr_sem.at[0], left)]
    sibs = [remote(sel, mine, ss_sem.at[0], sr_sem.at[0], sibling)]
    rights[0].start()
    lefts[0].start()
    sibs[0].start()
    for step in range(GROUP - 1):
        q_copy(step).start()
    place_experts()
    for t in range(1, 5):
        rights[t - 1].wait_recv()
        piece = chunk((z + Z - t) % Z)
        if t < 4:
            go = remote(piece, piece, rs_sem.at[t], rr_sem.at[t], right)
            go.start()
            rights.append(go)
        go = remote(piece, piece, ss_sem.at[2 * t - 1], sr_sem.at[2 * t - 1], sibling)
        go.start()
        sibs.append(go)
        if t < 4:
            lefts[t - 1].wait_recv()
            piece = chunk((z + t) % Z)
            if t < 3:
                go = remote(piece, piece, ls_sem.at[t], lr_sem.at[t], left)
                go.start()
                lefts.append(go)
            go = remote(piece, piece, ss_sem.at[2 * t], sr_sem.at[2 * t], sibling)
            go.start()
            sibs.append(go)
    for go in sibs:
        go.wait_recv()
    own_w.wait()

    for step in range(GROUP - 1):
        x_copy(step).wait_recv()
    own_x.wait()
    keep_x = pltpu.make_async_copy(xv, xg, keep_sem.at[0])
    keep_x.start()

    a_here, b_here = x * (1 - k) + y * k, x * k + y * (1 - k)

    def place(a, b):
        return a * (1 - k) + b * k, a * k + b * (1 - k)

    def plane_device(a, b):
        px, py = place(a, b)
        return device(px, py, z, k)

    lane = lax.broadcasted_iota(jnp.int32, (ROWS, MAIN), 1)
    place_in_side = lane % SIDE

    def ahead(h):
        return 1 if h == 0 else 3

    def a_device(step):
        return plane_device((a_here + step) % 4, b_here)

    def b_device(step):
        return plane_device(a_here, (b_here + step) % 4)

    def first_copy(h, kind, src, step):
        at = h * 3 + kind
        return remote(src, r1.at[h, kind], p1s_sem.at[at], p1r_sem.at[at], a_device(step))

    def far_copy(h):
        return first_copy(h, 0, p1.at[(a_here + 2) % 4, h], ahead(h))

    def sum_copy(h):
        return first_copy(h, 1, m1.at[h], ahead(h))

    def near_copy(h):
        return first_copy(h, 2, p1.at[(a_here + 4 - ahead(h)) % 4, h], 4 - ahead(h))

    def second_copy(h, j):
        b = (b_here + j) % 4
        at = h * 3 + j - 1
        return remote(s2.at[b, h], r2.at[b_here, h], p2s_sem.at[at], p2r_sem.at[at], plane_device(a_here, b))

    def hidden_place(a, b, h):
        px, py = place(a, b)
        return hg.at[px, py, h]

    def hidden_first(h, j):
        at = h * 3 + j - 1
        return remote(
            hid.at[h], hidden_place(a_here, b_here, h), has_sem.at[at], har_sem.at[at], a_device(j)
        )

    def hidden_near(h, j, step):
        at = (h * 4 + j) * 3 + (0 if step == 1 else 1)
        here = hidden_place((a_here + 4 - j) % 4, b_here, h)
        return remote(hid.at[h] if j == 0 else here, here, hbs_sem.at[at], hbr_sem.at[at], b_device(step))

    def hidden_far(h, j):
        at = (h * 4 + j) * 3 + 2
        here = hidden_place((a_here + 4 - j) % 4, (b_here + 4 - ahead(h)) % 4, h)
        return remote(here, here, hbs_sem.at[at], hbr_sem.at[at], b_device(ahead(h)))

    def hidden_keep(h):
        return pltpu.make_async_copy(hid.at[h], hidden_place(a_here, b_here, h), keep_sem.at[2 + h])

    def put_rows(px, h, block, value):
        for py in range(Y):
            pa, pb = px * (1 - k) + py * k, px * k + py * (1 - k)
            p1[pa, h, pb, block] = value[py * ROWS : (py + 1) * ROWS].astype(SUM_TYPE)

    lanes = lax.broadcasted_iota(jnp.int32, (GRAN, MAIN), 1)

    def side_by_side(tails):
        return jnp.where(lanes < SIDE, tails[0], pltpu.roll(tails[1], SIDE, 1))

    def project_x(i, carry):
        px, h, pair = i // (CHUNKS * PAIRS), (i // PAIRS) % CHUNKS, i % PAIRS
        tails = []
        for side in range(2):
            at = pair + side * PAIRS
            s = h * PART + at
            e = jnp.minimum(gexp[px * SLOT + s], EXPERTS - 1)
            xt = xv[px, s].reshape(GRAN, DC)
            main = dot_nt(xt, wg[e, 0 : 2 * MAIN])
            put_rows(px, h, 3 * at, main[:, :MAIN])
            put_rows(px, h, 3 * at + 1, main[:, MAIN:])
            tails.append(dot_nt(xt, wg[e, 3 * MAIN : LANES]))
        put_rows(px, h, 3 * PART + pair, side_by_side(tails))
        return carry

    lax.fori_loop(0, X * CHUNKS * PAIRS, project_x, 0)
    for step in range(GROUP - 1):
        q_copy(step).wait_recv()
    own_q.wait()
    keep_q = pltpu.make_async_copy(qv, qg, keep_sem.at[1])
    keep_q.start()
    for h in range(CHUNKS):

        def project_q(i, carry):
            px, pair = i // PAIRS, i % PAIRS
            tails = []
            for side in range(2):
                at = pair + side * PAIRS
                s = h * PART + at
                e = jnp.minimum(gexp[px * SLOT + s], EXPERTS - 1)
                rows = dot_nt(qv[px, s].reshape(GRAN, DC), wg[e, 2 * MAIN : LANES])
                put_rows(px, h, 3 * at + 2, rows[:, :MAIN])
                tails.append(rows[:, MAIN:])
            tail = side_by_side(tails).astype(SUM_TYPE)
            for py in range(Y):
                pa, pb = px * (1 - k) + py * k, px * k + py * (1 - k)
                at = (pa, h, pb, 3 * PART + pair)
                p1[at] = jnp.where(place_in_side < 2 * TAIL, p1[at], tail[py * ROWS : (py + 1) * ROWS])
            return carry

        lax.fori_loop(0, X * PAIRS, project_q, 0)
        far_copy(h).start()
        near_copy(h).start()

    for h in range(CHUNKS):
        far_copy(h).wait_recv()

        def relay(b, carry):
            m1[h, b] = p1[(a_here + ahead(h)) % 4, h, b] + r1[h, 0, b]
            return carry

        lax.fori_loop(0, 4, relay, 0)
        sum_copy(h).start()

    for h in range(CHUNKS):
        near_copy(h).wait_recv()
        sum_copy(h).wait_recv()

        def sum_first(b, carry):
            s2[b, h] = p1[a_here, h, b] + r1[h, 1, b] + r1[h, 2, b]
            return carry

        lax.fori_loop(0, 4, sum_first, 0)
        for j in (2, 1, 3):
            second_copy(h, j).start()

    def shift(v, amount):
        return pltpu.roll(v, amount % MAIN, 1)

    for h in range(CHUNKS):
        for j in (1, 2, 3):
            second_copy(h, j).wait_recv()

        def total(block):
            value = s2[b_here, h, block]
            for j in (1, 2, 3):
                value += r2[(b_here + j) % 4, h, block]
            return value

        for at in range(PART):
            for m, value in enumerate(swiglu_rows(total(3 * at), total(3 * at + 1), total(3 * at + 2))):
                hid[h, 3 * at + m] = value.astype(jnp.bfloat16)
        for pair in range(PAIRS):
            tail = total(3 * PART + pair)
            first, second, third = swiglu_rows(tail, shift(tail, -TAIL), shift(tail, -2 * TAIL))
            packed = jnp.where(
                place_in_side < TAIL,
                first,
                jnp.where(place_in_side < 2 * TAIL, shift(second, TAIL), shift(third, 2 * TAIL)),
            )
            hid[h, 3 * PART + pair] = jnp.where(place_in_side < 3 * TAIL, packed, 0.0).astype(jnp.bfloat16)
        for j in (2, 1, 3):
            hidden_first(h, j).start()
        for step in (1, 3):
            hidden_near(h, 0, step).start()
        hidden_keep(h).start()

    arrivals = (0, 1, 3, 2)
    for n, j in enumerate(arrivals):
        if n + 1 < len(arrivals):
            for h in range(CHUNKS):
                hidden_first(h, arrivals[n + 1]).wait_recv()
                for step in (1, 3):
                    hidden_near(h, arrivals[n + 1], step).start()
        for h in range(CHUNKS):
            hidden_near(h, j, ahead(h)).wait_recv()
            hidden_far(h, j).start()
    for h in range(CHUNKS):
        for j in range(4):
            hidden_near(h, j, 4 - ahead(h)).wait_recv()
            hidden_far(h, j).wait_recv()
    for h in range(CHUNKS):
        for j in range(4):
            for step in (1, 3):
                hidden_near(h, j, step).wait_send()
            hidden_far(h, j).wait_send()
        for j in (1, 2, 3):
            hidden_first(h, j).wait_send()
            second_copy(h, j).wait_send()
        far_copy(h).wait_send()
        near_copy(h).wait_send()
        sum_copy(h).wait_send()
        hidden_keep(h).wait()
    for step in range(GROUP - 1):
        x_copy(step).wait_send()
        q_copy(step).wait_send()
    for go in rights + lefts + sibs:
        go.wait_send()
    wait_bytes(wr.at[pl.ds(0, 31)], ws_sem)
    keep_x.wait()
    keep_q.wait()


def rows_and_hidden(counts, column, dest, live, tok, cot, wts):
    hbm = pl.BlockSpec(memory_space=pl.ANY)
    smem = pl.BlockSpec(memory_space=pltpu.SMEM)
    dma = pltpu.SemaphoreType.DMA
    spread = pltpu.VMEM((X, SLOT, Y, ROWS, DC), jnp.bfloat16)
    sums = pltpu.VMEM((4, CHUNKS, 4, BLOCKS, ROWS, MAIN), SUM_TYPE)
    arrived = pltpu.VMEM((CHUNKS, 3, 4, BLOCKS, ROWS, MAIN), SUM_TYPE)
    halfway = pltpu.VMEM((4, CHUNKS, BLOCKS, ROWS, MAIN), jnp.float32)
    return pl.pallas_call(
        rows_kernel,
        out_shape=(
            jax.ShapeDtypeStruct((X, SLOT, Y, ROWS, DC), jnp.bfloat16),
            jax.ShapeDtypeStruct((X, SLOT, Y, ROWS, DC), jnp.bfloat16),
            jax.ShapeDtypeStruct((X, Y, CHUNKS, BLOCKS, ROWS, MAIN), jnp.bfloat16),
            jax.ShapeDtypeStruct((NGRAN,), jnp.int32),
        ),
        in_specs=[smem, smem, smem, smem, hbm, hbm, hbm],
        out_specs=(hbm, hbm, hbm, smem),
        scratch_shapes=[
            pltpu.VMEM((32, 32, DC), jnp.bfloat16),
            pltpu.VMEM((EXPERTS, 32, DC), jnp.bfloat16),
            pltpu.VMEM((EXPERTS, LANES, DC), jnp.bfloat16),
            spread,
            spread,
            sums,
            pltpu.VMEM((CHUNKS, 4, BLOCKS, ROWS, MAIN), SUM_TYPE),
            arrived,
            halfway,
            halfway,
            pltpu.VMEM((CHUNKS, BLOCKS, ROWS, MAIN), jnp.bfloat16),
            dma((GROUP,)),
            dma((GROUP,)),
            dma((GROUP,)),
            dma((GROUP,)),
            dma,
            dma,
            dma((3,)),
            dma((4,)),
            dma((4,)),
            dma((3,)),
            dma((3,)),
            dma((8,)),
            dma((8,)),
            dma((3 * CHUNKS,)),
            dma((3 * CHUNKS,)),
            dma((3 * CHUNKS,)),
            dma((3 * CHUNKS,)),
            dma((3 * CHUNKS,)),
            dma((3 * CHUNKS,)),
            dma((12 * CHUNKS,)),
            dma((12 * CHUNKS,)),
            dma((2 + CHUNKS,)),
        ],
        compiler_params=pltpu.CompilerParams(
            collective_id=0, has_side_effects=True, vmem_limit_bytes=VMEM_LIMIT
        ),
        name="rows_and_hidden",
    )(counts, column, dest, live, tok, cot, wts)


def grads_kernel(gexp, xg, qg, hg, out, xs, qs, hs, acc, rounded, source, rank, ends, in_sem, out_sem):
    loads = [
        pltpu.make_async_copy(ref, held, in_sem.at[i]) for i, (ref, held) in enumerate(((hg, hs), (xg, xs), (qg, qs)))
    ]
    for load in loads:
        load.start()

    def clear(at, carry):
        source[at] = -1
        return carry

    def count(g, carry):
        e = gexp[g]
        rank[g] = ends[e]
        ends[e] = ends[e] + 1
        return carry

    lax.fori_loop(0, MAX_TILES * PER_TILE, clear, 0)
    for e in range(EXPERTS + 1):
        ends[e] = 0
    lax.fori_loop(0, NGRAN, count, 0)
    end = 0
    for e in range(EXPERTS):
        end += (ends[e] + PER_TILE - 1) // PER_TILE
        ends[e] = end

    def fill(g, carry):
        e = gexp[g]

        @pl.when(e < EXPERTS)
        def _():
            start = jnp.where(e > 0, ends[jnp.maximum(e - 1, 0)], 0)
            source[start * PER_TILE + rank[g]] = g

        return carry

    lax.fori_loop(0, NGRAN, fill, 0)
    acc[...] = jnp.zeros_like(acc)
    for load in loads:
        load.wait()
    tail_rows = lax.broadcasted_iota(jnp.int32, (MAIN, DC), 0) % SIDE < 2 * TAIL
    side = lax.broadcasted_iota(jnp.int32, (ROWS, MAIN), 1) // SIDE

    def expert_step(e, start):
        def tile_step(t, carry):
            xt, qt, mains, tails = [], [], ([], [], []), []
            for j in range(PER_TILE):
                found = source[t * PER_TILE + j]
                g = jnp.maximum(found, 0)
                px, h, at = g // SLOT, (g % SLOT) // PART, g % PART
                xt.append(xs[g])
                qt.append(qs[g])
                for py in range(Y):
                    for m in range(3):
                        block = hs[px, py, h, 3 * at + m]
                        mains[m].append(jnp.where(found >= 0, block, jnp.zeros_like(block)))
                    block = hs[px, py, h, 3 * PART + at % PAIRS].astype(jnp.float32)
                    mine = side == jnp.where(found >= 0, at // PAIRS, 2)
                    tails.append(jnp.where(mine, block, 0.0).astype(jnp.bfloat16))
            xt, qt = jnp.concatenate(xt, axis=0), jnp.concatenate(qt, axis=0)
            for m, rows in ((0, xt), (1, xt), (2, qt)):
                acc[e, m * MAIN : (m + 1) * MAIN] += dot_tn(jnp.concatenate(mains[m], axis=0), rows)
            tail = jnp.concatenate(tails, axis=0)
            both = jnp.where(tail_rows, dot_tn(tail, xt), dot_tn(tail, qt))
            acc[e, 3 * MAIN : GROWS] += both[:SIDE] + both[SIDE:]
            return carry

        end = ends[e]
        lax.fori_loop(start, end, tile_step, 0)
        rounded[e] = acc[e].astype(jnp.bfloat16)
        pltpu.make_async_copy(rounded.at[e], out.at[e], out_sem.at[e]).start()
        return end

    lax.fori_loop(0, EXPERTS, expert_step, 0)

    def finish(e, carry):
        pltpu.make_async_copy(rounded.at[e], out.at[e], out_sem.at[e]).wait()
        return carry

    lax.fori_loop(0, EXPERTS, finish, 0)


def gradients(gexp, xg, qg, hg):
    hbm = pl.BlockSpec(memory_space=pl.ANY)
    return pl.pallas_call(
        grads_kernel,
        out_shape=jax.ShapeDtypeStruct((EXPERTS, GROWS, DC), jnp.bfloat16),
        in_specs=[pl.BlockSpec(memory_space=pltpu.SMEM), hbm, hbm, hbm],
        out_specs=hbm,
        scratch_shapes=[
            pltpu.VMEM(xg.shape, jnp.bfloat16),
            pltpu.VMEM(qg.shape, jnp.bfloat16),
            pltpu.VMEM(hg.shape, jnp.bfloat16),
            pltpu.VMEM((EXPERTS, GROWS, DC), jnp.float32),
            pltpu.VMEM((EXPERTS, GROWS, DC), jnp.bfloat16),
            pltpu.SMEM((MAX_TILES * PER_TILE,), jnp.int32),
            pltpu.SMEM((NGRAN,), jnp.int32),
            pltpu.SMEM((EXPERTS + 1,), jnp.int32),
            pltpu.SemaphoreType.DMA((3,)),
            pltpu.SemaphoreType.DMA((EXPERTS,)),
        ],
        compiler_params=pltpu.CompilerParams(vmem_limit_bytes=VMEM_LIMIT),
        name="gradients",
    )(gexp, xg, qg, hg)


QUART = HALF // 2
PACK = 96
SHARE = 54
WINDOW = 256
OFFSETS = (4, 3, -3, 2, -2, 1, -1, 0)


def reduce_kernel(
    grads, out, own, sib, sbuf, rbuf, fin, win, wide, packf, pack, got, gotf, os_sem, ts_sem, tr_sem, cs_sem, cr_sem, swap_sem, send, recv,
    keep_sem,
):
    x, y, z, k = coords()
    zh, zl = z // 4, z % 4
    sibling = device(x, y, z, 1 - k)
    barrier = pltpu.get_barrier_semaphore()

    def target(share):
        return share // 2, (share % 2) * 4 + y

    def greet_share(share, carry):
        ty, tz = target(share)

        @pl.when((ty != y) | (tz != z))
        def _():
            signal(barrier, device(x, ty, tz, k))

        return carry

    def greet_source(pz, carry):
        @pl.when((zl != y) | (pz != z))
        def _():
            signal(barrier, device(x, zl, pz, k))

        return carry

    ahead = (device(x, y, (z + 1) % Z, k), device(x, y, (z + Z - 1) % Z, k))
    signal(barrier, sibling)
    signal(barrier, ahead[0])
    signal(barrier, ahead[1])
    lax.fori_loop(0, 8, greet_share, 0)
    lax.fori_loop(0, 8, greet_source, 0)
    self_here = jnp.where(zl == y, 1, 0)
    pl.semaphore_wait(barrier, 19 - 2 * self_here)

    def half(e, which):
        return grads.at[e, pl.ds(pl.multiple_of(which * HALF, HALF), HALF), :]

    trades, keeps = {}, {}
    for i, off in enumerate(OFFSETS):
        e = (z + off + Z) % Z
        trades[off] = remote(half(e, 1 - k), sib.at[e], ts_sem.at[i], tr_sem.at[i], sibling)
        keeps[off] = pltpu.make_async_copy(half(e, k), own.at[e], os_sem.at[i])
        trades[off].start()
        keeps[off].start()
    trades[-4], keeps[-4] = trades[4], keeps[4]
    ready = set()

    def ours(off, j):
        if abs(off) % 8 == 4:
            off = 4
        if off not in ready:
            trades[off].wait_recv()
            keeps[off].wait()
            ready.add(off)
        e = (z + off + Z) % Z
        cut = slice(j * QUART, (j + 1) * QUART)
        return own[e, cut].astype(jnp.float32) + sib[e, cut].astype(jnp.float32)

    chain = {}
    for dist in (4, 3, 2, 1):
        for way in range(2):
            for j in range(2):
                longest = 4 if way == j else 3
                if dist > longest:
                    continue
                value = ours(dist if way == 0 else -dist, j)
                if dist < longest:
                    chain[way, j, dist + 1].wait_recv()
                    value += rbuf[way, j, dist].astype(jnp.float32)
                sbuf[way, j, dist - 1] = value.astype(jnp.bfloat16)
                at = (way * 2 + j) * 4 + dist - 1
                go = remote(
                    sbuf.at[way, j, dist - 1], rbuf.at[way, j, dist - 1], cs_sem.at[at], cr_sem.at[at], ahead[way]
                )
                go.start()
                chain[way, j, dist] = go
    for j in range(2):
        value = ours(0, j)
        for way in range(2):
            chain[way, j, 1].wait_recv()
            value += rbuf[way, j, 0].astype(jnp.float32)
        fin[pl.ds(pl.multiple_of(k * HALF + j * QUART, 16), QUART)] = value
    mine = fin.at[pl.ds(pl.multiple_of(k * HALF, HALF), HALF)]
    swap = remote(mine, mine, swap_sem.at[0], swap_sem.at[1], sibling)
    swap.start()
    swap.wait()

    low = fin[:, 0:WINDOW]
    high = pltpu.roll(fin[:, DC - WINDOW : DC], DC // 2, 1)
    win[...] = jnp.where(k == 0, low, high)
    first_half = lax.broadcasted_iota(jnp.int32, (SHARE // 2, MAIN), 1) < SIDE
    for share in range(8):
        for m in range(3):
            if share < 7:
                lo = m * MAIN + 18 * share
                wide[share, 18 * m : 18 * m + 18] = win[lo : lo + 18]
            else:
                lo = m * MAIN + 126
                wide[share, 18 * m : 18 * m + 2] = win[lo : lo + 2]
                lo = 3 * MAIN + m * TAIL
                wide[share, 18 * m + 2 : 18 * m + 18] = win[lo : lo + TAIL]
        packf[share, 80:PACK] = jnp.zeros((PACK - 80, MAIN), jnp.float32)
        packf[share, 0:SHARE] = wide[share, 0:SHARE, :MAIN]
        packf[share, SHARE : SHARE + SHARE // 2] = jnp.where(
            first_half,
            wide[share, 0 : SHARE // 2, MAIN:],
            pltpu.roll(wide[share, SHARE // 2 : SHARE, MAIN:], SIDE, 1),
        )
        pack[share] = packf[share].astype(jnp.bfloat16)

    def share_copy(share):
        ty, tz = target(share)
        return remote(pack.at[share], got.at[z], send.at[share], recv.at[z], device(x, ty, tz, k))

    def start(share, carry):
        ty, tz = target(share)

        @pl.when((ty != y) | (tz != z))
        def _():
            share_copy(share).start()

        @pl.when((ty == y) & (tz == z))
        def _():
            pltpu.make_async_copy(pack.at[share], got.at[z], keep_sem).start()

        return carry

    def finish_send(share, carry):
        ty, tz = target(share)

        @pl.when((ty != y) | (tz != z))
        def _():
            share_copy(share).wait_send()

        @pl.when((ty == y) & (tz == z))
        def _():
            pltpu.make_async_copy(pack.at[share], got.at[z], keep_sem).wait()

        return carry

    def finish_recv(pz, carry):
        @pl.when((zl != y) | (pz != z))
        def _():
            pltpu.make_async_copy(got.at[pz], got.at[pz], recv.at[pz]).wait()

        return carry

    lax.fori_loop(0, 8, start, 0)
    lax.fori_loop(0, 8, finish_send, 0)
    def unpack(e, carry):
        value = got[e].astype(jnp.float32)
        gotf[0:PACK, :MAIN] = value
        gotf[0 : SHARE // 2, MAIN:] = gotf[SHARE : SHARE + SHARE // 2, :MAIN]
        gotf[SHARE // 2 : SHARE, MAIN:] = pltpu.roll(gotf[SHARE : SHARE + SHARE // 2, :MAIN], SIDE, 1)
        for m in range(3):
            out[e, m] = gotf[18 * m : 18 * m + 18, : DC // 2].astype(jnp.bfloat16)
        return carry

    lax.fori_loop(0, 8, finish_recv, 0)
    lax.fori_loop(0, 8, unpack, 0)
    for off in OFFSETS:
        trades[off].wait_send()
    for go in chain.values():
        go.wait_send()


def reduce_grads(grads):
    dma = pltpu.SemaphoreType.DMA
    wide = pltpu.VMEM((EXPERTS, HALF, DC), jnp.bfloat16)
    steps = pltpu.VMEM((2, 2, 4, QUART, DC), jnp.bfloat16)
    return pl.pallas_call(
        reduce_kernel,
        out_shape=jax.ShapeDtypeStruct((EXPERTS, 3, 18, DC // 2), jnp.bfloat16),
        in_specs=[pl.BlockSpec(memory_space=pl.ANY)],
        out_specs=pl.BlockSpec(memory_space=pltpu.VMEM),
        scratch_shapes=[
            wide,
            wide,
            steps,
            steps,
            pltpu.VMEM((GROWS, DC), jnp.float32),
            pltpu.VMEM((GROWS, WINDOW), jnp.float32),
            pltpu.VMEM((8, SHARE + 2, WINDOW), jnp.float32),
            pltpu.VMEM((8, PACK, MAIN), jnp.float32),
            pltpu.VMEM((8, PACK, MAIN), jnp.bfloat16),
            pltpu.VMEM((8, PACK, MAIN), jnp.bfloat16),
            pltpu.VMEM((PACK, WINDOW), jnp.float32),
            dma((8,)),
            dma((8,)),
            dma((8,)),
            dma((16,)),
            dma((16,)),
            dma((2,)),
            dma((8,)),
            dma((8,)),
            dma,
        ],
        compiler_params=pltpu.CompilerParams(
            collective_id=1, has_side_effects=True, vmem_limit_bytes=VMEM_LIMIT
        ),
        name="reduce_grads",
    )(grads)


def on_device(tok, cot, wts, counts, column, dest, live):
    xg, qg, hg, gexp = rows_and_hidden(counts, column, dest, live, tok, cot, wts)
    xg = xg.reshape(NGRAN, GRAN, DC)
    qg = qg.reshape(NGRAN, GRAN, DC)
    return reduce_grads(gradients(gexp, xg, qg, hg))


def solution(mesh):
    placed = (
        P("expert", "dp", None),
        P("expert", "dp", None),
        P("expert", None, None, None),
        P(),
        P(),
        P(),
        P(),
    )
    return jax.shard_map(
        on_device,
        mesh=mesh,
        in_specs=placed,
        out_specs=P(None, None, "dp", "expert"),
        check_vma=False,
    )
```

```python
import jax
import jax.numpy as jnp
from jax import lax
from jax.experimental import pallas as pl
from jax.experimental.pallas import tpu as pltpu
from jax.sharding import PartitionSpec as P

MESH = pl.DeviceIdType.MESH
EXPERTS = 8
X, Y, Z = 4, 4, 8
GROUP = X * Y
D = 6144
DC = D // GROUP
SLOT = 8
ROWS = 16
MAIN = 128
TAIL = 16
LANES = 512
GROWS = 448
HALF = GROWS // 2
GRAN = Y * ROWS
NGRAN = X * SLOT
TILE = 256
PER_TILE = TILE // GRAN
MAX_TILES = NGRAN // PER_TILE + EXPERTS - 1
VMEM_LIMIT = 56 * 1024 * 1024


def coords():
    d = lax.axis_index("dp")
    c = lax.axis_index("expert")
    return c // 8, d // 2, (d % 2) * 4 + (c // 2) % 4, c % 2


def device(x, y, z, k):
    return (y * 2 + z // 4, (x * 4 + z % 4) * 2 + k)


MOVES = (
    (1, 0), (0, 1), (3, 0), (0, 3), (2, 0), (0, 2), (1, 1), (3, 3), (1, 3), (3, 1), (2, 1), (1, 2), (2, 3), (3, 2), (2, 2),
)


def plane_peer(x, y, step):
    dx, dy = MOVES[step]
    return (x + dx) % X, (y + dy) % Y


def signal(sem, target):
    pl.semaphore_signal(sem, inc=1, device_id=target, device_id_type=MESH)


def remote(src, dst, send, recv, target):
    return pltpu.make_async_remote_copy(
        src_ref=src, dst_ref=dst, send_sem=send, recv_sem=recv, device_id=target, device_id_type=MESH
    )


def wait_bytes(ref, sem):
    pltpu.make_async_copy(ref, ref, sem).wait()


def swiglu_rows(gate, up, grad):
    sig = jax.nn.sigmoid(gate)
    act = gate * sig
    return grad * up * sig * (1.0 + gate * (1.0 - sig)), grad * act, act * up


def dot_nt(a, b):
    return lax.dot_general(a, b, (((1,), (1,)), ((), ())), preferred_element_type=jnp.float32)


def dot_tn(a, b):
    return lax.dot_general(a, b, (((0,), (0,)), ((), ())), preferred_element_type=jnp.float32)


CHUNKS = 2
PART = SLOT // CHUNKS
PAIRS = PART // 2
BLOCKS = 3 * PART + PAIRS
SIDE = 64


def rows_kernel(
    counts, column, dest, live, tok, cot, wts, xg, qg, hg, gexp, wr, sel, wg, xv, qv, pg, mg, rg, sg, tg,
    pq, mq, rq, sq, tq, hid, xs_sem, xr_sem, qs_sem, qr_sem,
    ws_sem, wr_sem, own_sem, rs_sem, rr_sem, ls_sem, lr_sem, ss_sem, sr_sem, p1s_sem, p1r_sem, p2s_sem, p2r_sem,
    has_sem, har_sem, hbs_sem, hbr_sem, keep_sem,
):
    x, y, z, k = coords()
    zl = z % 4
    me_col = (x * 4 + zl) * 2 + k
    barrier = pltpu.get_barrier_semaphore()

    def greet_copies(dx, carry):
        cx = (x + dx) % X
        for dz in (0, 1, 7, 2, 6):
            for ck in range(2):
                if dz == 0:

                    @pl.when((dx > 0) | (k != ck))
                    def _():
                        signal(barrier, device(cx, y, z, ck))

                else:
                    signal(barrier, device(cx, y, (z + dz) % Z, ck))
        return carry

    for step in range(GROUP - 1):
        px, py = plane_peer(x, y, step)
        signal(barrier, device(px, py, z, k))
    lax.fori_loop(0, X, greet_copies, 0)
    right, left = device(x, y, (z + 1) % Z, k), device(x, y, (z + Z - 1) % Z, k)
    sibling = device(x, y, z, 1 - k)
    pl.semaphore_wait(barrier, GROUP - 1 + 39)

    def weight_piece(cx, cz, ck, part):
        t = jnp.minimum((cz * 2 + ck) * 2 + part, 26)
        tail = t // 24
        m = (t // 8) * (1 - tail) + (t - 24) * tail
        row = (t % 8) * 16 * (1 - tail) + 128 * tail
        return wts.at[
            0,
            m,
            pl.ds(pl.multiple_of(row, 16), 16),
            pl.ds(pl.multiple_of((cx * Y + y) * DC, 128), DC),
        ]

    def send_weights(dx, carry):
        cx = (x + dx) % X

        def send(cz, ck):
            for part in range(2):
                remote(
                    weight_piece(cx, cz, ck, part),
                    wr.at[me_col, pl.ds(part * 16, 16), :],
                    ws_sem,
                    wr_sem,
                    device(cx, y, cz, ck),
                ).start()

        for dz, ck in ((2, 0), (6, 1), (1, 0), (7, 0), (1, 1), (7, 1), (0, 0), (0, 1)):
            if dz == 0:

                @pl.when((dx > 0) | (k != ck))
                def _():
                    send(z, ck)

            else:
                send((z + dz) % Z, ck)
        return carry

    lax.fori_loop(0, X, send_weights, 0)
    for part in range(2):
        pltpu.make_async_copy(
            weight_piece(x, z, k, part), wr.at[me_col, pl.ds(part * 16, 16), :], wr_sem
        ).start()

    def columns(ref, px, py):
        return ref.at[:, :, pl.ds(pl.multiple_of((px * Y + py) * DC, 128), DC)]

    def x_copy(step):
        px, py = plane_peer(x, y, step)
        return remote(
            columns(tok, px, py), xv.at[x, :, y], xs_sem.at[step], xr_sem.at[step], device(px, py, z, k)
        )

    def q_copy(step):
        px, py = plane_peer(x, y, step)
        return remote(
            columns(cot, px, py), qv.at[x, :, y], qs_sem.at[step], qr_sem.at[step], device(px, py, z, k)
        )

    for step in range(GROUP - 1):
        x_copy(step).start()
    own_x = pltpu.make_async_copy(columns(tok, x, y), xv.at[x, :, y], own_sem.at[0])
    own_q = pltpu.make_async_copy(columns(cot, x, y), qv.at[x, :, y], own_sem.at[1])
    own_x.start()
    own_q.start()

    firsts, lasts = [], []
    for e in range(EXPERTS):
        firsts.append(lasts[-1] if e else 0)
        lasts.append(firsts[-1] + counts[e])

    def place_experts():
        def one(g, carry):
            col = ((g // SLOT) * 4 + zl) * 2 + k
            replica = dest[col, g % SLOT]
            expert = 0
            for e in range(EXPERTS - 1):
                expert += (lasts[e] <= replica).astype(jnp.int32)
            gexp[g] = jnp.where(g % SLOT < live[col], expert, EXPERTS)
            return carry

        lax.fori_loop(0, NGRAN, one, 0)

    wait_bytes(wr, wr_sem)
    for e in range(EXPERTS):
        sel[e] = wr[column[firsts[e]]]

    def chunk(pz):
        return wg.at[:, pl.ds(pl.multiple_of((pz * 2 + k) * 32, 32), 32), :]

    mine = chunk(z)
    own_w = pltpu.make_async_copy(sel, mine, own_sem.at[2])
    own_w.start()
    rights = [remote(sel, mine, rs_sem.at[0], rr_sem.at[0], right)]
    lefts = [remote(sel, mine, ls_sem.at[0], lr_sem.at[0], left)]
    sibs = [remote(sel, mine, ss_sem.at[0], sr_sem.at[0], sibling)]
    rights[0].start()
    lefts[0].start()
    sibs[0].start()
    for step in range(GROUP - 1):
        q_copy(step).start()
    place_experts()
    for t in range(1, 5):
        rights[t - 1].wait_recv()
        piece = chunk((z + Z - t) % Z)
        if t < 4:
            go = remote(piece, piece, rs_sem.at[t], rr_sem.at[t], right)
            go.start()
            rights.append(go)
        go = remote(piece, piece, ss_sem.at[2 * t - 1], sr_sem.at[2 * t - 1], sibling)
        go.start()
        sibs.append(go)
        if t < 4:
            lefts[t - 1].wait_recv()
            piece = chunk((z + t) % Z)
            if t < 3:
                go = remote(piece, piece, ls_sem.at[t], lr_sem.at[t], left)
                go.start()
                lefts.append(go)
            go = remote(piece, piece, ss_sem.at[2 * t], sr_sem.at[2 * t], sibling)
            go.start()
            sibs.append(go)
    for go in sibs:
        go.wait_recv()
    own_w.wait()

    for step in range(GROUP - 1):
        x_copy(step).wait_recv()
    own_x.wait()
    keep_x = pltpu.make_async_copy(xv, xg, keep_sem.at[0])
    keep_x.start()

    a_here, b_here = x * (1 - k) + y * k, x * k + y * (1 - k)

    def place(a, b):
        return a * (1 - k) + b * k, a * k + b * (1 - k)

    def plane_device(a, b):
        px, py = place(a, b)
        return device(px, py, z, k)

    lane = lax.broadcasted_iota(jnp.int32, (ROWS, MAIN), 1)
    place_in_side = lane % SIDE

    def ahead(h):
        return 1 if h == 0 else 3

    def a_device(step):
        return plane_device((a_here + step) % 4, b_here)

    def b_device(step):
        return plane_device(a_here, (b_here + step) % 4)

    parts = ((pg, mg, rg, sg, tg), (pq, mq, rq, sq, tq))

    def first_copy(c, kind, src, step):
        at = c * 3 + kind
        return remote(src, parts[c][2].at[kind], p1s_sem.at[at], p1r_sem.at[at], a_device(step))

    def far_copy(c):
        return first_copy(c, 0, parts[c][0].at[(a_here + 2) % 4], ahead(c))

    def sum_copy(c):
        return first_copy(c, 1, parts[c][1], ahead(c))

    def near_copy(c):
        return first_copy(c, 2, parts[c][0].at[(a_here + 4 - ahead(c)) % 4], 4 - ahead(c))

    def second_copy(c, j):
        b = (b_here + j) % 4
        at = c * 3 + j - 1
        return remote(
            parts[c][3].at[b], parts[c][4].at[b_here], p2s_sem.at[at], p2r_sem.at[at], plane_device(a_here, b)
        )

    def hidden_place(a, b, h):
        px, py = place(a, b)
        return hg.at[px, py, h]

    def hidden_first(h, j):
        at = h * 3 + j - 1
        return remote(
            hid.at[h], hidden_place(a_here, b_here, h), has_sem.at[at], har_sem.at[at], a_device(j)
        )

    def hidden_near(h, j, step):
        at = (h * 4 + j) * 3 + (0 if step == 1 else 1)
        here = hidden_place((a_here + 4 - j) % 4, b_here, h)
        return remote(hid.at[h] if j == 0 else here, here, hbs_sem.at[at], hbr_sem.at[at], b_device(step))

    def hidden_far(h, j):
        at = (h * 4 + j) * 3 + 2
        here = hidden_place((a_here + 4 - j) % 4, (b_here + 4 - ahead(h)) % 4, h)
        return remote(here, here, hbs_sem.at[at], hbr_sem.at[at], b_device(ahead(h)))

    def hidden_keep(h):
        return pltpu.make_async_copy(hid.at[h], hidden_place(a_here, b_here, h), keep_sem.at[2 + h])

    def put_rows(ref, px, block, value):
        for py in range(Y):
            pa, pb = px * (1 - k) + py * k, px * k + py * (1 - k)
            ref[pa, pb, block] = value[py * ROWS : (py + 1) * ROWS]

    lanes = lax.broadcasted_iota(jnp.int32, (GRAN, MAIN), 1)

    def side_by_side(tails):
        return jnp.where(lanes < SIDE, tails[0], pltpu.roll(tails[1], SIDE, 1))

    def project_x(i, carry):
        px, pair = i // (CHUNKS * PAIRS), i % (CHUNKS * PAIRS)
        tails = []
        for side in range(2):
            s = (pair // PAIRS) * PART + pair % PAIRS + side * PAIRS
            e = jnp.minimum(gexp[px * SLOT + s], EXPERTS - 1)
            xt = xv[px, s].reshape(GRAN, DC)
            main = dot_nt(xt, wg[e, 0 : 2 * MAIN])
            put_rows(pg, px, s, main[:, :MAIN])
            put_rows(pg, px, SLOT + s, main[:, MAIN:])
            tails.append(dot_nt(xt, wg[e, 3 * MAIN : LANES]))
        put_rows(pq, px, SLOT + pair, side_by_side(tails))
        return carry

    def project_q(i, carry):
        px, pair = i // (CHUNKS * PAIRS), i % (CHUNKS * PAIRS)
        tails = []
        for side in range(2):
            s = (pair // PAIRS) * PART + pair % PAIRS + side * PAIRS
            e = jnp.minimum(gexp[px * SLOT + s], EXPERTS - 1)
            rows = dot_nt(qv[px, s].reshape(GRAN, DC), wg[e, 2 * MAIN : LANES])
            put_rows(pq, px, s, rows[:, :MAIN])
            tails.append(rows[:, MAIN:])
        tail = side_by_side(tails)
        for py in range(Y):
            pa, pb = px * (1 - k) + py * k, px * k + py * (1 - k)
            at = (pa, pb, SLOT + pair)
            pq[at] = jnp.where(place_in_side < 2 * TAIL, pq[at], tail[py * ROWS : (py + 1) * ROWS])
        return carry

    def relay(c):
        mine, passed, came = parts[c][:3]

        def one(b, carry):
            passed[b] = mine[(a_here + ahead(c)) % 4, b] + came[0, b]
            return carry

        far_copy(c).wait_recv()
        lax.fori_loop(0, 4, one, 0)
        sum_copy(c).start()

    def add_up(c):
        mine, _, came, sums, _ = parts[c]

        def one(b, carry):
            sums[b] = mine[a_here, b] + came[1, b] + came[2, b]
            return carry

        near_copy(c).wait_recv()
        sum_copy(c).wait_recv()
        lax.fori_loop(0, 4, one, 0)
        for j in (2, 1, 3):
            second_copy(c, j).start()

    lax.fori_loop(0, X * CHUNKS * PAIRS, project_x, 0)
    far_copy(0).start()
    near_copy(0).start()
    relay(0)
    for step in range(GROUP - 1):
        q_copy(step).wait_recv()
    own_q.wait()
    keep_q = pltpu.make_async_copy(qv, qg, keep_sem.at[1])
    keep_q.start()
    lax.fori_loop(0, X * CHUNKS * PAIRS, project_q, 0)
    far_copy(1).start()
    near_copy(1).start()
    add_up(0)
    relay(1)
    add_up(1)

    def shift(v, amount):
        return pltpu.roll(v, amount % MAIN, 1)

    for c in range(2):
        for j in (1, 2, 3):
            second_copy(c, j).wait_recv()

    def total(c, block):
        value = parts[c][3][b_here, block]
        for j in (1, 2, 3):
            value += parts[c][4][(b_here + j) % 4, block]
        return value

    for h in range(CHUNKS):
        for at in range(PART):
            s = h * PART + at
            for m, value in enumerate(swiglu_rows(total(0, s), total(0, SLOT + s), total(1, s))):
                hid[h, 3 * at + m] = value.astype(jnp.bfloat16)
        for pair in range(PAIRS):
            tail = total(1, SLOT + h * PAIRS + pair)
            first, second, third = swiglu_rows(tail, shift(tail, -TAIL), shift(tail, -2 * TAIL))
            packed = jnp.where(
                place_in_side < TAIL,
                first,
                jnp.where(place_in_side < 2 * TAIL, shift(second, TAIL), shift(third, 2 * TAIL)),
            )
            hid[h, 3 * PART + pair] = jnp.where(place_in_side < 3 * TAIL, packed, 0.0).astype(jnp.bfloat16)
        for j in (2, 1, 3):
            hidden_first(h, j).start()
        for step in (1, 3):
            hidden_near(h, 0, step).start()
        hidden_keep(h).start()

    arrivals = (0, 1, 3, 2)
    for n, j in enumerate(arrivals):
        if n + 1 < len(arrivals):
            for h in range(CHUNKS):
                hidden_first(h, arrivals[n + 1]).wait_recv()
                for step in (1, 3):
                    hidden_near(h, arrivals[n + 1], step).start()
        for h in range(CHUNKS):
            hidden_near(h, j, ahead(h)).wait_recv()
            hidden_far(h, j).start()
    for h in range(CHUNKS):
        for j in range(4):
            hidden_near(h, j, 4 - ahead(h)).wait_recv()
            hidden_far(h, j).wait_recv()
    for h in range(CHUNKS):
        for j in range(4):
            for step in (1, 3):
                hidden_near(h, j, step).wait_send()
            hidden_far(h, j).wait_send()
        for j in (1, 2, 3):
            hidden_first(h, j).wait_send()
            second_copy(h, j).wait_send()
        far_copy(h).wait_send()
        near_copy(h).wait_send()
        sum_copy(h).wait_send()
        hidden_keep(h).wait()
    for step in range(GROUP - 1):
        x_copy(step).wait_send()
        q_copy(step).wait_send()
    for go in rights + lefts + sibs:
        go.wait_send()
    wait_bytes(wr.at[pl.ds(0, 31)], ws_sem)
    keep_x.wait()
    keep_q.wait()


def rows_and_hidden(counts, column, dest, live, tok, cot, wts):
    hbm = pl.BlockSpec(memory_space=pl.ANY)
    smem = pl.BlockSpec(memory_space=pltpu.SMEM)
    dma = pltpu.SemaphoreType.DMA
    spread = pltpu.VMEM((X, SLOT, Y, ROWS, DC), jnp.bfloat16)
    sums = []
    for blocks in (2 * SLOT, SLOT + CHUNKS * PAIRS):
        for lead in ((4, 4), (4,), (3, 4), (4,), (4,)):
            sums.append(pltpu.VMEM((*lead, blocks, ROWS, MAIN), jnp.float32))
    return pl.pallas_call(
        rows_kernel,
        out_shape=(
            jax.ShapeDtypeStruct((X, SLOT, Y, ROWS, DC), jnp.bfloat16),
            jax.ShapeDtypeStruct((X, SLOT, Y, ROWS, DC), jnp.bfloat16),
            jax.ShapeDtypeStruct((X, Y, CHUNKS, BLOCKS, ROWS, MAIN), jnp.bfloat16),
            jax.ShapeDtypeStruct((NGRAN,), jnp.int32),
        ),
        in_specs=[smem, smem, smem, smem, hbm, hbm, hbm],
        out_specs=(hbm, hbm, hbm, smem),
        scratch_shapes=[
            pltpu.VMEM((32, 32, DC), jnp.bfloat16),
            pltpu.VMEM((EXPERTS, 32, DC), jnp.bfloat16),
            pltpu.VMEM((EXPERTS, LANES, DC), jnp.bfloat16),
            spread,
            spread,
            *sums,
            pltpu.VMEM((CHUNKS, BLOCKS, ROWS, MAIN), jnp.bfloat16),
            dma((GROUP,)),
            dma((GROUP,)),
            dma((GROUP,)),
            dma((GROUP,)),
            dma,
            dma,
            dma((3,)),
            dma((4,)),
            dma((4,)),
            dma((3,)),
            dma((3,)),
            dma((8,)),
            dma((8,)),
            dma((3 * CHUNKS,)),
            dma((3 * CHUNKS,)),
            dma((3 * CHUNKS,)),
            dma((3 * CHUNKS,)),
            dma((3 * CHUNKS,)),
            dma((3 * CHUNKS,)),
            dma((12 * CHUNKS,)),
            dma((12 * CHUNKS,)),
            dma((2 + CHUNKS,)),
        ],
        compiler_params=pltpu.CompilerParams(
            collective_id=0, has_side_effects=True, vmem_limit_bytes=VMEM_LIMIT
        ),
        name="rows_and_hidden",
    )(counts, column, dest, live, tok, cot, wts)


def grads_kernel(gexp, xg, qg, hg, out, xs, qs, hs, acc, rounded, source, rank, ends, in_sem, out_sem):
    loads = [
        pltpu.make_async_copy(ref, held, in_sem.at[i]) for i, (ref, held) in enumerate(((hg, hs), (xg, xs), (qg, qs)))
    ]
    for load in loads:
        load.start()

    def clear(at, carry):
        source[at] = -1
        return carry

    def count(g, carry):
        e = gexp[g]
        rank[g] = ends[e]
        ends[e] = ends[e] + 1
        return carry

    lax.fori_loop(0, MAX_TILES * PER_TILE, clear, 0)
    for e in range(EXPERTS + 1):
        ends[e] = 0
    lax.fori_loop(0, NGRAN, count, 0)
    end = 0
    for e in range(EXPERTS):
        end += (ends[e] + PER_TILE - 1) // PER_TILE
        ends[e] = end

    def fill(g, carry):
        e = gexp[g]

        @pl.when(e < EXPERTS)
        def _():
            start = jnp.where(e > 0, ends[jnp.maximum(e - 1, 0)], 0)
            source[start * PER_TILE + rank[g]] = g

        return carry

    lax.fori_loop(0, NGRAN, fill, 0)
    acc[...] = jnp.zeros_like(acc)
    for load in loads:
        load.wait()
    tail_rows = lax.broadcasted_iota(jnp.int32, (MAIN, DC), 0) % SIDE < 2 * TAIL
    side = lax.broadcasted_iota(jnp.int32, (ROWS, MAIN), 1) // SIDE

    def expert_step(e, start):
        def tile_step(t, carry):
            xt, qt, mains, tails = [], [], ([], [], []), []
            for j in range(PER_TILE):
                found = source[t * PER_TILE + j]
                g = jnp.maximum(found, 0)
                px, h, at = g // SLOT, (g % SLOT) // PART, g % PART
                xt.append(xs[g])
                qt.append(qs[g])
                for py in range(Y):
                    for m in range(3):
                        block = hs[px, py, h, 3 * at + m]
                        mains[m].append(jnp.where(found >= 0, block, jnp.zeros_like(block)))
                    block = hs[px, py, h, 3 * PART + at % PAIRS].astype(jnp.float32)
                    mine = side == jnp.where(found >= 0, at // PAIRS, 2)
                    tails.append(jnp.where(mine, block, 0.0).astype(jnp.bfloat16))
            xt, qt = jnp.concatenate(xt, axis=0), jnp.concatenate(qt, axis=0)
            for m, rows in ((0, xt), (1, xt), (2, qt)):
                acc[e, m * MAIN : (m + 1) * MAIN] += dot_tn(jnp.concatenate(mains[m], axis=0), rows)
            tail = jnp.concatenate(tails, axis=0)
            both = jnp.where(tail_rows, dot_tn(tail, xt), dot_tn(tail, qt))
            acc[e, 3 * MAIN : GROWS] += both[:SIDE] + both[SIDE:]
            return carry

        end = ends[e]
        lax.fori_loop(start, end, tile_step, 0)
        rounded[e] = acc[e].astype(jnp.bfloat16)
        pltpu.make_async_copy(rounded.at[e], out.at[e], out_sem.at[e]).start()
        return end

    lax.fori_loop(0, EXPERTS, expert_step, 0)

    def finish(e, carry):
        pltpu.make_async_copy(rounded.at[e], out.at[e], out_sem.at[e]).wait()
        return carry

    lax.fori_loop(0, EXPERTS, finish, 0)


def gradients(gexp, xg, qg, hg):
    hbm = pl.BlockSpec(memory_space=pl.ANY)
    return pl.pallas_call(
        grads_kernel,
        out_shape=jax.ShapeDtypeStruct((EXPERTS, GROWS, DC), jnp.bfloat16),
        in_specs=[pl.BlockSpec(memory_space=pltpu.SMEM), hbm, hbm, hbm],
        out_specs=hbm,
        scratch_shapes=[
            pltpu.VMEM(xg.shape, jnp.bfloat16),
            pltpu.VMEM(qg.shape, jnp.bfloat16),
            pltpu.VMEM(hg.shape, jnp.bfloat16),
            pltpu.VMEM((EXPERTS, GROWS, DC), jnp.float32),
            pltpu.VMEM((EXPERTS, GROWS, DC), jnp.bfloat16),
            pltpu.SMEM((MAX_TILES * PER_TILE,), jnp.int32),
            pltpu.SMEM((NGRAN,), jnp.int32),
            pltpu.SMEM((EXPERTS + 1,), jnp.int32),
            pltpu.SemaphoreType.DMA((3,)),
            pltpu.SemaphoreType.DMA((EXPERTS,)),
        ],
        compiler_params=pltpu.CompilerParams(vmem_limit_bytes=VMEM_LIMIT),
        name="gradients",
    )(gexp, xg, qg, hg)


QUART = HALF // 2
PACK = 96
SHARE = 54
WINDOW = 256
OFFSETS = (4, 3, -3, 2, -2, 1, -1, 0)


def reduce_kernel(
    grads, out, own, sib, sbuf, rbuf, fin, win, wide, packf, pack, got, gotf, os_sem, ts_sem, tr_sem, cs_sem, cr_sem, swap_sem, send, recv,
    keep_sem,
):
    x, y, z, k = coords()
    zh, zl = z // 4, z % 4
    sibling = device(x, y, z, 1 - k)
    barrier = pltpu.get_barrier_semaphore()

    def target(share):
        return share // 2, (share % 2) * 4 + y

    def greet_share(share, carry):
        ty, tz = target(share)

        @pl.when((ty != y) | (tz != z))
        def _():
            signal(barrier, device(x, ty, tz, k))

        return carry

    def greet_source(pz, carry):
        @pl.when((zl != y) | (pz != z))
        def _():
            signal(barrier, device(x, zl, pz, k))

        return carry

    ahead = (device(x, y, (z + 1) % Z, k), device(x, y, (z + Z - 1) % Z, k))
    signal(barrier, sibling)
    signal(barrier, ahead[0])
    signal(barrier, ahead[1])
    lax.fori_loop(0, 8, greet_share, 0)
    lax.fori_loop(0, 8, greet_source, 0)
    self_here = jnp.where(zl == y, 1, 0)
    pl.semaphore_wait(barrier, 19 - 2 * self_here)

    def half(e, which):
        return grads.at[e, pl.ds(pl.multiple_of(which * HALF, HALF), HALF), :]

    trades, keeps = {}, {}
    for i, off in enumerate(OFFSETS):
        e = (z + off + Z) % Z
        trades[off] = remote(half(e, 1 - k), sib.at[e], ts_sem.at[i], tr_sem.at[i], sibling)
        keeps[off] = pltpu.make_async_copy(half(e, k), own.at[e], os_sem.at[i])
        trades[off].start()
        keeps[off].start()
    trades[-4], keeps[-4] = trades[4], keeps[4]
    ready = set()

    def ours(off, j):
        if abs(off) % 8 == 4:
            off = 4
        if off not in ready:
            trades[off].wait_recv()
            keeps[off].wait()
            ready.add(off)
        e = (z + off + Z) % Z
        cut = slice(j * QUART, (j + 1) * QUART)
        return own[e, cut].astype(jnp.float32) + sib[e, cut].astype(jnp.float32)

    chain = {}
    for dist in (4, 3, 2, 1):
        for way in range(2):
            for j in range(2):
                longest = 4 if way == j else 3
                if dist > longest:
                    continue
                value = ours(dist if way == 0 else -dist, j)
                if dist < longest:
                    chain[way, j, dist + 1].wait_recv()
                    value += rbuf[way, j, dist].astype(jnp.float32)
                sbuf[way, j, dist - 1] = value.astype(jnp.bfloat16)
                at = (way * 2 + j) * 4 + dist - 1
                go = remote(
                    sbuf.at[way, j, dist - 1], rbuf.at[way, j, dist - 1], cs_sem.at[at], cr_sem.at[at], ahead[way]
                )
                go.start()
                chain[way, j, dist] = go
    for j in range(2):
        value = ours(0, j)
        for way in range(2):
            chain[way, j, 1].wait_recv()
            value += rbuf[way, j, 0].astype(jnp.float32)
        fin[pl.ds(pl.multiple_of(k * HALF + j * QUART, 16), QUART)] = value
    mine = fin.at[pl.ds(pl.multiple_of(k * HALF, HALF), HALF)]
    swap = remote(mine, mine, swap_sem.at[0], swap_sem.at[1], sibling)
    swap.start()
    swap.wait()

    low = fin[:, 0:WINDOW]
    high = pltpu.roll(fin[:, DC - WINDOW : DC], DC // 2, 1)
    win[...] = jnp.where(k == 0, low, high)
    first_half = lax.broadcasted_iota(jnp.int32, (SHARE // 2, MAIN), 1) < SIDE
    for share in range(8):
        for m in range(3):
            if share < 7:
                lo = m * MAIN + 18 * share
                wide[share, 18 * m : 18 * m + 18] = win[lo : lo + 18]
            else:
                lo = m * MAIN + 126
                wide[share, 18 * m : 18 * m + 2] = win[lo : lo + 2]
                lo = 3 * MAIN + m * TAIL
                wide[share, 18 * m + 2 : 18 * m + 18] = win[lo : lo + TAIL]
        packf[share, 80:PACK] = jnp.zeros((PACK - 80, MAIN), jnp.float32)
        packf[share, 0:SHARE] = wide[share, 0:SHARE, :MAIN]
        packf[share, SHARE : SHARE + SHARE // 2] = jnp.where(
            first_half,
            wide[share, 0 : SHARE // 2, MAIN:],
            pltpu.roll(wide[share, SHARE // 2 : SHARE, MAIN:], SIDE, 1),
        )
        pack[share] = packf[share].astype(jnp.bfloat16)

    def share_copy(share):
        ty, tz = target(share)
        return remote(pack.at[share], got.at[z], send.at[share], recv.at[z], device(x, ty, tz, k))

    def start(share, carry):
        ty, tz = target(share)

        @pl.when((ty != y) | (tz != z))
        def _():
            share_copy(share).start()

        @pl.when((ty == y) & (tz == z))
        def _():
            pltpu.make_async_copy(pack.at[share], got.at[z], keep_sem).start()

        return carry

    def finish_send(share, carry):
        ty, tz = target(share)

        @pl.when((ty != y) | (tz != z))
        def _():
            share_copy(share).wait_send()

        @pl.when((ty == y) & (tz == z))
        def _():
            pltpu.make_async_copy(pack.at[share], got.at[z], keep_sem).wait()

        return carry

    def finish_recv(pz, carry):
        @pl.when((zl != y) | (pz != z))
        def _():
            pltpu.make_async_copy(got.at[pz], got.at[pz], recv.at[pz]).wait()

        return carry

    lax.fori_loop(0, 8, start, 0)
    lax.fori_loop(0, 8, finish_send, 0)
    def unpack(e, carry):
        value = got[e].astype(jnp.float32)
        gotf[0:PACK, :MAIN] = value
        gotf[0 : SHARE // 2, MAIN:] = gotf[SHARE : SHARE + SHARE // 2, :MAIN]
        gotf[SHARE // 2 : SHARE, MAIN:] = pltpu.roll(gotf[SHARE : SHARE + SHARE // 2, :MAIN], SIDE, 1)
        for m in range(3):
            out[e, m] = gotf[18 * m : 18 * m + 18, : DC // 2].astype(jnp.bfloat16)
        return carry

    lax.fori_loop(0, 8, finish_recv, 0)
    lax.fori_loop(0, 8, unpack, 0)
    for off in OFFSETS:
        trades[off].wait_send()
    for go in chain.values():
        go.wait_send()


def reduce_grads(grads):
    dma = pltpu.SemaphoreType.DMA
    wide = pltpu.VMEM((EXPERTS, HALF, DC), jnp.bfloat16)
    steps = pltpu.VMEM((2, 2, 4, QUART, DC), jnp.bfloat16)
    return pl.pallas_call(
        reduce_kernel,
        out_shape=jax.ShapeDtypeStruct((EXPERTS, 3, 18, DC // 2), jnp.bfloat16),
        in_specs=[pl.BlockSpec(memory_space=pl.ANY)],
        out_specs=pl.BlockSpec(memory_space=pltpu.VMEM),
        scratch_shapes=[
            wide,
            wide,
            steps,
            steps,
            pltpu.VMEM((GROWS, DC), jnp.float32),
            pltpu.VMEM((GROWS, WINDOW), jnp.float32),
            pltpu.VMEM((8, SHARE + 2, WINDOW), jnp.float32),
            pltpu.VMEM((8, PACK, MAIN), jnp.float32),
            pltpu.VMEM((8, PACK, MAIN), jnp.bfloat16),
            pltpu.VMEM((8, PACK, MAIN), jnp.bfloat16),
            pltpu.VMEM((PACK, WINDOW), jnp.float32),
            dma((8,)),
            dma((8,)),
            dma((8,)),
            dma((16,)),
            dma((16,)),
            dma((2,)),
            dma((8,)),
            dma((8,)),
            dma,
        ],
        compiler_params=pltpu.CompilerParams(
            collective_id=1, has_side_effects=True, vmem_limit_bytes=VMEM_LIMIT
        ),
        name="reduce_grads",
    )(grads)


def on_device(tok, cot, wts, counts, column, dest, live):
    xg, qg, hg, gexp = rows_and_hidden(counts, column, dest, live, tok, cot, wts)
    xg = xg.reshape(NGRAN, GRAN, DC)
    qg = qg.reshape(NGRAN, GRAN, DC)
    return reduce_grads(gradients(gexp, xg, qg, hg))


def solution(mesh):
    placed = (
        P("expert", "dp", None),
        P("expert", "dp", None),
        P("expert", None, None, None),
        P(),
        P(),
        P(),
        P(),
    )
    return jax.shard_map(
        on_device,
        mesh=mesh,
        in_specs=placed,
        out_specs=P(None, None, "dp", "expert"),
        check_vma=False,
    )
```

```python
import jax
import jax.numpy as jnp
from jax import lax
from jax.experimental import pallas as pl
from jax.experimental.pallas import tpu as pltpu
from jax.sharding import PartitionSpec as P

MESH = pl.DeviceIdType.MESH
EXPERTS = 8
X, Y, Z = 4, 4, 8
GROUP = X * Y
D = 6144
DC = D // GROUP
SLOT = 8
ROWS = 16
MAIN = 128
TAIL = 16
LANES = 512
GROWS = 448
HALF = GROWS // 2
GRAN = Y * ROWS
NGRAN = X * SLOT
TILE = 256
PER_TILE = TILE // GRAN
MAX_TILES = NGRAN // PER_TILE + EXPERTS - 1
VMEM_LIMIT = 56 * 1024 * 1024


def coords():
    d = lax.axis_index("dp")
    c = lax.axis_index("expert")
    return c // 8, d // 2, (d % 2) * 4 + (c // 2) % 4, c % 2


def device(x, y, z, k):
    return (y * 2 + z // 4, (x * 4 + z % 4) * 2 + k)


MOVES = (
    (1, 0), (0, 1), (3, 0), (0, 3), (2, 0), (0, 2), (1, 1), (3, 3), (1, 3), (3, 1), (2, 1), (1, 2), (2, 3), (3, 2), (2, 2),
)


def plane_peer(x, y, step):
    dx, dy = MOVES[step]
    return (x + dx) % X, (y + dy) % Y


def signal(sem, target):
    pl.semaphore_signal(sem, inc=1, device_id=target, device_id_type=MESH)


def remote(src, dst, send, recv, target):
    return pltpu.make_async_remote_copy(
        src_ref=src, dst_ref=dst, send_sem=send, recv_sem=recv, device_id=target, device_id_type=MESH
    )


def wait_bytes(ref, sem):
    pltpu.make_async_copy(ref, ref, sem).wait()


def swiglu_rows(gate, up, grad):
    sig = jax.nn.sigmoid(gate)
    act = gate * sig
    return grad * up * sig * (1.0 + gate * (1.0 - sig)), grad * act, act * up


def dot_nt(a, b):
    return lax.dot_general(a, b, (((1,), (1,)), ((), ())), preferred_element_type=jnp.float32)


def dot_tn(a, b):
    return lax.dot_general(a, b, (((0,), (0,)), ((), ())), preferred_element_type=jnp.float32)


CHUNKS = 4
PART = SLOT // CHUNKS
PAIRS = PART // 2
BLOCKS = 3 * PART + PAIRS
SIDE = 64
SUM_TYPE = jnp.float32


def rows_kernel(
    counts, column, dest, live, tok, cot, wts, xg, qg, hg, gexp, wr, sel, wg, xv, qv, p1, m1, r1, s2, r2, hid, xs_sem, xr_sem, qs_sem, qr_sem,
    ws_sem, wr_sem, own_sem, rs_sem, rr_sem, ls_sem, lr_sem, ss_sem, sr_sem, p1s_sem, p1r_sem, p2s_sem, p2r_sem,
    has_sem, har_sem, hbs_sem, hbr_sem, keep_sem,
):
    x, y, z, k = coords()
    zh, zl = z // 4, z % 4
    me_col = (x * 4 + zl) * 2 + k
    barrier = pltpu.get_barrier_semaphore()

    def greet_column(step, carry):
        signal(barrier, (y * 2 + zh, (me_col + step) % 32))
        return carry

    for step in range(GROUP - 1):
        px, py = plane_peer(x, y, step)
        signal(barrier, device(px, py, z, k))
    lax.fori_loop(1, 32, greet_column, 0)
    right, left = device(x, y, (z + 1) % Z, k), device(x, y, (z + Z - 1) % Z, k)
    sibling = device(x, y, z, 1 - k)
    signal(barrier, right)
    signal(barrier, left)
    pl.semaphore_wait(barrier, GROUP - 1 + 31 + 2)

    def weight_piece(col, part):
        cx, cz, ck = col // 8, zh * 4 + (col // 2) % 4, col % 2
        t = jnp.minimum((cz * 2 + ck) * 2 + part, 26)
        tail = t // 24
        m = (t // 8) * (1 - tail) + (t - 24) * tail
        row = (t % 8) * 16 * (1 - tail) + 128 * tail
        return wts.at[
            0,
            m,
            pl.ds(pl.multiple_of(row, 16), 16),
            pl.ds(pl.multiple_of((cx * Y + y) * DC, 128), DC),
        ]

    def send_weights(step, carry):
        col = (me_col + step) % 32
        for part in range(2):
            remote(
                weight_piece(col, part), wr.at[me_col, pl.ds(part * 16, 16), :], ws_sem, wr_sem, (y * 2 + zh, col)
            ).start()
        return carry

    lax.fori_loop(1, 32, send_weights, 0)
    for part in range(2):
        pltpu.make_async_copy(
            weight_piece(me_col, part), wr.at[me_col, pl.ds(part * 16, 16), :], wr_sem
        ).start()

    def columns(ref, px, py):
        return ref.at[:, :, pl.ds(pl.multiple_of((px * Y + py) * DC, 128), DC)]

    def x_copy(step):
        px, py = plane_peer(x, y, step)
        return remote(
            columns(tok, px, py), xv.at[x, :, y], xs_sem.at[step], xr_sem.at[step], device(px, py, z, k)
        )

    def q_copy(step):
        px, py = plane_peer(x, y, step)
        return remote(
            columns(cot, px, py), qv.at[x, :, y], qs_sem.at[step], qr_sem.at[step], device(px, py, z, k)
        )

    for step in range(GROUP - 1):
        x_copy(step).start()
    own_x = pltpu.make_async_copy(columns(tok, x, y), xv.at[x, :, y], own_sem.at[0])
    own_q = pltpu.make_async_copy(columns(cot, x, y), qv.at[x, :, y], own_sem.at[1])
    own_x.start()
    own_q.start()

    firsts, lasts = [], []
    for e in range(EXPERTS):
        firsts.append(lasts[-1] if e else 0)
        lasts.append(firsts[-1] + counts[e])

    def place_experts():
        def one(g, carry):
            col = ((g // SLOT) * 4 + zl) * 2 + k
            replica = dest[col, g % SLOT]
            expert = 0
            for e in range(EXPERTS - 1):
                expert += (lasts[e] <= replica).astype(jnp.int32)
            gexp[g] = jnp.where(g % SLOT < live[col], expert, EXPERTS)
            return carry

        lax.fori_loop(0, NGRAN, one, 0)

    wait_bytes(wr, wr_sem)
    for e in range(EXPERTS):
        sel[e] = wr[column[firsts[e]]]

    def chunk(pz):
        return wg.at[:, pl.ds(pl.multiple_of((pz * 2 + k) * 32, 32), 32), :]

    mine = chunk(z)
    own_w = pltpu.make_async_copy(sel, mine, own_sem.at[2])
    own_w.start()
    rights = [remote(sel, mine, rs_sem.at[0], rr_sem.at[0], right)]
    lefts = [remote(sel, mine, ls_sem.at[0], lr_sem.at[0], left)]
    sibs = [remote(sel, mine, ss_sem.at[0], sr_sem.at[0], sibling)]
    rights[0].start()
    lefts[0].start()
    sibs[0].start()
    for step in range(GROUP - 1):
        q_copy(step).start()
    place_experts()
    for t in range(1, 5):
        rights[t - 1].wait_recv()
        piece = chunk((z + Z - t) % Z)
        if t < 4:
            go = remote(piece, piece, rs_sem.at[t], rr_sem.at[t], right)
            go.start()
            rights.append(go)
        go = remote(piece, piece, ss_sem.at[2 * t - 1], sr_sem.at[2 * t - 1], sibling)
        go.start()
        sibs.append(go)
        if t < 4:
            lefts[t - 1].wait_recv()
            piece = chunk((z + t) % Z)
            if t < 3:
                go = remote(piece, piece, ls_sem.at[t], lr_sem.at[t], left)
                go.start()
                lefts.append(go)
            go = remote(piece, piece, ss_sem.at[2 * t], sr_sem.at[2 * t], sibling)
            go.start()
            sibs.append(go)
    for go in sibs:
        go.wait_recv()
    own_w.wait()

    for step in range(GROUP - 1):
        x_copy(step).wait_recv()
    own_x.wait()
    keep_x = pltpu.make_async_copy(xv, xg, keep_sem.at[0])
    keep_x.start()

    a_here, b_here = x * (1 - k) + y * k, x * k + y * (1 - k)

    def place(a, b):
        return a * (1 - k) + b * k, a * k + b * (1 - k)

    def plane_device(a, b):
        px, py = place(a, b)
        return device(px, py, z, k)

    lane = lax.broadcasted_iota(jnp.int32, (ROWS, MAIN), 1)
    place_in_side = lane % SIDE

    def ahead(h):
        return 1 if h % 2 == 0 else 3

    def a_device(step):
        return plane_device((a_here + step) % 4, b_here)

    def b_device(step):
        return plane_device(a_here, (b_here + step) % 4)

    def first_copy(h, kind, src, step):
        at = h * 3 + kind
        return remote(src, r1.at[h, kind], p1s_sem.at[at], p1r_sem.at[at], a_device(step))

    def far_copy(h):
        return first_copy(h, 0, p1.at[(a_here + 2) % 4, h], ahead(h))

    def sum_copy(h):
        return first_copy(h, 1, m1.at[h], ahead(h))

    def near_copy(h):
        return first_copy(h, 2, p1.at[(a_here + 4 - ahead(h)) % 4, h], 4 - ahead(h))

    def second_copy(h, j):
        b = (b_here + j) % 4
        at = h * 3 + j - 1
        return remote(s2.at[b, h], r2.at[b_here, h], p2s_sem.at[at], p2r_sem.at[at], plane_device(a_here, b))

    def hidden_place(a, b, h):
        px, py = place(a, b)
        return hg.at[px, py, h]

    def hidden_first(h, j):
        at = h * 3 + j - 1
        return remote(
            hid.at[h], hidden_place(a_here, b_here, h), has_sem.at[at], har_sem.at[at], a_device(j)
        )

    def hidden_near(h, j, step):
        at = (h * 4 + j) * 3 + (0 if step == 1 else 1)
        here = hidden_place((a_here + 4 - j) % 4, b_here, h)
        return remote(hid.at[h] if j == 0 else here, here, hbs_sem.at[at], hbr_sem.at[at], b_device(step))

    def hidden_far(h, j):
        at = (h * 4 + j) * 3 + 2
        here = hidden_place((a_here + 4 - j) % 4, (b_here + 4 - ahead(h)) % 4, h)
        return remote(here, here, hbs_sem.at[at], hbr_sem.at[at], b_device(ahead(h)))

    def hidden_keep(h):
        return pltpu.make_async_copy(hid.at[h], hidden_place(a_here, b_here, h), keep_sem.at[2 + h])

    def put_rows(px, h, block, value):
        for py in range(Y):
            pa, pb = px * (1 - k) + py * k, px * k + py * (1 - k)
            p1[pa, h, pb, block] = value[py * ROWS : (py + 1) * ROWS].astype(SUM_TYPE)

    lanes = lax.broadcasted_iota(jnp.int32, (GRAN, MAIN), 1)

    def side_by_side(tails):
        return jnp.where(lanes < SIDE, tails[0], pltpu.roll(tails[1], SIDE, 1))

    def project_x(i, carry):
        px, h, pair = i // (CHUNKS * PAIRS), (i // PAIRS) % CHUNKS, i % PAIRS
        tails = []
        for side in range(2):
            at = pair + side * PAIRS
            s = h * PART + at
            e = jnp.minimum(gexp[px * SLOT + s], EXPERTS - 1)
            xt = xv[px, s].reshape(GRAN, DC)
            main = dot_nt(xt, wg[e, 0 : 2 * MAIN])
            put_rows(px, h, 3 * at, main[:, :MAIN])
            put_rows(px, h, 3 * at + 1, main[:, MAIN:])
            tails.append(dot_nt(xt, wg[e, 3 * MAIN : LANES]))
        put_rows(px, h, 3 * PART + pair, side_by_side(tails))
        return carry

    lax.fori_loop(0, X * CHUNKS * PAIRS, project_x, 0)
    for step in range(GROUP - 1):
        q_copy(step).wait_recv()
    own_q.wait()
    keep_q = pltpu.make_async_copy(qv, qg, keep_sem.at[1])
    keep_q.start()
    for h in range(CHUNKS):

        def project_q(i, carry):
            px, pair = i // PAIRS, i % PAIRS
            tails = []
            for side in range(2):
                at = pair + side * PAIRS
                s = h * PART + at
                e = jnp.minimum(gexp[px * SLOT + s], EXPERTS - 1)
                rows = dot_nt(qv[px, s].reshape(GRAN, DC), wg[e, 2 * MAIN : LANES])
                put_rows(px, h, 3 * at + 2, rows[:, :MAIN])
                tails.append(rows[:, MAIN:])
            tail = side_by_side(tails).astype(SUM_TYPE)
            for py in range(Y):
                pa, pb = px * (1 - k) + py * k, px * k + py * (1 - k)
                at = (pa, h, pb, 3 * PART + pair)
                p1[at] = jnp.where(place_in_side < 2 * TAIL, p1[at], tail[py * ROWS : (py + 1) * ROWS])
            return carry

        lax.fori_loop(0, X * PAIRS, project_q, 0)
        far_copy(h).start()
        near_copy(h).start()

    for h in range(CHUNKS):
        far_copy(h).wait_recv()

        def relay(b, carry):
            m1[h, b] = p1[(a_here + ahead(h)) % 4, h, b] + r1[h, 0, b]
            return carry

        lax.fori_loop(0, 4, relay, 0)
        sum_copy(h).start()

    for h in range(CHUNKS):
        near_copy(h).wait_recv()
        sum_copy(h).wait_recv()

        def sum_first(b, carry):
            s2[b, h] = p1[a_here, h, b] + r1[h, 1, b] + r1[h, 2, b]
            return carry

        lax.fori_loop(0, 4, sum_first, 0)
        for j in (2, 1, 3):
            second_copy(h, j).start()

    def shift(v, amount):
        return pltpu.roll(v, amount % MAIN, 1)

    for h in range(CHUNKS):
        for j in (1, 2, 3):
            second_copy(h, j).wait_recv()

        def total(block):
            value = s2[b_here, h, block]
            for j in (1, 2, 3):
                value += r2[(b_here + j) % 4, h, block]
            return value

        for at in range(PART):
            for m, value in enumerate(swiglu_rows(total(3 * at), total(3 * at + 1), total(3 * at + 2))):
                hid[h, 3 * at + m] = value.astype(jnp.bfloat16)
        for pair in range(PAIRS):
            tail = total(3 * PART + pair)
            first, second, third = swiglu_rows(tail, shift(tail, -TAIL), shift(tail, -2 * TAIL))
            packed = jnp.where(
                place_in_side < TAIL,
                first,
                jnp.where(place_in_side < 2 * TAIL, shift(second, TAIL), shift(third, 2 * TAIL)),
            )
            hid[h, 3 * PART + pair] = jnp.where(place_in_side < 3 * TAIL, packed, 0.0).astype(jnp.bfloat16)
        for j in (2, 1, 3):
            hidden_first(h, j).start()
        for step in (1, 3):
            hidden_near(h, 0, step).start()
        hidden_keep(h).start()

    arrivals = (0, 1, 3, 2)
    for n, j in enumerate(arrivals):
        if n + 1 < len(arrivals):
            for h in range(CHUNKS):
                hidden_first(h, arrivals[n + 1]).wait_recv()
                for step in (1, 3):
                    hidden_near(h, arrivals[n + 1], step).start()
        for h in range(CHUNKS):
            hidden_near(h, j, ahead(h)).wait_recv()
            hidden_far(h, j).start()
    for h in range(CHUNKS):
        for j in range(4):
            hidden_near(h, j, 4 - ahead(h)).wait_recv()
            hidden_far(h, j).wait_recv()
    for h in range(CHUNKS):
        for j in range(4):
            for step in (1, 3):
                hidden_near(h, j, step).wait_send()
            hidden_far(h, j).wait_send()
        for j in (1, 2, 3):
            hidden_first(h, j).wait_send()
            second_copy(h, j).wait_send()
        far_copy(h).wait_send()
        near_copy(h).wait_send()
        sum_copy(h).wait_send()
        hidden_keep(h).wait()
    for step in range(GROUP - 1):
        x_copy(step).wait_send()
        q_copy(step).wait_send()
    for go in rights + lefts + sibs:
        go.wait_send()
    wait_bytes(wr.at[pl.ds(0, 31)], ws_sem)
    keep_x.wait()
    keep_q.wait()


def rows_and_hidden(counts, column, dest, live, tok, cot, wts):
    hbm = pl.BlockSpec(memory_space=pl.ANY)
    smem = pl.BlockSpec(memory_space=pltpu.SMEM)
    dma = pltpu.SemaphoreType.DMA
    spread = pltpu.VMEM((X, SLOT, Y, ROWS, DC), jnp.bfloat16)
    sums = pltpu.VMEM((4, CHUNKS, 4, BLOCKS, ROWS, MAIN), SUM_TYPE)
    arrived = pltpu.VMEM((CHUNKS, 3, 4, BLOCKS, ROWS, MAIN), SUM_TYPE)
    halfway = pltpu.VMEM((4, CHUNKS, BLOCKS, ROWS, MAIN), jnp.float32)
    return pl.pallas_call(
        rows_kernel,
        out_shape=(
            jax.ShapeDtypeStruct((X, SLOT, Y, ROWS, DC), jnp.bfloat16),
            jax.ShapeDtypeStruct((X, SLOT, Y, ROWS, DC), jnp.bfloat16),
            jax.ShapeDtypeStruct((X, Y, CHUNKS, BLOCKS, ROWS, MAIN), jnp.bfloat16),
            jax.ShapeDtypeStruct((NGRAN,), jnp.int32),
        ),
        in_specs=[smem, smem, smem, smem, hbm, hbm, hbm],
        out_specs=(hbm, hbm, pl.BlockSpec(memory_space=pltpu.VMEM), smem),
        scratch_shapes=[
            pltpu.VMEM((32, 32, DC), jnp.bfloat16),
            pltpu.VMEM((EXPERTS, 32, DC), jnp.bfloat16),
            pltpu.VMEM((EXPERTS, LANES, DC), jnp.bfloat16),
            spread,
            spread,
            sums,
            pltpu.VMEM((CHUNKS, 4, BLOCKS, ROWS, MAIN), SUM_TYPE),
            arrived,
            halfway,
            halfway,
            pltpu.VMEM((CHUNKS, BLOCKS, ROWS, MAIN), jnp.bfloat16),
            dma((GROUP,)),
            dma((GROUP,)),
            dma((GROUP,)),
            dma((GROUP,)),
            dma,
            dma,
            dma((3,)),
            dma((4,)),
            dma((4,)),
            dma((3,)),
            dma((3,)),
            dma((8,)),
            dma((8,)),
            dma((3 * CHUNKS,)),
            dma((3 * CHUNKS,)),
            dma((3 * CHUNKS,)),
            dma((3 * CHUNKS,)),
            dma((3 * CHUNKS,)),
            dma((3 * CHUNKS,)),
            dma((12 * CHUNKS,)),
            dma((12 * CHUNKS,)),
            dma((2 + CHUNKS,)),
        ],
        compiler_params=pltpu.CompilerParams(
            collective_id=0, has_side_effects=True, vmem_limit_bytes=VMEM_LIMIT
        ),
        name="rows_and_hidden",
    )(counts, column, dest, live, tok, cot, wts)


def grads_kernel(gexp, xg, qg, hg, out, xs, qs, hs, acc, rounded, source, rank, ends, in_sem, out_sem):
    loads = [
        pltpu.make_async_copy(ref, held, in_sem.at[i]) for i, (ref, held) in enumerate(((hg, hs), (xg, xs), (qg, qs)))
    ]
    for load in loads:
        load.start()

    def clear(at, carry):
        source[at] = -1
        return carry

    def count(g, carry):
        e = gexp[g]
        rank[g] = ends[e]
        ends[e] = ends[e] + 1
        return carry

    lax.fori_loop(0, MAX_TILES * PER_TILE, clear, 0)
    for e in range(EXPERTS + 1):
        ends[e] = 0
    lax.fori_loop(0, NGRAN, count, 0)
    end = 0
    for e in range(EXPERTS):
        end += (ends[e] + PER_TILE - 1) // PER_TILE
        ends[e] = end

    def fill(g, carry):
        e = gexp[g]

        @pl.when(e < EXPERTS)
        def _():
            start = jnp.where(e > 0, ends[jnp.maximum(e - 1, 0)], 0)
            source[start * PER_TILE + rank[g]] = g

        return carry

    lax.fori_loop(0, NGRAN, fill, 0)
    acc[...] = jnp.zeros_like(acc)
    for load in loads:
        load.wait()
    tail_rows = lax.broadcasted_iota(jnp.int32, (MAIN, DC), 0) % SIDE < 2 * TAIL
    side = lax.broadcasted_iota(jnp.int32, (ROWS, MAIN), 1) // SIDE

    def expert_step(e, start):
        def tile_step(t, carry):
            xt, qt, mains, tails = [], [], ([], [], []), []
            for j in range(PER_TILE):
                found = source[t * PER_TILE + j]
                g = jnp.maximum(found, 0)
                px, h, at = g // SLOT, (g % SLOT) // PART, g % PART
                xt.append(xs[g])
                qt.append(qs[g])
                for py in range(Y):
                    for m in range(3):
                        block = hs[px, py, h, 3 * at + m]
                        mains[m].append(jnp.where(found >= 0, block, jnp.zeros_like(block)))
                    block = hs[px, py, h, 3 * PART + at % PAIRS].astype(jnp.float32)
                    mine = side == jnp.where(found >= 0, at // PAIRS, 2)
                    tails.append(jnp.where(mine, block, 0.0).astype(jnp.bfloat16))
            xt, qt = jnp.concatenate(xt, axis=0), jnp.concatenate(qt, axis=0)
            for m, rows in ((0, xt), (1, xt), (2, qt)):
                acc[e, m * MAIN : (m + 1) * MAIN] += dot_tn(jnp.concatenate(mains[m], axis=0), rows)
            tail = jnp.concatenate(tails, axis=0)
            both = jnp.where(tail_rows, dot_tn(tail, xt), dot_tn(tail, qt))
            acc[e, 3 * MAIN : GROWS] += both[:SIDE] + both[SIDE:]
            return carry

        end = ends[e]
        lax.fori_loop(start, end, tile_step, 0)
        rounded[e] = acc[e].astype(jnp.bfloat16)
        pltpu.make_async_copy(rounded.at[e], out.at[e], out_sem.at[e]).start()
        return end

    lax.fori_loop(0, EXPERTS, expert_step, 0)

    def finish(e, carry):
        pltpu.make_async_copy(rounded.at[e], out.at[e], out_sem.at[e]).wait()
        return carry

    lax.fori_loop(0, EXPERTS, finish, 0)


def gradients(gexp, xg, qg, hg):
    hbm = pl.BlockSpec(memory_space=pl.ANY)
    return pl.pallas_call(
        grads_kernel,
        out_shape=jax.ShapeDtypeStruct((EXPERTS, GROWS, DC), jnp.bfloat16),
        in_specs=[pl.BlockSpec(memory_space=pltpu.SMEM), hbm, hbm, hbm],
        out_specs=hbm,
        scratch_shapes=[
            pltpu.VMEM(xg.shape, jnp.bfloat16),
            pltpu.VMEM(qg.shape, jnp.bfloat16),
            pltpu.VMEM(hg.shape, jnp.bfloat16),
            pltpu.VMEM((EXPERTS, GROWS, DC), jnp.float32),
            pltpu.VMEM((EXPERTS, GROWS, DC), jnp.bfloat16),
            pltpu.SMEM((MAX_TILES * PER_TILE,), jnp.int32),
            pltpu.SMEM((NGRAN,), jnp.int32),
            pltpu.SMEM((EXPERTS + 1,), jnp.int32),
            pltpu.SemaphoreType.DMA((3,)),
            pltpu.SemaphoreType.DMA((EXPERTS,)),
        ],
        compiler_params=pltpu.CompilerParams(vmem_limit_bytes=VMEM_LIMIT),
        name="gradients",
    )(gexp, xg, qg, hg)


QUART = HALF // 2
PACK = 96
SHARE = 54
WINDOW = 256
OFFSETS = (4, 3, -3, 2, -2, 1, -1, 0)


def reduce_kernel(
    grads, out, own, sib, sbuf, rbuf, fin, win, wide, packf, pack, got, gotf, os_sem, ts_sem, tr_sem, cs_sem, cr_sem, swap_sem, send, recv,
    keep_sem,
):
    x, y, z, k = coords()
    zh, zl = z // 4, z % 4
    sibling = device(x, y, z, 1 - k)
    barrier = pltpu.get_barrier_semaphore()

    def target(share):
        return share // 2, (share % 2) * 4 + y

    def greet_share(share, carry):
        ty, tz = target(share)

        @pl.when((ty != y) | (tz != z))
        def _():
            signal(barrier, device(x, ty, tz, k))

        return carry

    def greet_source(pz, carry):
        @pl.when((zl != y) | (pz != z))
        def _():
            signal(barrier, device(x, zl, pz, k))

        return carry

    ahead = (device(x, y, (z + 1) % Z, k), device(x, y, (z + Z - 1) % Z, k))
    signal(barrier, sibling)
    signal(barrier, ahead[0])
    signal(barrier, ahead[1])
    lax.fori_loop(0, 8, greet_share, 0)
    lax.fori_loop(0, 8, greet_source, 0)
    self_here = jnp.where(zl == y, 1, 0)
    pl.semaphore_wait(barrier, 19 - 2 * self_here)

    def half(e, which):
        return grads.at[e, pl.ds(pl.multiple_of(which * HALF, HALF), HALF), :]

    trades, keeps = {}, {}
    for i, off in enumerate(OFFSETS):
        e = (z + off + Z) % Z
        trades[off] = remote(half(e, 1 - k), sib.at[e], ts_sem.at[i], tr_sem.at[i], sibling)
        keeps[off] = pltpu.make_async_copy(half(e, k), own.at[e], os_sem.at[i])
        trades[off].start()
        keeps[off].start()
    trades[-4], keeps[-4] = trades[4], keeps[4]
    ready = set()

    def ours(off, j):
        if abs(off) % 8 == 4:
            off = 4
        if off not in ready:
            trades[off].wait_recv()
            keeps[off].wait()
            ready.add(off)
        e = (z + off + Z) % Z
        cut = slice(j * QUART, (j + 1) * QUART)
        return own[e, cut].astype(jnp.float32) + sib[e, cut].astype(jnp.float32)

    chain = {}
    for dist in (4, 3, 2, 1):
        for way in range(2):
            for j in range(2):
                longest = 4 if way == j else 3
                if dist > longest:
                    continue
                value = ours(dist if way == 0 else -dist, j)
                if dist < longest:
                    chain[way, j, dist + 1].wait_recv()
                    value += rbuf[way, j, dist].astype(jnp.float32)
                sbuf[way, j, dist - 1] = value.astype(jnp.bfloat16)
                at = (way * 2 + j) * 4 + dist - 1
                go = remote(
                    sbuf.at[way, j, dist - 1], rbuf.at[way, j, dist - 1], cs_sem.at[at], cr_sem.at[at], ahead[way]
                )
                go.start()
                chain[way, j, dist] = go
    for j in range(2):
        value = ours(0, j)
        for way in range(2):
            chain[way, j, 1].wait_recv()
            value += rbuf[way, j, 0].astype(jnp.float32)
        fin[pl.ds(pl.multiple_of(k * HALF + j * QUART, 16), QUART)] = value
    mine = fin.at[pl.ds(pl.multiple_of(k * HALF, HALF), HALF)]
    swap = remote(mine, mine, swap_sem.at[0], swap_sem.at[1], sibling)
    swap.start()
    swap.wait()

    low = fin[:, 0:WINDOW]
    high = pltpu.roll(fin[:, DC - WINDOW : DC], DC // 2, 1)
    win[...] = jnp.where(k == 0, low, high)
    first_half = lax.broadcasted_iota(jnp.int32, (SHARE // 2, MAIN), 1) < SIDE
    for share in range(8):
        for m in range(3):
            if share < 7:
                lo = m * MAIN + 18 * share
                wide[share, 18 * m : 18 * m + 18] = win[lo : lo + 18]
            else:
                lo = m * MAIN + 126
                wide[share, 18 * m : 18 * m + 2] = win[lo : lo + 2]
                lo = 3 * MAIN + m * TAIL
                wide[share, 18 * m + 2 : 18 * m + 18] = win[lo : lo + TAIL]
        packf[share, 80:PACK] = jnp.zeros((PACK - 80, MAIN), jnp.float32)
        packf[share, 0:SHARE] = wide[share, 0:SHARE, :MAIN]
        packf[share, SHARE : SHARE + SHARE // 2] = jnp.where(
            first_half,
            wide[share, 0 : SHARE // 2, MAIN:],
            pltpu.roll(wide[share, SHARE // 2 : SHARE, MAIN:], SIDE, 1),
        )
        pack[share] = packf[share].astype(jnp.bfloat16)

    def share_copy(share):
        ty, tz = target(share)
        return remote(pack.at[share], got.at[z], send.at[share], recv.at[z], device(x, ty, tz, k))

    def start(share, carry):
        ty, tz = target(share)

        @pl.when((ty != y) | (tz != z))
        def _():
            share_copy(share).start()

        @pl.when((ty == y) & (tz == z))
        def _():
            pltpu.make_async_copy(pack.at[share], got.at[z], keep_sem).start()

        return carry

    def finish_send(share, carry):
        ty, tz = target(share)

        @pl.when((ty != y) | (tz != z))
        def _():
            share_copy(share).wait_send()

        @pl.when((ty == y) & (tz == z))
        def _():
            pltpu.make_async_copy(pack.at[share], got.at[z], keep_sem).wait()

        return carry

    def finish_recv(pz, carry):
        @pl.when((zl != y) | (pz != z))
        def _():
            pltpu.make_async_copy(got.at[pz], got.at[pz], recv.at[pz]).wait()

        return carry

    lax.fori_loop(0, 8, start, 0)
    lax.fori_loop(0, 8, finish_send, 0)
    def unpack(e, carry):
        value = got[e].astype(jnp.float32)
        gotf[0:PACK, :MAIN] = value
        gotf[0 : SHARE // 2, MAIN:] = gotf[SHARE : SHARE + SHARE // 2, :MAIN]
        gotf[SHARE // 2 : SHARE, MAIN:] = pltpu.roll(gotf[SHARE : SHARE + SHARE // 2, :MAIN], SIDE, 1)
        for m in range(3):
            out[e, m] = gotf[18 * m : 18 * m + 18, : DC // 2].astype(jnp.bfloat16)
        return carry

    lax.fori_loop(0, 8, finish_recv, 0)
    lax.fori_loop(0, 8, unpack, 0)
    for off in OFFSETS:
        trades[off].wait_send()
    for go in chain.values():
        go.wait_send()


def reduce_grads(grads):
    dma = pltpu.SemaphoreType.DMA
    wide = pltpu.VMEM((EXPERTS, HALF, DC), jnp.bfloat16)
    steps = pltpu.VMEM((2, 2, 4, QUART, DC), jnp.bfloat16)
    return pl.pallas_call(
        reduce_kernel,
        out_shape=jax.ShapeDtypeStruct((EXPERTS, 3, 18, DC // 2), jnp.bfloat16),
        in_specs=[pl.BlockSpec(memory_space=pl.ANY)],
        out_specs=pl.BlockSpec(memory_space=pltpu.VMEM),
        scratch_shapes=[
            wide,
            wide,
            steps,
            steps,
            pltpu.VMEM((GROWS, DC), jnp.float32),
            pltpu.VMEM((GROWS, WINDOW), jnp.float32),
            pltpu.VMEM((8, SHARE + 2, WINDOW), jnp.float32),
            pltpu.VMEM((8, PACK, MAIN), jnp.float32),
            pltpu.VMEM((8, PACK, MAIN), jnp.bfloat16),
            pltpu.VMEM((8, PACK, MAIN), jnp.bfloat16),
            pltpu.VMEM((PACK, WINDOW), jnp.float32),
            dma((8,)),
            dma((8,)),
            dma((8,)),
            dma((16,)),
            dma((16,)),
            dma((2,)),
            dma((8,)),
            dma((8,)),
            dma,
        ],
        compiler_params=pltpu.CompilerParams(
            collective_id=1, has_side_effects=True, vmem_limit_bytes=VMEM_LIMIT
        ),
        name="reduce_grads",
    )(grads)


def on_device(tok, cot, wts, counts, column, dest, live):
    xg, qg, hg, gexp = rows_and_hidden(counts, column, dest, live, tok, cot, wts)
    xg = xg.reshape(NGRAN, GRAN, DC)
    qg = qg.reshape(NGRAN, GRAN, DC)
    return reduce_grads(gradients(gexp, xg, qg, hg))


def solution(mesh):
    placed = (
        P("expert", "dp", None),
        P("expert", "dp", None),
        P("expert", None, None, None),
        P(),
        P(),
        P(),
        P(),
    )
    return jax.shard_map(
        on_device,
        mesh=mesh,
        in_specs=placed,
        out_specs=P(None, None, "dp", "expert"),
        check_vma=False,
    )
```

```python
import jax
import jax.numpy as jnp
from jax import lax
from jax.experimental import pallas as pl
from jax.experimental.pallas import tpu as pltpu
from jax.sharding import PartitionSpec as P

MESH = pl.DeviceIdType.MESH
EXPERTS = 8
X, Y, Z = 4, 4, 8
GROUP = X * Y
D = 6144
DC = D // GROUP
SLOT = 8
ROWS = 16
MAIN = 128
TAIL = 16
LANES = 512
GROWS = 448
HALF = GROWS // 2
GRAN = Y * ROWS
NGRAN = X * SLOT
TILE = 256
PER_TILE = TILE // GRAN
MAX_TILES = NGRAN // PER_TILE + EXPERTS - 1
VMEM_LIMIT = 56 * 1024 * 1024


def coords():
    d = lax.axis_index("dp")
    c = lax.axis_index("expert")
    return c // 8, d // 2, (d % 2) * 4 + (c // 2) % 4, c % 2


def device(x, y, z, k):
    return (y * 2 + z // 4, (x * 4 + z % 4) * 2 + k)


MOVES = (
    (1, 0), (0, 1), (3, 0), (0, 3), (2, 0), (0, 2), (1, 1), (3, 3), (1, 3), (3, 1), (2, 1), (1, 2), (2, 3), (3, 2), (2, 2),
)


def plane_peer(x, y, step):
    dx, dy = MOVES[step]
    return (x + dx) % X, (y + dy) % Y


def signal(sem, target):
    pl.semaphore_signal(sem, inc=1, device_id=target, device_id_type=MESH)


def remote(src, dst, send, recv, target):
    return pltpu.make_async_remote_copy(
        src_ref=src, dst_ref=dst, send_sem=send, recv_sem=recv, device_id=target, device_id_type=MESH
    )


def wait_bytes(ref, sem):
    pltpu.make_async_copy(ref, ref, sem).wait()


def swiglu_rows(gate, up, grad):
    sig = jax.nn.sigmoid(gate)
    act = gate * sig
    return grad * up * sig * (1.0 + gate * (1.0 - sig)), grad * act, act * up


def dot_nt(a, b):
    return lax.dot_general(a, b, (((1,), (1,)), ((), ())), preferred_element_type=jnp.float32)


def dot_tn(a, b):
    return lax.dot_general(a, b, (((0,), (0,)), ((), ())), preferred_element_type=jnp.float32)


CHUNKS = 4
PART = SLOT // CHUNKS
PAIRS = PART // 2
BLOCKS = 3 * PART + PAIRS
SIDE = 64
SUM_TYPE = jnp.float32


def rows_kernel(
    counts, column, dest, live, tok, cot, wts, xg, qg, hg, gexp, wr, sel, wg, xv, qv, p1, m1, r1, n1, rn, s2, r2, hid, xs_sem, xr_sem, qs_sem, qr_sem,
    ws_sem, wr_sem, own_sem, rs_sem, rr_sem, ls_sem, lr_sem, ss_sem, sr_sem, p1s_sem, p1r_sem, p2s_sem, p2r_sem,
    has_sem, har_sem, hbs_sem, hbr_sem, keep_sem,
):
    x, y, z, k = coords()
    zh, zl = z // 4, z % 4
    me_col = (x * 4 + zl) * 2 + k
    barrier = pltpu.get_barrier_semaphore()

    def greet_column(step, carry):
        signal(barrier, (y * 2 + zh, (me_col + step) % 32))
        return carry

    for step in range(GROUP - 1):
        px, py = plane_peer(x, y, step)
        signal(barrier, device(px, py, z, k))
    lax.fori_loop(1, 32, greet_column, 0)
    right, left = device(x, y, (z + 1) % Z, k), device(x, y, (z + Z - 1) % Z, k)
    sibling = device(x, y, z, 1 - k)
    signal(barrier, right)
    signal(barrier, left)
    pl.semaphore_wait(barrier, GROUP - 1 + 31 + 2)

    def weight_piece(col, part):
        cx, cz, ck = col // 8, zh * 4 + (col // 2) % 4, col % 2
        t = jnp.minimum((cz * 2 + ck) * 2 + part, 26)
        tail = t // 24
        m = (t // 8) * (1 - tail) + (t - 24) * tail
        row = (t % 8) * 16 * (1 - tail) + 128 * tail
        return wts.at[
            0,
            m,
            pl.ds(pl.multiple_of(row, 16), 16),
            pl.ds(pl.multiple_of((cx * Y + y) * DC, 128), DC),
        ]

    def send_weights(step, carry):
        col = (me_col + step) % 32
        for part in range(2):
            remote(
                weight_piece(col, part), wr.at[me_col, pl.ds(part * 16, 16), :], ws_sem, wr_sem, (y * 2 + zh, col)
            ).start()
        return carry

    def columns(ref, px, py):
        return ref.at[:, :, pl.ds(pl.multiple_of((px * Y + py) * DC, 128), DC)]

    def x_copy(step):
        px, py = plane_peer(x, y, step)
        return remote(
            columns(tok, px, py), xv.at[x, :, y], xs_sem.at[step], xr_sem.at[step], device(px, py, z, k)
        )

    def q_copy(step):
        px, py = plane_peer(x, y, step)
        return remote(
            columns(cot, px, py), qv.at[x, :, y], qs_sem.at[step], qr_sem.at[step], device(px, py, z, k)
        )

    for step in range(5):
        x_copy(step).start()
    lax.fori_loop(1, 32, send_weights, 0)
    for part in range(2):
        pltpu.make_async_copy(
            weight_piece(me_col, part), wr.at[me_col, pl.ds(part * 16, 16), :], wr_sem
        ).start()
    for step in range(5, GROUP - 1):
        x_copy(step).start()
    own_x = pltpu.make_async_copy(columns(tok, x, y), xv.at[x, :, y], own_sem.at[0])
    own_q = pltpu.make_async_copy(columns(cot, x, y), qv.at[x, :, y], own_sem.at[1])
    own_x.start()
    own_q.start()

    firsts, lasts = [], []
    for e in range(EXPERTS):
        firsts.append(lasts[-1] if e else 0)
        lasts.append(firsts[-1] + counts[e])

    def place_experts():
        def one(g, carry):
            col = ((g // SLOT) * 4 + zl) * 2 + k
            replica = dest[col, g % SLOT]
            expert = 0
            for e in range(EXPERTS - 1):
                expert += (lasts[e] <= replica).astype(jnp.int32)
            gexp[g] = jnp.where(g % SLOT < live[col], expert, EXPERTS)
            return carry

        lax.fori_loop(0, NGRAN, one, 0)

    wait_bytes(wr, wr_sem)
    for e in range(EXPERTS):
        sel[e] = wr[column[firsts[e]]]

    def chunk(pz):
        return wg.at[:, pl.ds(pl.multiple_of((pz * 2 + k) * 32, 32), 32), :]

    mine = chunk(z)
    own_w = pltpu.make_async_copy(sel, mine, own_sem.at[2])
    own_w.start()
    rights = [remote(sel, mine, rs_sem.at[0], rr_sem.at[0], right)]
    lefts = [remote(sel, mine, ls_sem.at[0], lr_sem.at[0], left)]
    sibs = [remote(sel, mine, ss_sem.at[0], sr_sem.at[0], sibling)]
    rights[0].start()
    lefts[0].start()
    sibs[0].start()
    for step in range(GROUP - 1):
        q_copy(step).start()
    place_experts()
    for t in range(1, 5):
        rights[t - 1].wait_recv()
        piece = chunk((z + Z - t) % Z)
        if t < 4:
            go = remote(piece, piece, rs_sem.at[t], rr_sem.at[t], right)
            go.start()
            rights.append(go)
        go = remote(piece, piece, ss_sem.at[2 * t - 1], sr_sem.at[2 * t - 1], sibling)
        go.start()
        sibs.append(go)
        if t < 4:
            lefts[t - 1].wait_recv()
            piece = chunk((z + t) % Z)
            if t < 3:
                go = remote(piece, piece, ls_sem.at[t], lr_sem.at[t], left)
                go.start()
                lefts.append(go)
            go = remote(piece, piece, ss_sem.at[2 * t], sr_sem.at[2 * t], sibling)
            go.start()
            sibs.append(go)
    for go in sibs:
        go.wait_recv()
    own_w.wait()

    for step in range(GROUP - 1):
        x_copy(step).wait_recv()
    own_x.wait()
    keep_x = pltpu.make_async_copy(xv, xg, keep_sem.at[0])
    keep_x.start()

    a_here, b_here = x * (1 - k) + y * k, x * k + y * (1 - k)

    def place(a, b):
        return a * (1 - k) + b * k, a * k + b * (1 - k)

    def plane_device(a, b):
        px, py = place(a, b)
        return device(px, py, z, k)

    lane = lax.broadcasted_iota(jnp.int32, (ROWS, MAIN), 1)
    place_in_side = lane % SIDE

    def ahead(h):
        return 1 if h % 2 == 0 else 3

    def a_device(step):
        return plane_device((a_here + step) % 4, b_here)

    def b_device(step):
        return plane_device(a_here, (b_here + step) % 4)

    def first_copy(h, kind, src, dst, step):
        at = h * 3 + kind
        return remote(src, dst, p1s_sem.at[at], p1r_sem.at[at], a_device(step))

    def far_copy(h):
        return first_copy(h, 0, n1.at[h, 0], rn.at[h, 0], ahead(h))

    def sum_copy(h):
        return first_copy(h, 1, m1.at[h], r1.at[h], ahead(h))

    def near_copy(h):
        return first_copy(h, 2, n1.at[h, 1], rn.at[h, 1], 4 - ahead(h))

    def second_copy(h, j):
        b = (b_here + j) % 4
        at = h * 3 + j - 1
        return remote(s2.at[b, h], r2.at[b_here, h], p2s_sem.at[at], p2r_sem.at[at], plane_device(a_here, b))

    def hidden_place(a, b, h):
        px, py = place(a, b)
        return hg.at[px, py, h]

    def hidden_first(h, j):
        at = h * 3 + j - 1
        return remote(
            hid.at[h], hidden_place(a_here, b_here, h), has_sem.at[at], har_sem.at[at], a_device(j)
        )

    def hidden_near(h, j, step):
        at = (h * 4 + j) * 3 + (0 if step == 1 else 1)
        here = hidden_place((a_here + 4 - j) % 4, b_here, h)
        return remote(hid.at[h] if j == 0 else here, here, hbs_sem.at[at], hbr_sem.at[at], b_device(step))

    def hidden_far(h, j):
        at = (h * 4 + j) * 3 + 2
        here = hidden_place((a_here + 4 - j) % 4, (b_here + 4 - ahead(h)) % 4, h)
        return remote(here, here, hbs_sem.at[at], hbr_sem.at[at], b_device(ahead(h)))

    def hidden_keep(h):
        return pltpu.make_async_copy(hid.at[h], hidden_place(a_here, b_here, h), keep_sem.at[2 + h])

    def put_rows(px, h, block, value):
        for py in range(Y):
            pa, pb = px * (1 - k) + py * k, px * k + py * (1 - k)
            p1[pa, h, pb, block] = value[py * ROWS : (py + 1) * ROWS].astype(SUM_TYPE)

    lanes = lax.broadcasted_iota(jnp.int32, (GRAN, MAIN), 1)

    def side_by_side(tails):
        return jnp.where(lanes < SIDE, tails[0], pltpu.roll(tails[1], SIDE, 1))

    def project_x(i, carry):
        px, h, pair = i // (CHUNKS * PAIRS), (i // PAIRS) % CHUNKS, i % PAIRS
        tails = []
        for side in range(2):
            at = pair + side * PAIRS
            s = h * PART + at
            e = jnp.minimum(gexp[px * SLOT + s], EXPERTS - 1)
            xt = xv[px, s].reshape(GRAN, DC)
            main = dot_nt(xt, wg[e, 0 : 2 * MAIN])
            put_rows(px, h, 3 * at, main[:, :MAIN])
            put_rows(px, h, 3 * at + 1, main[:, MAIN:])
            tails.append(dot_nt(xt, wg[e, 3 * MAIN : LANES]))
        put_rows(px, h, 3 * PART + pair, side_by_side(tails))
        return carry

    lax.fori_loop(0, X * CHUNKS * PAIRS, project_x, 0)
    for step in range(GROUP - 1):
        q_copy(step).wait_recv()
    own_q.wait()
    keep_q = pltpu.make_async_copy(qv, qg, keep_sem.at[1])
    keep_q.start()
    for h in range(CHUNKS):

        def project_q(i, carry):
            px, pair = i // PAIRS, i % PAIRS
            tails = []
            for side in range(2):
                at = pair + side * PAIRS
                s = h * PART + at
                e = jnp.minimum(gexp[px * SLOT + s], EXPERTS - 1)
                rows = dot_nt(qv[px, s].reshape(GRAN, DC), wg[e, 2 * MAIN : LANES])
                put_rows(px, h, 3 * at + 2, rows[:, :MAIN])
                tails.append(rows[:, MAIN:])
            tail = side_by_side(tails).astype(SUM_TYPE)
            for py in range(Y):
                pa, pb = px * (1 - k) + py * k, px * k + py * (1 - k)
                at = (pa, h, pb, 3 * PART + pair)
                p1[at] = jnp.where(place_in_side < 2 * TAIL, p1[at], tail[py * ROWS : (py + 1) * ROWS])
            return carry

        lax.fori_loop(0, X * PAIRS, project_q, 0)

        def narrow(b, carry):
            n1[h, 0, b] = p1[(a_here + 2) % 4, h, b].astype(jnp.bfloat16)
            n1[h, 1, b] = p1[(a_here + 4 - ahead(h)) % 4, h, b].astype(jnp.bfloat16)
            return carry

        lax.fori_loop(0, 4, narrow, 0)
        far_copy(h).start()
        near_copy(h).start()

    for h in range(CHUNKS):
        far_copy(h).wait_recv()

        def relay(b, carry):
            m1[h, b] = p1[(a_here + ahead(h)) % 4, h, b] + rn[h, 0, b].astype(jnp.float32)
            return carry

        lax.fori_loop(0, 4, relay, 0)
        sum_copy(h).start()

    for h in range(CHUNKS):
        near_copy(h).wait_recv()
        sum_copy(h).wait_recv()

        def sum_first(b, carry):
            s2[b, h] = p1[a_here, h, b] + r1[h, b] + rn[h, 1, b].astype(jnp.float32)
            return carry

        lax.fori_loop(0, 4, sum_first, 0)
        for j in (2, 1, 3):
            second_copy(h, j).start()

    def shift(v, amount):
        return pltpu.roll(v, amount % MAIN, 1)

    for h in range(CHUNKS):
        for j in (1, 2, 3):
            second_copy(h, j).wait_recv()

        def total(block):
            value = s2[b_here, h, block]
            for j in (1, 2, 3):
                value += r2[(b_here + j) % 4, h, block]
            return value

        for at in range(PART):
            for m, value in enumerate(swiglu_rows(total(3 * at), total(3 * at + 1), total(3 * at + 2))):
                hid[h, 3 * at + m] = value.astype(jnp.bfloat16)
        for pair in range(PAIRS):
            tail = total(3 * PART + pair)
            first, second, third = swiglu_rows(tail, shift(tail, -TAIL), shift(tail, -2 * TAIL))
            packed = jnp.where(
                place_in_side < TAIL,
                first,
                jnp.where(place_in_side < 2 * TAIL, shift(second, TAIL), shift(third, 2 * TAIL)),
            )
            hid[h, 3 * PART + pair] = jnp.where(place_in_side < 3 * TAIL, packed, 0.0).astype(jnp.bfloat16)
        for j in (2, 1, 3):
            hidden_first(h, j).start()
        for step in (1, 3):
            hidden_near(h, 0, step).start()
        hidden_keep(h).start()

    arrivals = (0, 1, 3, 2)
    for n, j in enumerate(arrivals):
        if n + 1 < len(arrivals):
            for h in range(CHUNKS):
                hidden_first(h, arrivals[n + 1]).wait_recv()
                for step in (1, 3):
                    hidden_near(h, arrivals[n + 1], step).start()
        for h in range(CHUNKS):
            hidden_near(h, j, ahead(h)).wait_recv()
            hidden_far(h, j).start()
    for h in range(CHUNKS):
        for j in range(4):
            hidden_near(h, j, 4 - ahead(h)).wait_recv()
            hidden_far(h, j).wait_recv()
    for h in range(CHUNKS):
        for j in range(4):
            for step in (1, 3):
                hidden_near(h, j, step).wait_send()
            hidden_far(h, j).wait_send()
        for j in (1, 2, 3):
            hidden_first(h, j).wait_send()
            second_copy(h, j).wait_send()
        far_copy(h).wait_send()
        near_copy(h).wait_send()
        sum_copy(h).wait_send()
        hidden_keep(h).wait()
    for step in range(GROUP - 1):
        x_copy(step).wait_send()
        q_copy(step).wait_send()
    for go in rights + lefts + sibs:
        go.wait_send()
    wait_bytes(wr.at[pl.ds(0, 31)], ws_sem)
    keep_x.wait()
    keep_q.wait()


def rows_and_hidden(counts, column, dest, live, tok, cot, wts):
    hbm = pl.BlockSpec(memory_space=pl.ANY)
    smem = pl.BlockSpec(memory_space=pltpu.SMEM)
    dma = pltpu.SemaphoreType.DMA
    spread = pltpu.VMEM((X, SLOT, Y, ROWS, DC), jnp.bfloat16)
    sums = pltpu.VMEM((4, CHUNKS, 4, BLOCKS, ROWS, MAIN), SUM_TYPE)
    relayed = pltpu.VMEM((CHUNKS, 4, BLOCKS, ROWS, MAIN), SUM_TYPE)
    narrow = pltpu.VMEM((CHUNKS, 2, 4, BLOCKS, ROWS, MAIN), jnp.bfloat16)
    halfway = pltpu.VMEM((4, CHUNKS, BLOCKS, ROWS, MAIN), jnp.float32)
    return pl.pallas_call(
        rows_kernel,
        out_shape=(
            jax.ShapeDtypeStruct((X, SLOT, Y, ROWS, DC), jnp.bfloat16),
            jax.ShapeDtypeStruct((X, SLOT, Y, ROWS, DC), jnp.bfloat16),
            jax.ShapeDtypeStruct((X, Y, CHUNKS, BLOCKS, ROWS, MAIN), jnp.bfloat16),
            jax.ShapeDtypeStruct((NGRAN,), jnp.int32),
        ),
        in_specs=[smem, smem, smem, smem, hbm, hbm, hbm],
        out_specs=(hbm, hbm, pl.BlockSpec(memory_space=pltpu.VMEM), smem),
        scratch_shapes=[
            pltpu.VMEM((32, 32, DC), jnp.bfloat16),
            pltpu.VMEM((EXPERTS, 32, DC), jnp.bfloat16),
            pltpu.VMEM((EXPERTS, LANES, DC), jnp.bfloat16),
            spread,
            spread,
            sums,
            relayed,
            relayed,
            narrow,
            narrow,
            halfway,
            halfway,
            pltpu.VMEM((CHUNKS, BLOCKS, ROWS, MAIN), jnp.bfloat16),
            dma((GROUP,)),
            dma((GROUP,)),
            dma((GROUP,)),
            dma((GROUP,)),
            dma,
            dma,
            dma((3,)),
            dma((4,)),
            dma((4,)),
            dma((3,)),
            dma((3,)),
            dma((8,)),
            dma((8,)),
            dma((3 * CHUNKS,)),
            dma((3 * CHUNKS,)),
            dma((3 * CHUNKS,)),
            dma((3 * CHUNKS,)),
            dma((3 * CHUNKS,)),
            dma((3 * CHUNKS,)),
            dma((12 * CHUNKS,)),
            dma((12 * CHUNKS,)),
            dma((2 + CHUNKS,)),
        ],
        compiler_params=pltpu.CompilerParams(
            collective_id=0, has_side_effects=True, vmem_limit_bytes=VMEM_LIMIT
        ),
        name="rows_and_hidden",
    )(counts, column, dest, live, tok, cot, wts)


def grads_kernel(gexp, xg, qg, hg, out, xs, qs, hs, acc, rounded, source, rank, ends, in_sem, out_sem):
    loads = [
        pltpu.make_async_copy(ref, held, in_sem.at[i]) for i, (ref, held) in enumerate(((hg, hs), (xg, xs), (qg, qs)))
    ]
    for load in loads:
        load.start()

    def clear(at, carry):
        source[at] = -1
        return carry

    def count(g, carry):
        e = gexp[g]
        rank[g] = ends[e]
        ends[e] = ends[e] + 1
        return carry

    lax.fori_loop(0, MAX_TILES * PER_TILE, clear, 0)
    for e in range(EXPERTS + 1):
        ends[e] = 0
    lax.fori_loop(0, NGRAN, count, 0)
    end = 0
    for e in range(EXPERTS):
        end += (ends[e] + PER_TILE - 1) // PER_TILE
        ends[e] = end

    def fill(g, carry):
        e = gexp[g]

        @pl.when(e < EXPERTS)
        def _():
            start = jnp.where(e > 0, ends[jnp.maximum(e - 1, 0)], 0)
            source[start * PER_TILE + rank[g]] = g

        return carry

    lax.fori_loop(0, NGRAN, fill, 0)
    acc[...] = jnp.zeros_like(acc)
    for load in loads:
        load.wait()
    tail_rows = lax.broadcasted_iota(jnp.int32, (MAIN, DC), 0) % SIDE < 2 * TAIL
    side = lax.broadcasted_iota(jnp.int32, (ROWS, MAIN), 1) // SIDE

    def expert_step(e, start):
        def tile_step(t, carry):
            xt, qt, mains, tails = [], [], ([], [], []), []
            for j in range(PER_TILE):
                found = source[t * PER_TILE + j]
                g = jnp.maximum(found, 0)
                px, h, at = g // SLOT, (g % SLOT) // PART, g % PART
                xt.append(xs[g])
                qt.append(qs[g])
                for py in range(Y):
                    for m in range(3):
                        block = hs[px, py, h, 3 * at + m]
                        mains[m].append(jnp.where(found >= 0, block, jnp.zeros_like(block)))
                    block = hs[px, py, h, 3 * PART + at % PAIRS].astype(jnp.float32)
                    mine = side == jnp.where(found >= 0, at // PAIRS, 2)
                    tails.append(jnp.where(mine, block, 0.0).astype(jnp.bfloat16))
            xt, qt = jnp.concatenate(xt, axis=0), jnp.concatenate(qt, axis=0)
            for m, rows in ((0, xt), (1, xt), (2, qt)):
                acc[e, m * MAIN : (m + 1) * MAIN] += dot_tn(jnp.concatenate(mains[m], axis=0), rows)
            tail = jnp.concatenate(tails, axis=0)
            both = jnp.where(tail_rows, dot_tn(tail, xt), dot_tn(tail, qt))
            acc[e, 3 * MAIN : GROWS] += both[:SIDE] + both[SIDE:]
            return carry

        end = ends[e]
        lax.fori_loop(start, end, tile_step, 0)
        rounded[e] = acc[e].astype(jnp.bfloat16)
        pltpu.make_async_copy(rounded.at[e], out.at[e], out_sem.at[e]).start()
        return end

    lax.fori_loop(0, EXPERTS, expert_step, 0)

    def finish(e, carry):
        pltpu.make_async_copy(rounded.at[e], out.at[e], out_sem.at[e]).wait()
        return carry

    lax.fori_loop(0, EXPERTS, finish, 0)


def gradients(gexp, xg, qg, hg):
    hbm = pl.BlockSpec(memory_space=pl.ANY)
    return pl.pallas_call(
        grads_kernel,
        out_shape=jax.ShapeDtypeStruct((EXPERTS, GROWS, DC), jnp.bfloat16),
        in_specs=[pl.BlockSpec(memory_space=pltpu.SMEM), hbm, hbm, hbm],
        out_specs=hbm,
        scratch_shapes=[
            pltpu.VMEM(xg.shape, jnp.bfloat16),
            pltpu.VMEM(qg.shape, jnp.bfloat16),
            pltpu.VMEM(hg.shape, jnp.bfloat16),
            pltpu.VMEM((EXPERTS, GROWS, DC), jnp.float32),
            pltpu.VMEM((EXPERTS, GROWS, DC), jnp.bfloat16),
            pltpu.SMEM((MAX_TILES * PER_TILE,), jnp.int32),
            pltpu.SMEM((NGRAN,), jnp.int32),
            pltpu.SMEM((EXPERTS + 1,), jnp.int32),
            pltpu.SemaphoreType.DMA((3,)),
            pltpu.SemaphoreType.DMA((EXPERTS,)),
        ],
        compiler_params=pltpu.CompilerParams(vmem_limit_bytes=VMEM_LIMIT),
        name="gradients",
    )(gexp, xg, qg, hg)


QUART = HALF // 2
PACK = 96
SHARE = 54
WINDOW = 256
OFFSETS = (4, 3, -3, 2, -2, 1, -1, 0)


def reduce_kernel(
    grads, out, own, sib, sbuf, rbuf, fin, win, wide, packf, pack, got, gotf, os_sem, ts_sem, tr_sem, cs_sem, cr_sem, swap_sem, send, recv,
    keep_sem,
):
    x, y, z, k = coords()
    zh, zl = z // 4, z % 4
    sibling = device(x, y, z, 1 - k)
    barrier = pltpu.get_barrier_semaphore()

    def target(share):
        return share // 2, (share % 2) * 4 + y

    def greet_share(share, carry):
        ty, tz = target(share)

        @pl.when((ty != y) | (tz != z))
        def _():
            signal(barrier, device(x, ty, tz, k))

        return carry

    def greet_source(pz, carry):
        @pl.when((zl != y) | (pz != z))
        def _():
            signal(barrier, device(x, zl, pz, k))

        return carry

    ahead = (device(x, y, (z + 1) % Z, k), device(x, y, (z + Z - 1) % Z, k))
    signal(barrier, sibling)
    signal(barrier, ahead[0])
    signal(barrier, ahead[1])
    lax.fori_loop(0, 8, greet_share, 0)
    lax.fori_loop(0, 8, greet_source, 0)
    self_here = jnp.where(zl == y, 1, 0)
    pl.semaphore_wait(barrier, 19 - 2 * self_here)

    def half(e, which):
        return grads.at[e, pl.ds(pl.multiple_of(which * HALF, HALF), HALF), :]

    trades, keeps = {}, {}
    for i, off in enumerate(OFFSETS):
        e = (z + off + Z) % Z
        trades[off] = remote(half(e, 1 - k), sib.at[e], ts_sem.at[i], tr_sem.at[i], sibling)
        keeps[off] = pltpu.make_async_copy(half(e, k), own.at[e], os_sem.at[i])
        trades[off].start()
        keeps[off].start()
    trades[-4], keeps[-4] = trades[4], keeps[4]
    ready = set()

    def ours(off, j):
        if abs(off) % 8 == 4:
            off = 4
        if off not in ready:
            trades[off].wait_recv()
            keeps[off].wait()
            ready.add(off)
        e = (z + off + Z) % Z
        cut = slice(j * QUART, (j + 1) * QUART)
        return own[e, cut].astype(jnp.float32) + sib[e, cut].astype(jnp.float32)

    chain = {}
    for dist in (4, 3, 2, 1):
        for way in range(2):
            for j in range(2):
                longest = 4 if way == j else 3
                if dist > longest:
                    continue
                value = ours(dist if way == 0 else -dist, j)
                if dist < longest:
                    chain[way, j, dist + 1].wait_recv()
                    value += rbuf[way, j, dist].astype(jnp.float32)
                sbuf[way, j, dist - 1] = value.astype(jnp.bfloat16)
                at = (way * 2 + j) * 4 + dist - 1
                go = remote(
                    sbuf.at[way, j, dist - 1], rbuf.at[way, j, dist - 1], cs_sem.at[at], cr_sem.at[at], ahead[way]
                )
                go.start()
                chain[way, j, dist] = go
    for j in range(2):
        value = ours(0, j)
        for way in range(2):
            chain[way, j, 1].wait_recv()
            value += rbuf[way, j, 0].astype(jnp.float32)
        fin[pl.ds(pl.multiple_of(k * HALF + j * QUART, 16), QUART)] = value
    mine = fin.at[pl.ds(pl.multiple_of(k * HALF, HALF), HALF)]
    swap = remote(mine, mine, swap_sem.at[0], swap_sem.at[1], sibling)
    swap.start()
    swap.wait()

    low = fin[:, 0:WINDOW]
    high = pltpu.roll(fin[:, DC - WINDOW : DC], DC // 2, 1)
    win[...] = jnp.where(k == 0, low, high)
    first_half = lax.broadcasted_iota(jnp.int32, (SHARE // 2, MAIN), 1) < SIDE
    for share in range(8):
        for m in range(3):
            if share < 7:
                lo = m * MAIN + 18 * share
                wide[share, 18 * m : 18 * m + 18] = win[lo : lo + 18]
            else:
                lo = m * MAIN + 126
                wide[share, 18 * m : 18 * m + 2] = win[lo : lo + 2]
                lo = 3 * MAIN + m * TAIL
                wide[share, 18 * m + 2 : 18 * m + 18] = win[lo : lo + TAIL]
        packf[share, 80:PACK] = jnp.zeros((PACK - 80, MAIN), jnp.float32)
        packf[share, 0:SHARE] = wide[share, 0:SHARE, :MAIN]
        packf[share, SHARE : SHARE + SHARE // 2] = jnp.where(
            first_half,
            wide[share, 0 : SHARE // 2, MAIN:],
            pltpu.roll(wide[share, SHARE // 2 : SHARE, MAIN:], SIDE, 1),
        )
        pack[share] = packf[share].astype(jnp.bfloat16)

    def share_copy(share):
        ty, tz = target(share)
        return remote(pack.at[share], got.at[z], send.at[share], recv.at[z], device(x, ty, tz, k))

    def start(share, carry):
        ty, tz = target(share)

        @pl.when((ty != y) | (tz != z))
        def _():
            share_copy(share).start()

        @pl.when((ty == y) & (tz == z))
        def _():
            pltpu.make_async_copy(pack.at[share], got.at[z], keep_sem).start()

        return carry

    def finish_send(share, carry):
        ty, tz = target(share)

        @pl.when((ty != y) | (tz != z))
        def _():
            share_copy(share).wait_send()

        @pl.when((ty == y) & (tz == z))
        def _():
            pltpu.make_async_copy(pack.at[share], got.at[z], keep_sem).wait()

        return carry

    def finish_recv(pz, carry):
        @pl.when((zl != y) | (pz != z))
        def _():
            pltpu.make_async_copy(got.at[pz], got.at[pz], recv.at[pz]).wait()

        return carry

    lax.fori_loop(0, 8, start, 0)
    lax.fori_loop(0, 8, finish_send, 0)
    def unpack(e, carry):
        value = got[e].astype(jnp.float32)
        gotf[0:PACK, :MAIN] = value
        gotf[0 : SHARE // 2, MAIN:] = gotf[SHARE : SHARE + SHARE // 2, :MAIN]
        gotf[SHARE // 2 : SHARE, MAIN:] = pltpu.roll(gotf[SHARE : SHARE + SHARE // 2, :MAIN], SIDE, 1)
        for m in range(3):
            out[e, m] = gotf[18 * m : 18 * m + 18, : DC // 2].astype(jnp.bfloat16)
        return carry

    lax.fori_loop(0, 8, finish_recv, 0)
    lax.fori_loop(0, 8, unpack, 0)
    for off in OFFSETS:
        trades[off].wait_send()
    for go in chain.values():
        go.wait_send()


def reduce_grads(grads):
    dma = pltpu.SemaphoreType.DMA
    wide = pltpu.VMEM((EXPERTS, HALF, DC), jnp.bfloat16)
    steps = pltpu.VMEM((2, 2, 4, QUART, DC), jnp.bfloat16)
    return pl.pallas_call(
        reduce_kernel,
        out_shape=jax.ShapeDtypeStruct((EXPERTS, 3, 18, DC // 2), jnp.bfloat16),
        in_specs=[pl.BlockSpec(memory_space=pl.ANY)],
        out_specs=pl.BlockSpec(memory_space=pltpu.VMEM),
        scratch_shapes=[
            wide,
            wide,
            steps,
            steps,
            pltpu.VMEM((GROWS, DC), jnp.float32),
            pltpu.VMEM((GROWS, WINDOW), jnp.float32),
            pltpu.VMEM((8, SHARE + 2, WINDOW), jnp.float32),
            pltpu.VMEM((8, PACK, MAIN), jnp.float32),
            pltpu.VMEM((8, PACK, MAIN), jnp.bfloat16),
            pltpu.VMEM((8, PACK, MAIN), jnp.bfloat16),
            pltpu.VMEM((PACK, WINDOW), jnp.float32),
            dma((8,)),
            dma((8,)),
            dma((8,)),
            dma((16,)),
            dma((16,)),
            dma((2,)),
            dma((8,)),
            dma((8,)),
            dma,
        ],
        compiler_params=pltpu.CompilerParams(
            collective_id=1, has_side_effects=True, vmem_limit_bytes=VMEM_LIMIT
        ),
        name="reduce_grads",
    )(grads)


def on_device(tok, cot, wts, counts, column, dest, live):
    xg, qg, hg, gexp = rows_and_hidden(counts, column, dest, live, tok, cot, wts)
    xg = xg.reshape(NGRAN, GRAN, DC)
    qg = qg.reshape(NGRAN, GRAN, DC)
    return reduce_grads(gradients(gexp, xg, qg, hg))


def solution(mesh):
    placed = (
        P("expert", "dp", None),
        P("expert", "dp", None),
        P("expert", None, None, None),
        P(),
        P(),
        P(),
        P(),
    )
    return jax.shard_map(
        on_device,
        mesh=mesh,
        in_specs=placed,
        out_specs=P(None, None, "dp", "expert"),
        check_vma=False,
    )
```

```python
import jax
import jax.numpy as jnp
from jax import lax
from jax.experimental import pallas as pl
from jax.experimental.pallas import tpu as pltpu
from jax.sharding import PartitionSpec as P

MESH = pl.DeviceIdType.MESH
EXPERTS = 8
X, Y, Z = 4, 4, 8
GROUP = X * Y
D = 6144
DC = D // GROUP
SLOT = 8
ROWS = 16
MAIN = 128
TAIL = 16
LANES = 512
GROWS = 448
HALF = GROWS // 2
GRAN = Y * ROWS
NGRAN = X * SLOT
TILE = 256
PER_TILE = TILE // GRAN
MAX_TILES = NGRAN // PER_TILE + EXPERTS - 1
VMEM_LIMIT = 56 * 1024 * 1024


def coords():
    d = lax.axis_index("dp")
    c = lax.axis_index("expert")
    return c // 8, d // 2, (d % 2) * 4 + (c // 2) % 4, c % 2


def device(x, y, z, k):
    return (y * 2 + z // 4, (x * 4 + z % 4) * 2 + k)


MOVES = (
    (1, 0), (0, 1), (3, 0), (0, 3), (2, 0), (0, 2), (1, 1), (3, 3), (1, 3), (3, 1), (2, 1), (1, 2), (2, 3), (3, 2), (2, 2),
)


def plane_peer(x, y, step):
    dx, dy = MOVES[step]
    return (x + dx) % X, (y + dy) % Y


def signal(sem, target):
    pl.semaphore_signal(sem, inc=1, device_id=target, device_id_type=MESH)


def remote(src, dst, send, recv, target):
    return pltpu.make_async_remote_copy(
        src_ref=src, dst_ref=dst, send_sem=send, recv_sem=recv, device_id=target, device_id_type=MESH
    )


def wait_bytes(ref, sem):
    pltpu.make_async_copy(ref, ref, sem).wait()


def swiglu_rows(gate, up, grad):
    sig = jax.nn.sigmoid(gate)
    act = gate * sig
    return grad * up * sig * (1.0 + gate * (1.0 - sig)), grad * act, act * up


def dot_nt(a, b):
    return lax.dot_general(a, b, (((1,), (1,)), ((), ())), preferred_element_type=jnp.float32)


def dot_tn(a, b):
    return lax.dot_general(a, b, (((0,), (0,)), ((), ())), preferred_element_type=jnp.float32)


CHUNKS = 4
PART = SLOT // CHUNKS
PAIRS = PART // 2
BLOCKS = 3 * PART + PAIRS
SIDE = 64
SUM_TYPE = jnp.float32


def rows_kernel(
    counts, column, dest, live, tok, cot, wts, xg, qg, hg, gexp, wr, sel, wg, xv, qv, p1, m1, r1, n1, rn, s2, r2, hid, xs_sem, xr_sem, qs_sem, qr_sem,
    ws_sem, wr_sem, own_sem, rs_sem, rr_sem, ls_sem, lr_sem, ss_sem, sr_sem, p1s_sem, p1r_sem, p2s_sem, p2r_sem,
    has_sem, har_sem, hbs_sem, hbr_sem, keep_sem,
):
    x, y, z, k = coords()
    zh, zl = z // 4, z % 4
    me_col = (x * 4 + zl) * 2 + k
    barrier = pltpu.get_barrier_semaphore()

    def greet_column(step, carry):
        signal(barrier, (y * 2 + zh, (me_col + step) % 32))
        return carry

    for step in range(GROUP - 1):
        px, py = plane_peer(x, y, step)
        signal(barrier, device(px, py, z, k))
    lax.fori_loop(1, 32, greet_column, 0)
    right, left = device(x, y, (z + 1) % Z, k), device(x, y, (z + Z - 1) % Z, k)
    sibling = device(x, y, z, 1 - k)
    signal(barrier, right)
    signal(barrier, left)
    pl.semaphore_wait(barrier, GROUP - 1 + 31 + 2)

    def weight_piece(col, part):
        cx, cz, ck = col // 8, zh * 4 + (col // 2) % 4, col % 2
        t = jnp.minimum((cz * 2 + ck) * 2 + part, 26)
        tail = t // 24
        m = (t // 8) * (1 - tail) + (t - 24) * tail
        row = (t % 8) * 16 * (1 - tail) + 128 * tail
        return wts.at[
            0,
            m,
            pl.ds(pl.multiple_of(row, 16), 16),
            pl.ds(pl.multiple_of((cx * Y + y) * DC, 128), DC),
        ]

    def send_weights(step, carry):
        col = (me_col + step) % 32
        for part in range(2):
            remote(
                weight_piece(col, part), wr.at[me_col, pl.ds(part * 16, 16), :], ws_sem, wr_sem, (y * 2 + zh, col)
            ).start()
        return carry

    def columns(ref, px, py):
        return ref.at[:, :, pl.ds(pl.multiple_of((px * Y + py) * DC, 128), DC)]

    def x_copy(step):
        px, py = plane_peer(x, y, step)
        return remote(
            columns(tok, px, py), xv.at[x, :, y], xs_sem.at[step], xr_sem.at[step], device(px, py, z, k)
        )

    def q_copy(step):
        px, py = plane_peer(x, y, step)
        return remote(
            columns(cot, px, py), qv.at[x, :, y], qs_sem.at[step], qr_sem.at[step], device(px, py, z, k)
        )

    for step in range(5):
        x_copy(step).start()
    lax.fori_loop(1, 32, send_weights, 0)
    for part in range(2):
        pltpu.make_async_copy(
            weight_piece(me_col, part), wr.at[me_col, pl.ds(part * 16, 16), :], wr_sem
        ).start()
    for step in range(5, GROUP - 1):
        x_copy(step).start()
    own_x = pltpu.make_async_copy(columns(tok, x, y), xv.at[x, :, y], own_sem.at[0])
    own_q = pltpu.make_async_copy(columns(cot, x, y), qv.at[x, :, y], own_sem.at[1])
    own_x.start()
    own_q.start()

    firsts, lasts = [], []
    for e in range(EXPERTS):
        firsts.append(lasts[-1] if e else 0)
        lasts.append(firsts[-1] + counts[e])

    def place_experts():
        def one(g, carry):
            col = ((g // SLOT) * 4 + zl) * 2 + k
            replica = dest[col, g % SLOT]
            expert = 0
            for e in range(EXPERTS - 1):
                expert += (lasts[e] <= replica).astype(jnp.int32)
            gexp[g] = jnp.where(g % SLOT < live[col], expert, EXPERTS)
            return carry

        lax.fori_loop(0, NGRAN, one, 0)

    wait_bytes(wr, wr_sem)
    for e in range(EXPERTS):
        sel[e] = wr[column[firsts[e]]]

    def chunk(pz):
        return wg.at[:, pl.ds(pl.multiple_of((pz * 2 + k) * 32, 32), 32), :]

    mine = chunk(z)
    own_w = pltpu.make_async_copy(sel, mine, own_sem.at[2])
    own_w.start()
    rights = [remote(sel, mine, rs_sem.at[0], rr_sem.at[0], right)]
    lefts = [remote(sel, mine, ls_sem.at[0], lr_sem.at[0], left)]
    sibs = [remote(sel, mine, ss_sem.at[0], sr_sem.at[0], sibling)]
    rights[0].start()
    lefts[0].start()
    sibs[0].start()
    for step in range(GROUP - 1):
        q_copy(step).start()
    place_experts()
    for t in range(1, 5):
        rights[t - 1].wait_recv()
        piece = chunk((z + Z - t) % Z)
        if t < 4:
            go = remote(piece, piece, rs_sem.at[t], rr_sem.at[t], right)
            go.start()
            rights.append(go)
        go = remote(piece, piece, ss_sem.at[2 * t - 1], sr_sem.at[2 * t - 1], sibling)
        go.start()
        sibs.append(go)
        if t < 4:
            lefts[t - 1].wait_recv()
            piece = chunk((z + t) % Z)
            if t < 3:
                go = remote(piece, piece, ls_sem.at[t], lr_sem.at[t], left)
                go.start()
                lefts.append(go)
            go = remote(piece, piece, ss_sem.at[2 * t], sr_sem.at[2 * t], sibling)
            go.start()
            sibs.append(go)
    for go in sibs:
        go.wait_recv()
    own_w.wait()

    for step in range(GROUP - 1):
        x_copy(step).wait_recv()
    own_x.wait()
    keep_x = pltpu.make_async_copy(xv, xg, keep_sem.at[0])
    keep_x.start()

    a_here, b_here = x * (1 - k) + y * k, x * k + y * (1 - k)

    def place(a, b):
        return a * (1 - k) + b * k, a * k + b * (1 - k)

    def plane_device(a, b):
        px, py = place(a, b)
        return device(px, py, z, k)

    lane = lax.broadcasted_iota(jnp.int32, (ROWS, MAIN), 1)
    place_in_side = lane % SIDE

    def ahead(h):
        return 1 if h % 2 == 0 else 3

    def a_device(step):
        return plane_device((a_here + step) % 4, b_here)

    def b_device(step):
        return plane_device(a_here, (b_here + step) % 4)

    def first_copy(h, kind, src, dst, step):
        at = h * 3 + kind
        return remote(src, dst, p1s_sem.at[at], p1r_sem.at[at], a_device(step))

    def far_copy(h):
        return first_copy(h, 0, n1.at[h, 0], rn.at[h, 0], ahead(h))

    def sum_copy(h):
        return first_copy(h, 1, m1.at[h], r1.at[h], ahead(h))

    def near_copy(h):
        return first_copy(h, 2, n1.at[h, 1], rn.at[h, 1], 4 - ahead(h))

    def second_copy(h, j):
        b = (b_here + j) % 4
        at = h * 3 + j - 1
        return remote(s2.at[b, h], r2.at[b_here, h], p2s_sem.at[at], p2r_sem.at[at], plane_device(a_here, b))

    def hidden_place(a, b, h):
        px, py = place(a, b)
        return hg.at[px, py, h]

    def hidden_first(h, j):
        at = h * 3 + j - 1
        return remote(
            hid.at[h], hidden_place(a_here, b_here, h), has_sem.at[at], har_sem.at[at], a_device(j)
        )

    def hidden_near(h, j, step):
        at = (h * 4 + j) * 3 + (0 if step == 1 else 1)
        here = hidden_place((a_here + 4 - j) % 4, b_here, h)
        return remote(hid.at[h] if j == 0 else here, here, hbs_sem.at[at], hbr_sem.at[at], b_device(step))

    def hidden_far(h, j):
        at = (h * 4 + j) * 3 + 2
        here = hidden_place((a_here + 4 - j) % 4, (b_here + 4 - ahead(h)) % 4, h)
        return remote(here, here, hbs_sem.at[at], hbr_sem.at[at], b_device(ahead(h)))

    def hidden_keep(h):
        return pltpu.make_async_copy(hid.at[h], hidden_place(a_here, b_here, h), keep_sem.at[2 + h])

    def put_rows(px, h, block, value):
        for py in range(Y):
            pa, pb = px * (1 - k) + py * k, px * k + py * (1 - k)
            p1[pa, h, pb, block] = value[py * ROWS : (py + 1) * ROWS].astype(SUM_TYPE)

    lanes = lax.broadcasted_iota(jnp.int32, (GRAN, MAIN), 1)

    def side_by_side(tails):
        return jnp.where(lanes < SIDE, tails[0], pltpu.roll(tails[1], SIDE, 1))

    def project_x(i, carry):
        px, h, pair = i // (CHUNKS * PAIRS), (i // PAIRS) % CHUNKS, i % PAIRS
        tails = []
        for side in range(2):
            at = pair + side * PAIRS
            s = h * PART + at
            e = jnp.minimum(gexp[px * SLOT + s], EXPERTS - 1)
            xt = xv[px, s].reshape(GRAN, DC)
            main = dot_nt(xt, wg[e, 0 : 2 * MAIN])
            put_rows(px, h, 3 * at, main[:, :MAIN])
            put_rows(px, h, 3 * at + 1, main[:, MAIN:])
            tails.append(dot_nt(xt, wg[e, 3 * MAIN : LANES]))
        put_rows(px, h, 3 * PART + pair, side_by_side(tails))
        return carry

    lax.fori_loop(0, X * CHUNKS * PAIRS, project_x, 0)
    for step in range(GROUP - 1):
        q_copy(step).wait_recv()
    own_q.wait()
    keep_q = pltpu.make_async_copy(qv, qg, keep_sem.at[1])
    keep_q.start()
    for h in range(CHUNKS):

        def project_q(i, carry):
            px, pair = i // PAIRS, i % PAIRS
            tails = []
            for side in range(2):
                at = pair + side * PAIRS
                s = h * PART + at
                e = jnp.minimum(gexp[px * SLOT + s], EXPERTS - 1)
                rows = dot_nt(qv[px, s].reshape(GRAN, DC), wg[e, 2 * MAIN : LANES])
                put_rows(px, h, 3 * at + 2, rows[:, :MAIN])
                tails.append(rows[:, MAIN:])
            tail = side_by_side(tails).astype(SUM_TYPE)
            for py in range(Y):
                pa, pb = px * (1 - k) + py * k, px * k + py * (1 - k)
                at = (pa, h, pb, 3 * PART + pair)
                p1[at] = jnp.where(place_in_side < 2 * TAIL, p1[at], tail[py * ROWS : (py + 1) * ROWS])
            return carry

        lax.fori_loop(0, X * PAIRS, project_q, 0)

        def narrow(b, carry):
            n1[h, 0, b] = p1[(a_here + 2) % 4, h, b].astype(jnp.bfloat16)
            n1[h, 1, b] = p1[(a_here + 4 - ahead(h)) % 4, h, b].astype(jnp.bfloat16)
            return carry

        lax.fori_loop(0, 4, narrow, 0)
        far_copy(h).start()
        near_copy(h).start()

    for h in range(CHUNKS):
        far_copy(h).wait_recv()

        def relay(b, carry):
            m1[h, b] = p1[(a_here + ahead(h)) % 4, h, b] + rn[h, 0, b].astype(jnp.float32)
            return carry

        lax.fori_loop(0, 4, relay, 0)
        sum_copy(h).start()

    for h in range(CHUNKS):
        near_copy(h).wait_recv()
        sum_copy(h).wait_recv()

        def sum_first(b, carry):
            s2[b, h] = p1[a_here, h, b] + r1[h, b] + rn[h, 1, b].astype(jnp.float32)
            return carry

        lax.fori_loop(0, 4, sum_first, 0)
        for j in (2, 1, 3):
            second_copy(h, j).start()

    def shift(v, amount):
        return pltpu.roll(v, amount % MAIN, 1)

    for h in range(CHUNKS):
        for j in (1, 2, 3):
            second_copy(h, j).wait_recv()

        def total(block):
            value = s2[b_here, h, block]
            for j in (1, 2, 3):
                value += r2[(b_here + j) % 4, h, block]
            return value

        for at in range(PART):
            for m, value in enumerate(swiglu_rows(total(3 * at), total(3 * at + 1), total(3 * at + 2))):
                hid[h, 3 * at + m] = value.astype(jnp.bfloat16)
        for pair in range(PAIRS):
            tail = total(3 * PART + pair)
            first, second, third = swiglu_rows(tail, shift(tail, -TAIL), shift(tail, -2 * TAIL))
            packed = jnp.where(
                place_in_side < TAIL,
                first,
                jnp.where(place_in_side < 2 * TAIL, shift(second, TAIL), shift(third, 2 * TAIL)),
            )
            hid[h, 3 * PART + pair] = jnp.where(place_in_side < 3 * TAIL, packed, 0.0).astype(jnp.bfloat16)
        for j in (2, 1, 3):
            hidden_first(h, j).start()
        for step in (1, 3):
            hidden_near(h, 0, step).start()
        hidden_keep(h).start()

    arrivals = (0, 1, 3, 2)
    for n, j in enumerate(arrivals):
        if n + 1 < len(arrivals):
            for h in range(CHUNKS):
                hidden_first(h, arrivals[n + 1]).wait_recv()
                for step in (1, 3):
                    hidden_near(h, arrivals[n + 1], step).start()
        for h in range(CHUNKS):
            hidden_near(h, j, ahead(h)).wait_recv()
            hidden_far(h, j).start()
    for h in range(CHUNKS):
        for j in range(4):
            hidden_near(h, j, 4 - ahead(h)).wait_recv()
            hidden_far(h, j).wait_recv()
    for h in range(CHUNKS):
        for j in range(4):
            for step in (1, 3):
                hidden_near(h, j, step).wait_send()
            hidden_far(h, j).wait_send()
        for j in (1, 2, 3):
            hidden_first(h, j).wait_send()
            second_copy(h, j).wait_send()
        far_copy(h).wait_send()
        near_copy(h).wait_send()
        sum_copy(h).wait_send()
        hidden_keep(h).wait()
    for step in range(GROUP - 1):
        x_copy(step).wait_send()
        q_copy(step).wait_send()
    for go in rights + lefts + sibs:
        go.wait_send()
    wait_bytes(wr.at[pl.ds(0, 31)], ws_sem)
    keep_x.wait()
    keep_q.wait()


def rows_and_hidden(counts, column, dest, live, tok, cot, wts):
    hbm = pl.BlockSpec(memory_space=pl.ANY)
    smem = pl.BlockSpec(memory_space=pltpu.SMEM)
    dma = pltpu.SemaphoreType.DMA
    spread = pltpu.VMEM((X, SLOT, Y, ROWS, DC), jnp.bfloat16)
    sums = pltpu.VMEM((4, CHUNKS, 4, BLOCKS, ROWS, MAIN), SUM_TYPE)
    relayed = pltpu.VMEM((CHUNKS, 4, BLOCKS, ROWS, MAIN), SUM_TYPE)
    narrow = pltpu.VMEM((CHUNKS, 2, 4, BLOCKS, ROWS, MAIN), jnp.bfloat16)
    halfway = pltpu.VMEM((4, CHUNKS, BLOCKS, ROWS, MAIN), jnp.float32)
    return pl.pallas_call(
        rows_kernel,
        out_shape=(
            jax.ShapeDtypeStruct((X, SLOT, Y, ROWS, DC), jnp.bfloat16),
            jax.ShapeDtypeStruct((X, SLOT, Y, ROWS, DC), jnp.bfloat16),
            jax.ShapeDtypeStruct((X, Y, CHUNKS, BLOCKS, ROWS, MAIN), jnp.bfloat16),
            jax.ShapeDtypeStruct((NGRAN,), jnp.int32),
        ),
        in_specs=[smem, smem, smem, smem, hbm, hbm, hbm],
        out_specs=(hbm, hbm, pl.BlockSpec(memory_space=pltpu.VMEM), smem),
        scratch_shapes=[
            pltpu.VMEM((32, 32, DC), jnp.bfloat16),
            pltpu.VMEM((EXPERTS, 32, DC), jnp.bfloat16),
            pltpu.VMEM((EXPERTS, LANES, DC), jnp.bfloat16),
            spread,
            spread,
            sums,
            relayed,
            relayed,
            narrow,
            narrow,
            halfway,
            halfway,
            pltpu.VMEM((CHUNKS, BLOCKS, ROWS, MAIN), jnp.bfloat16),
            dma((GROUP,)),
            dma((GROUP,)),
            dma((GROUP,)),
            dma((GROUP,)),
            dma,
            dma,
            dma((3,)),
            dma((4,)),
            dma((4,)),
            dma((3,)),
            dma((3,)),
            dma((8,)),
            dma((8,)),
            dma((3 * CHUNKS,)),
            dma((3 * CHUNKS,)),
            dma((3 * CHUNKS,)),
            dma((3 * CHUNKS,)),
            dma((3 * CHUNKS,)),
            dma((3 * CHUNKS,)),
            dma((12 * CHUNKS,)),
            dma((12 * CHUNKS,)),
            dma((2 + CHUNKS,)),
        ],
        compiler_params=pltpu.CompilerParams(
            collective_id=0, has_side_effects=True, vmem_limit_bytes=VMEM_LIMIT
        ),
        name="rows_and_hidden",
    )(counts, column, dest, live, tok, cot, wts)


def grads_kernel(gexp, xg, qg, hg, out, xs, qs, hs, acc, source, rank, ends, in_sem, out_sem):
    loads = [
        pltpu.make_async_copy(ref, held, in_sem.at[i]) for i, (ref, held) in enumerate(((hg, hs), (xg, xs), (qg, qs)))
    ]
    for load in loads:
        load.start()

    def clear(at, carry):
        source[at] = -1
        return carry

    def count(g, carry):
        e = gexp[g]
        rank[g] = ends[e]
        ends[e] = ends[e] + 1
        return carry

    lax.fori_loop(0, MAX_TILES * PER_TILE, clear, 0)
    for e in range(EXPERTS + 1):
        ends[e] = 0
    lax.fori_loop(0, NGRAN, count, 0)
    end = 0
    for e in range(EXPERTS):
        end += (ends[e] + PER_TILE - 1) // PER_TILE
        ends[e] = end

    def fill(g, carry):
        e = gexp[g]

        @pl.when(e < EXPERTS)
        def _():
            start = jnp.where(e > 0, ends[jnp.maximum(e - 1, 0)], 0)
            source[start * PER_TILE + rank[g]] = g

        return carry

    lax.fori_loop(0, NGRAN, fill, 0)
    acc[...] = jnp.zeros_like(acc)
    for load in loads:
        load.wait()
    tail_rows = lax.broadcasted_iota(jnp.int32, (MAIN, DC), 0) % SIDE < 2 * TAIL
    side = lax.broadcasted_iota(jnp.int32, (ROWS, MAIN), 1) // SIDE

    def expert_step(e, start):
        def tile_step(t, carry):
            xt, qt, mains, tails = [], [], ([], [], []), []
            for j in range(PER_TILE):
                found = source[t * PER_TILE + j]
                g = jnp.maximum(found, 0)
                px, h, at = g // SLOT, (g % SLOT) // PART, g % PART
                xt.append(xs[g])
                qt.append(qs[g])
                for py in range(Y):
                    for m in range(3):
                        block = hs[px, py, h, 3 * at + m]
                        mains[m].append(jnp.where(found >= 0, block, jnp.zeros_like(block)))
                    block = hs[px, py, h, 3 * PART + at % PAIRS].astype(jnp.float32)
                    mine = side == jnp.where(found >= 0, at // PAIRS, 2)
                    tails.append(jnp.where(mine, block, 0.0).astype(jnp.bfloat16))
            xt, qt = jnp.concatenate(xt, axis=0), jnp.concatenate(qt, axis=0)
            for m, rows in ((0, xt), (1, xt), (2, qt)):
                acc[e, m * MAIN : (m + 1) * MAIN] += dot_tn(jnp.concatenate(mains[m], axis=0), rows)
            tail = jnp.concatenate(tails, axis=0)
            both = jnp.where(tail_rows, dot_tn(tail, xt), dot_tn(tail, qt))
            acc[e, 3 * MAIN : GROWS] += both[:SIDE] + both[SIDE:]
            return carry

        end = ends[e]
        lax.fori_loop(start, end, tile_step, 0)
        pltpu.make_async_copy(acc.at[e], out.at[e], out_sem.at[e]).start()
        return end

    lax.fori_loop(0, EXPERTS, expert_step, 0)

    def finish(e, carry):
        pltpu.make_async_copy(acc.at[e], out.at[e], out_sem.at[e]).wait()
        return carry

    lax.fori_loop(0, EXPERTS, finish, 0)


def gradients(gexp, xg, qg, hg):
    hbm = pl.BlockSpec(memory_space=pl.ANY)
    return pl.pallas_call(
        grads_kernel,
        out_shape=jax.ShapeDtypeStruct((EXPERTS, GROWS, DC), jnp.float32),
        in_specs=[pl.BlockSpec(memory_space=pltpu.SMEM), hbm, hbm, hbm],
        out_specs=hbm,
        scratch_shapes=[
            pltpu.VMEM(xg.shape, jnp.bfloat16),
            pltpu.VMEM(qg.shape, jnp.bfloat16),
            pltpu.VMEM(hg.shape, jnp.bfloat16),
            pltpu.VMEM((EXPERTS, GROWS, DC), jnp.float32),
            pltpu.SMEM((MAX_TILES * PER_TILE,), jnp.int32),
            pltpu.SMEM((NGRAN,), jnp.int32),
            pltpu.SMEM((EXPERTS + 1,), jnp.int32),
            pltpu.SemaphoreType.DMA((3,)),
            pltpu.SemaphoreType.DMA((EXPERTS,)),
        ],
        compiler_params=pltpu.CompilerParams(vmem_limit_bytes=VMEM_LIMIT),
        name="gradients",
    )(gexp, xg, qg, hg)


QUART = HALF // 2
PACK = 96
SHARE = 54
WINDOW = 256
OFFSETS = (4, 3, -3, 2, -2, 1, -1, 0)


def reduce_kernel(
    grads, out, own, sib, sbuf, rbuf, fin, win, wide, packf, pack, got, gotf, os_sem, ts_sem, tr_sem, cs_sem, cr_sem, swap_sem, send, recv,
    keep_sem,
):
    x, y, z, k = coords()
    zh, zl = z // 4, z % 4
    sibling = device(x, y, z, 1 - k)
    barrier = pltpu.get_barrier_semaphore()

    def target(share):
        return share // 2, (share % 2) * 4 + y

    def greet_share(share, carry):
        ty, tz = target(share)

        @pl.when((ty != y) | (tz != z))
        def _():
            signal(barrier, device(x, ty, tz, k))

        return carry

    def greet_source(pz, carry):
        @pl.when((zl != y) | (pz != z))
        def _():
            signal(barrier, device(x, zl, pz, k))

        return carry

    ahead = (device(x, y, (z + 1) % Z, k), device(x, y, (z + Z - 1) % Z, k))
    signal(barrier, sibling)
    signal(barrier, ahead[0])
    signal(barrier, ahead[1])
    lax.fori_loop(0, 8, greet_share, 0)
    lax.fori_loop(0, 8, greet_source, 0)
    self_here = jnp.where(zl == y, 1, 0)
    pl.semaphore_wait(barrier, 19 - 2 * self_here)

    def half(e, which):
        return grads.at[e, pl.ds(pl.multiple_of(which * HALF, HALF), HALF), :]

    trades, keeps = {}, {}
    for i, off in enumerate(OFFSETS):
        e = (z + off + Z) % Z
        trades[off] = remote(half(e, 1 - k), sib.at[e], ts_sem.at[i], tr_sem.at[i], sibling)
        keeps[off] = pltpu.make_async_copy(half(e, k), own.at[e], os_sem.at[i])
        trades[off].start()
        keeps[off].start()
    trades[-4], keeps[-4] = trades[4], keeps[4]
    ready = set()

    def ours(off, j):
        if abs(off) % 8 == 4:
            off = 4
        if off not in ready:
            trades[off].wait_recv()
            keeps[off].wait()
            ready.add(off)
        e = (z + off + Z) % Z
        cut = slice(j * QUART, (j + 1) * QUART)
        return own[e, cut] + sib[e, cut]

    chain = {}
    for dist in (4, 3, 2, 1):
        for way in range(2):
            for j in range(2):
                longest = 4 if way == j else 3
                if dist > longest:
                    continue
                value = ours(dist if way == 0 else -dist, j)
                if dist < longest:
                    chain[way, j, dist + 1].wait_recv()
                    value += rbuf[way, j, dist].astype(jnp.float32)
                sbuf[way, j, dist - 1] = value.astype(jnp.bfloat16)
                at = (way * 2 + j) * 4 + dist - 1
                go = remote(
                    sbuf.at[way, j, dist - 1], rbuf.at[way, j, dist - 1], cs_sem.at[at], cr_sem.at[at], ahead[way]
                )
                go.start()
                chain[way, j, dist] = go
    for j in range(2):
        value = ours(0, j)
        for way in range(2):
            chain[way, j, 1].wait_recv()
            value += rbuf[way, j, 0].astype(jnp.float32)
        fin[pl.ds(pl.multiple_of(k * HALF + j * QUART, 16), QUART)] = value
    mine = fin.at[pl.ds(pl.multiple_of(k * HALF, HALF), HALF)]
    swap = remote(mine, mine, swap_sem.at[0], swap_sem.at[1], sibling)
    swap.start()
    swap.wait()

    low = fin[:, 0:WINDOW]
    high = pltpu.roll(fin[:, DC - WINDOW : DC], DC // 2, 1)
    win[...] = jnp.where(k == 0, low, high)
    first_half = lax.broadcasted_iota(jnp.int32, (SHARE // 2, MAIN), 1) < SIDE
    for share in range(8):
        for m in range(3):
            if share < 7:
                lo = m * MAIN + 18 * share
                wide[share, 18 * m : 18 * m + 18] = win[lo : lo + 18]
            else:
                lo = m * MAIN + 126
                wide[share, 18 * m : 18 * m + 2] = win[lo : lo + 2]
                lo = 3 * MAIN + m * TAIL
                wide[share, 18 * m + 2 : 18 * m + 18] = win[lo : lo + TAIL]
        packf[share, 80:PACK] = jnp.zeros((PACK - 80, MAIN), jnp.float32)
        packf[share, 0:SHARE] = wide[share, 0:SHARE, :MAIN]
        packf[share, SHARE : SHARE + SHARE // 2] = jnp.where(
            first_half,
            wide[share, 0 : SHARE // 2, MAIN:],
            pltpu.roll(wide[share, SHARE // 2 : SHARE, MAIN:], SIDE, 1),
        )
        pack[share] = packf[share].astype(jnp.bfloat16)

    def share_copy(share):
        ty, tz = target(share)
        return remote(pack.at[share], got.at[z], send.at[share], recv.at[z], device(x, ty, tz, k))

    def start(share, carry):
        ty, tz = target(share)

        @pl.when((ty != y) | (tz != z))
        def _():
            share_copy(share).start()

        @pl.when((ty == y) & (tz == z))
        def _():
            pltpu.make_async_copy(pack.at[share], got.at[z], keep_sem).start()

        return carry

    def finish_send(share, carry):
        ty, tz = target(share)

        @pl.when((ty != y) | (tz != z))
        def _():
            share_copy(share).wait_send()

        @pl.when((ty == y) & (tz == z))
        def _():
            pltpu.make_async_copy(pack.at[share], got.at[z], keep_sem).wait()

        return carry

    def finish_recv(pz, carry):
        @pl.when((zl != y) | (pz != z))
        def _():
            pltpu.make_async_copy(got.at[pz], got.at[pz], recv.at[pz]).wait()

        return carry

    lax.fori_loop(0, 8, start, 0)
    lax.fori_loop(0, 8, finish_send, 0)
    def unpack(e, carry):
        value = got[e].astype(jnp.float32)
        gotf[0:PACK, :MAIN] = value
        gotf[0 : SHARE // 2, MAIN:] = gotf[SHARE : SHARE + SHARE // 2, :MAIN]
        gotf[SHARE // 2 : SHARE, MAIN:] = pltpu.roll(gotf[SHARE : SHARE + SHARE // 2, :MAIN], SIDE, 1)
        for m in range(3):
            out[e, m] = gotf[18 * m : 18 * m + 18, : DC // 2].astype(jnp.bfloat16)
        return carry

    lax.fori_loop(0, 8, finish_recv, 0)
    lax.fori_loop(0, 8, unpack, 0)
    for off in OFFSETS:
        trades[off].wait_send()
    for go in chain.values():
        go.wait_send()


def reduce_grads(grads):
    dma = pltpu.SemaphoreType.DMA
    wide = pltpu.VMEM((EXPERTS, HALF, DC), jnp.float32)
    steps = pltpu.VMEM((2, 2, 4, QUART, DC), jnp.bfloat16)
    return pl.pallas_call(
        reduce_kernel,
        out_shape=jax.ShapeDtypeStruct((EXPERTS, 3, 18, DC // 2), jnp.bfloat16),
        in_specs=[pl.BlockSpec(memory_space=pl.ANY)],
        out_specs=pl.BlockSpec(memory_space=pltpu.VMEM),
        scratch_shapes=[
            wide,
            wide,
            steps,
            steps,
            pltpu.VMEM((GROWS, DC), jnp.float32),
            pltpu.VMEM((GROWS, WINDOW), jnp.float32),
            pltpu.VMEM((8, SHARE + 2, WINDOW), jnp.float32),
            pltpu.VMEM((8, PACK, MAIN), jnp.float32),
            pltpu.VMEM((8, PACK, MAIN), jnp.bfloat16),
            pltpu.VMEM((8, PACK, MAIN), jnp.bfloat16),
            pltpu.VMEM((PACK, WINDOW), jnp.float32),
            dma((8,)),
            dma((8,)),
            dma((8,)),
            dma((16,)),
            dma((16,)),
            dma((2,)),
            dma((8,)),
            dma((8,)),
            dma,
        ],
        compiler_params=pltpu.CompilerParams(
            collective_id=1, has_side_effects=True, vmem_limit_bytes=VMEM_LIMIT
        ),
        name="reduce_grads",
    )(grads)


def on_device(tok, cot, wts, counts, column, dest, live):
    xg, qg, hg, gexp = rows_and_hidden(counts, column, dest, live, tok, cot, wts)
    xg = xg.reshape(NGRAN, GRAN, DC)
    qg = qg.reshape(NGRAN, GRAN, DC)
    return reduce_grads(gradients(gexp, xg, qg, hg))


def solution(mesh):
    placed = (
        P("expert", "dp", None),
        P("expert", "dp", None),
        P("expert", None, None, None),
        P(),
        P(),
        P(),
        P(),
    )
    return jax.shard_map(
        on_device,
        mesh=mesh,
        in_specs=placed,
        out_specs=P(None, None, "dp", "expert"),
        check_vma=False,
    )
```

```python
import jax
import jax.numpy as jnp
from jax import lax
from jax.experimental import pallas as pl
from jax.experimental.pallas import tpu as pltpu
from jax.sharding import PartitionSpec as P

MESH = pl.DeviceIdType.MESH
EXPERTS = 8
X, Y, Z = 4, 4, 8
GROUP = X * Y
D = 6144
DC = D // GROUP
SLOT = 8
ROWS = 16
MAIN = 128
TAIL = 16
LANES = 512
GROWS = 448
HALF = GROWS // 2
GRAN = Y * ROWS
NGRAN = X * SLOT
TILE = 256
PER_TILE = TILE // GRAN
MAX_TILES = NGRAN // PER_TILE + EXPERTS - 1
VMEM_LIMIT = 56 * 1024 * 1024


def coords():
    d = lax.axis_index("dp")
    c = lax.axis_index("expert")
    return c // 8, d // 2, (d % 2) * 4 + (c // 2) % 4, c % 2


def device(x, y, z, k):
    return (y * 2 + z // 4, (x * 4 + z % 4) * 2 + k)


MOVES = (
    (1, 0), (0, 1), (3, 0), (0, 3), (2, 0), (0, 2), (1, 1), (3, 3), (1, 3), (3, 1), (2, 1), (1, 2), (2, 3), (3, 2), (2, 2),
)


def plane_peer(x, y, step):
    dx, dy = MOVES[step]
    return (x + dx) % X, (y + dy) % Y


def signal(sem, target):
    pl.semaphore_signal(sem, inc=1, device_id=target, device_id_type=MESH)


def remote(src, dst, send, recv, target):
    return pltpu.make_async_remote_copy(
        src_ref=src, dst_ref=dst, send_sem=send, recv_sem=recv, device_id=target, device_id_type=MESH
    )


def wait_bytes(ref, sem):
    pltpu.make_async_copy(ref, ref, sem).wait()


def swiglu_rows(gate, up, grad):
    sig = jax.nn.sigmoid(gate)
    act = gate * sig
    return grad * up * sig * (1.0 + gate * (1.0 - sig)), grad * act, act * up


def dot_nt(a, b):
    return lax.dot_general(a, b, (((1,), (1,)), ((), ())), preferred_element_type=jnp.float32)


def dot_tn(a, b):
    return lax.dot_general(a, b, (((0,), (0,)), ((), ())), preferred_element_type=jnp.float32)


CHUNKS = 4
PART = SLOT // CHUNKS
PAIRS = PART // 2
BLOCKS = 3 * PART + PAIRS
SIDE = 64
SUM_TYPE = jnp.float32


def rows_kernel(
    counts, column, dest, live, tok, cot, wts, xg, qg, hg, gexp, wr, sel, wg, xv, qv, p1, m1, r1, n1, rn, s2, r2, hid, xs_sem, xr_sem, qs_sem, qr_sem,
    ws_sem, wr_sem, own_sem, rs_sem, rr_sem, ls_sem, lr_sem, ss_sem, sr_sem, p1s_sem, p1r_sem, p2s_sem, p2r_sem,
    has_sem, har_sem, hbs_sem, hbr_sem, keep_sem,
):
    x, y, z, k = coords()
    zh, zl = z // 4, z % 4
    me_col = (x * 4 + zl) * 2 + k
    barrier = pltpu.get_barrier_semaphore()

    def greet_column(step, carry):
        signal(barrier, (y * 2 + zh, (me_col + step) % 32))
        return carry

    for step in range(GROUP - 1):
        px, py = plane_peer(x, y, step)
        signal(barrier, device(px, py, z, k))
    lax.fori_loop(1, 32, greet_column, 0)
    right, left = device(x, y, (z + 1) % Z, k), device(x, y, (z + Z - 1) % Z, k)
    sibling = device(x, y, z, 1 - k)
    signal(barrier, right)
    signal(barrier, left)
    pl.semaphore_wait(barrier, GROUP - 1 + 31 + 2)

    def weight_piece(col, part):
        cx, cz, ck = col // 8, zh * 4 + (col // 2) % 4, col % 2
        t = jnp.minimum((cz * 2 + ck) * 2 + part, 26)
        tail = t // 24
        m = (t // 8) * (1 - tail) + (t - 24) * tail
        row = (t % 8) * 16 * (1 - tail) + 128 * tail
        return wts.at[
            0,
            m,
            pl.ds(pl.multiple_of(row, 16), 16),
            pl.ds(pl.multiple_of((cx * Y + y) * DC, 128), DC),
        ]

    def send_weights(step, carry):
        col = (me_col + step) % 32
        for part in range(2):
            remote(
                weight_piece(col, part), wr.at[me_col, pl.ds(part * 16, 16), :], ws_sem, wr_sem, (y * 2 + zh, col)
            ).start()
        return carry

    def columns(ref, px, py):
        return ref.at[:, :, pl.ds(pl.multiple_of((px * Y + py) * DC, 128), DC)]

    def x_copy(step):
        px, py = plane_peer(x, y, step)
        return remote(
            columns(tok, px, py), xv.at[x, :, y], xs_sem.at[step], xr_sem.at[step], device(px, py, z, k)
        )

    def q_copy(step):
        px, py = plane_peer(x, y, step)
        return remote(
            columns(cot, px, py), qv.at[x, :, y], qs_sem.at[step], qr_sem.at[step], device(px, py, z, k)
        )

    for step in range(5):
        x_copy(step).start()
    lax.fori_loop(1, 32, send_weights, 0)
    for part in range(2):
        pltpu.make_async_copy(
            weight_piece(me_col, part), wr.at[me_col, pl.ds(part * 16, 16), :], wr_sem
        ).start()
    for step in range(5, GROUP - 1):
        x_copy(step).start()
    own_x = pltpu.make_async_copy(columns(tok, x, y), xv.at[x, :, y], own_sem.at[0])
    own_q = pltpu.make_async_copy(columns(cot, x, y), qv.at[x, :, y], own_sem.at[1])
    own_x.start()
    own_q.start()

    firsts, lasts = [], []
    for e in range(EXPERTS):
        firsts.append(lasts[-1] if e else 0)
        lasts.append(firsts[-1] + counts[e])

    def place_experts():
        def one(g, carry):
            col = ((g // SLOT) * 4 + zl) * 2 + k
            replica = dest[col, g % SLOT]
            expert = 0
            for e in range(EXPERTS - 1):
                expert += (lasts[e] <= replica).astype(jnp.int32)
            gexp[g] = jnp.where(g % SLOT < live[col], expert, EXPERTS)
            return carry

        lax.fori_loop(0, NGRAN, one, 0)

    wait_bytes(wr, wr_sem)
    for e in range(EXPERTS):
        sel[e] = wr[column[firsts[e]]]

    def chunk(pz):
        return wg.at[:, pl.ds(pl.multiple_of((pz * 2 + k) * 32, 32), 32), :]

    mine = chunk(z)
    own_w = pltpu.make_async_copy(sel, mine, own_sem.at[2])
    own_w.start()
    rights = [remote(sel, mine, rs_sem.at[0], rr_sem.at[0], right)]
    lefts = [remote(sel, mine, ls_sem.at[0], lr_sem.at[0], left)]
    sibs = [remote(sel, mine, ss_sem.at[0], sr_sem.at[0], sibling)]
    rights[0].start()
    lefts[0].start()
    sibs[0].start()
    for step in range(GROUP - 1):
        q_copy(step).start()
    place_experts()
    for t in range(1, 5):
        rights[t - 1].wait_recv()
        piece = chunk((z + Z - t) % Z)
        if t < 4:
            go = remote(piece, piece, rs_sem.at[t], rr_sem.at[t], right)
            go.start()
            rights.append(go)
        go = remote(piece, piece, ss_sem.at[2 * t - 1], sr_sem.at[2 * t - 1], sibling)
        go.start()
        sibs.append(go)
        if t < 4:
            lefts[t - 1].wait_recv()
            piece = chunk((z + t) % Z)
            if t < 3:
                go = remote(piece, piece, ls_sem.at[t], lr_sem.at[t], left)
                go.start()
                lefts.append(go)
            go = remote(piece, piece, ss_sem.at[2 * t], sr_sem.at[2 * t], sibling)
            go.start()
            sibs.append(go)
    for go in sibs:
        go.wait_recv()
    own_w.wait()

    for step in range(GROUP - 1):
        x_copy(step).wait_recv()
    own_x.wait()
    keep_x = pltpu.make_async_copy(xv, xg, keep_sem.at[0])
    keep_x.start()

    a_here, b_here = x * (1 - k) + y * k, x * k + y * (1 - k)

    def place(a, b):
        return a * (1 - k) + b * k, a * k + b * (1 - k)

    def plane_device(a, b):
        px, py = place(a, b)
        return device(px, py, z, k)

    lane = lax.broadcasted_iota(jnp.int32, (ROWS, MAIN), 1)
    place_in_side = lane % SIDE

    def ahead(h):
        return 1 if h % 2 == 0 else 3

    def a_device(step):
        return plane_device((a_here + step) % 4, b_here)

    def b_device(step):
        return plane_device(a_here, (b_here + step) % 4)

    def first_copy(h, kind, src, dst, step):
        at = h * 3 + kind
        return remote(src, dst, p1s_sem.at[at], p1r_sem.at[at], a_device(step))

    def far_copy(h):
        return first_copy(h, 0, n1.at[h, 0], rn.at[h, 0], ahead(h))

    def sum_copy(h):
        return first_copy(h, 1, m1.at[h], r1.at[h], ahead(h))

    def near_copy(h):
        return first_copy(h, 2, n1.at[h, 1], rn.at[h, 1], 4 - ahead(h))

    def second_copy(h, j):
        b = (b_here + j) % 4
        at = h * 3 + j - 1
        return remote(s2.at[b, h], r2.at[b_here, h], p2s_sem.at[at], p2r_sem.at[at], plane_device(a_here, b))

    def hidden_place(a, b, h):
        px, py = place(a, b)
        return hg.at[px, py, h]

    def hidden_first(h, j):
        at = h * 3 + j - 1
        return remote(
            hid.at[h], hidden_place(a_here, b_here, h), has_sem.at[at], har_sem.at[at], a_device(j)
        )

    def hidden_near(h, j, step):
        at = (h * 4 + j) * 3 + (0 if step == 1 else 1)
        here = hidden_place((a_here + 4 - j) % 4, b_here, h)
        return remote(hid.at[h] if j == 0 else here, here, hbs_sem.at[at], hbr_sem.at[at], b_device(step))

    def hidden_far(h, j):
        at = (h * 4 + j) * 3 + 2
        here = hidden_place((a_here + 4 - j) % 4, (b_here + 4 - ahead(h)) % 4, h)
        return remote(here, here, hbs_sem.at[at], hbr_sem.at[at], b_device(ahead(h)))

    def hidden_keep(h):
        return pltpu.make_async_copy(hid.at[h], hidden_place(a_here, b_here, h), keep_sem.at[2 + h])

    def put_rows(px, h, block, value):
        for py in range(Y):
            pa, pb = px * (1 - k) + py * k, px * k + py * (1 - k)
            p1[pa, h, pb, block] = value[py * ROWS : (py + 1) * ROWS].astype(SUM_TYPE)

    lanes = lax.broadcasted_iota(jnp.int32, (GRAN, MAIN), 1)

    def side_by_side(tails):
        return jnp.where(lanes < SIDE, tails[0], pltpu.roll(tails[1], SIDE, 1))

    def project_x(i, carry):
        px, h, pair = i // (CHUNKS * PAIRS), (i // PAIRS) % CHUNKS, i % PAIRS
        tails = []
        for side in range(2):
            at = pair + side * PAIRS
            s = h * PART + at
            e = jnp.minimum(gexp[px * SLOT + s], EXPERTS - 1)
            xt = xv[px, s].reshape(GRAN, DC)
            main = dot_nt(xt, wg[e, 0 : 2 * MAIN])
            put_rows(px, h, 3 * at, main[:, :MAIN])
            put_rows(px, h, 3 * at + 1, main[:, MAIN:])
            tails.append(dot_nt(xt, wg[e, 3 * MAIN : LANES]))
        put_rows(px, h, 3 * PART + pair, side_by_side(tails))
        return carry

    lax.fori_loop(0, X * CHUNKS * PAIRS, project_x, 0)
    for step in range(GROUP - 1):
        q_copy(step).wait_recv()
    own_q.wait()
    keep_q = pltpu.make_async_copy(qv, qg, keep_sem.at[1])
    keep_q.start()
    for h in range(CHUNKS):

        def project_q(i, carry):
            px, pair = i // PAIRS, i % PAIRS
            tails = []
            for side in range(2):
                at = pair + side * PAIRS
                s = h * PART + at
                e = jnp.minimum(gexp[px * SLOT + s], EXPERTS - 1)
                rows = dot_nt(qv[px, s].reshape(GRAN, DC), wg[e, 2 * MAIN : LANES])
                put_rows(px, h, 3 * at + 2, rows[:, :MAIN])
                tails.append(rows[:, MAIN:])
            tail = side_by_side(tails).astype(SUM_TYPE)
            for py in range(Y):
                pa, pb = px * (1 - k) + py * k, px * k + py * (1 - k)
                at = (pa, h, pb, 3 * PART + pair)
                p1[at] = jnp.where(place_in_side < 2 * TAIL, p1[at], tail[py * ROWS : (py + 1) * ROWS])
            return carry

        lax.fori_loop(0, X * PAIRS, project_q, 0)

        def narrow(b, carry):
            n1[h, 0, b] = p1[(a_here + 2) % 4, h, b].astype(jnp.bfloat16)
            n1[h, 1, b] = p1[(a_here + 4 - ahead(h)) % 4, h, b].astype(jnp.bfloat16)
            return carry

        lax.fori_loop(0, 4, narrow, 0)
        far_copy(h).start()
        near_copy(h).start()

    for h in range(CHUNKS):
        far_copy(h).wait_recv()

        def relay(b, carry):
            m1[h, b] = p1[(a_here + ahead(h)) % 4, h, b] + rn[h, 0, b].astype(jnp.float32)
            return carry

        lax.fori_loop(0, 4, relay, 0)
        sum_copy(h).start()

    for h in range(CHUNKS):
        near_copy(h).wait_recv()
        sum_copy(h).wait_recv()

        def sum_first(b, carry):
            s2[b, h] = p1[a_here, h, b] + r1[h, b] + rn[h, 1, b].astype(jnp.float32)
            return carry

        lax.fori_loop(0, 4, sum_first, 0)
        for j in (2, 1, 3):
            second_copy(h, j).start()

    def shift(v, amount):
        return pltpu.roll(v, amount % MAIN, 1)

    for h in range(CHUNKS):
        for j in (1, 2, 3):
            second_copy(h, j).wait_recv()

        def total(block):
            value = s2[b_here, h, block]
            for j in (1, 2, 3):
                value += r2[(b_here + j) % 4, h, block]
            return value

        for at in range(PART):
            for m, value in enumerate(swiglu_rows(total(3 * at), total(3 * at + 1), total(3 * at + 2))):
                hid[h, 3 * at + m] = value.astype(jnp.bfloat16)
        for pair in range(PAIRS):
            tail = total(3 * PART + pair)
            first, second, third = swiglu_rows(tail, shift(tail, -TAIL), shift(tail, -2 * TAIL))
            packed = jnp.where(
                place_in_side < TAIL,
                first,
                jnp.where(place_in_side < 2 * TAIL, shift(second, TAIL), shift(third, 2 * TAIL)),
            )
            hid[h, 3 * PART + pair] = jnp.where(place_in_side < 3 * TAIL, packed, 0.0).astype(jnp.bfloat16)
        for j in (2, 1, 3):
            hidden_first(h, j).start()
        for step in (1, 3):
            hidden_near(h, 0, step).start()
        hidden_keep(h).start()

    def pass_on(h, j):
        hidden_first(h, j).wait_recv()
        for step in (1, 3):
            hidden_near(h, j, step).start()

    def pass_far(h, j):
        hidden_near(h, j, ahead(h)).wait_recv()
        hidden_far(h, j).start()

    for h in range(CHUNKS):
        for j in (1, 3, 2):
            pass_on(h, j)
    for h in range(CHUNKS):
        for j in (0, 1, 3, 2):
            pass_far(h, j)
    for h in range(CHUNKS):
        for j in range(4):
            hidden_near(h, j, 4 - ahead(h)).wait_recv()
            hidden_far(h, j).wait_recv()
    for h in range(CHUNKS):
        for j in range(4):
            for step in (1, 3):
                hidden_near(h, j, step).wait_send()
            hidden_far(h, j).wait_send()
        for j in (1, 2, 3):
            hidden_first(h, j).wait_send()
            second_copy(h, j).wait_send()
        far_copy(h).wait_send()
        near_copy(h).wait_send()
        sum_copy(h).wait_send()
        hidden_keep(h).wait()
    for step in range(GROUP - 1):
        x_copy(step).wait_send()
        q_copy(step).wait_send()
    for go in rights + lefts + sibs:
        go.wait_send()
    wait_bytes(wr.at[pl.ds(0, 31)], ws_sem)
    keep_x.wait()
    keep_q.wait()


def rows_and_hidden(counts, column, dest, live, tok, cot, wts):
    hbm = pl.BlockSpec(memory_space=pl.ANY)
    smem = pl.BlockSpec(memory_space=pltpu.SMEM)
    dma = pltpu.SemaphoreType.DMA
    spread = pltpu.VMEM((X, SLOT, Y, ROWS, DC), jnp.bfloat16)
    sums = pltpu.VMEM((4, CHUNKS, 4, BLOCKS, ROWS, MAIN), SUM_TYPE)
    relayed = pltpu.VMEM((CHUNKS, 4, BLOCKS, ROWS, MAIN), SUM_TYPE)
    narrow = pltpu.VMEM((CHUNKS, 2, 4, BLOCKS, ROWS, MAIN), jnp.bfloat16)
    halfway = pltpu.VMEM((4, CHUNKS, BLOCKS, ROWS, MAIN), jnp.float32)
    return pl.pallas_call(
        rows_kernel,
        out_shape=(
            jax.ShapeDtypeStruct((X, SLOT, Y, ROWS, DC), jnp.bfloat16),
            jax.ShapeDtypeStruct((X, SLOT, Y, ROWS, DC), jnp.bfloat16),
            jax.ShapeDtypeStruct((X, Y, CHUNKS, BLOCKS, ROWS, MAIN), jnp.bfloat16),
            jax.ShapeDtypeStruct((NGRAN,), jnp.int32),
        ),
        in_specs=[smem, smem, smem, smem, hbm, hbm, hbm],
        out_specs=(hbm, hbm, pl.BlockSpec(memory_space=pltpu.VMEM), smem),
        scratch_shapes=[
            pltpu.VMEM((32, 32, DC), jnp.bfloat16),
            pltpu.VMEM((EXPERTS, 32, DC), jnp.bfloat16),
            pltpu.VMEM((EXPERTS, LANES, DC), jnp.bfloat16),
            spread,
            spread,
            sums,
            relayed,
            relayed,
            narrow,
            narrow,
            halfway,
            halfway,
            pltpu.VMEM((CHUNKS, BLOCKS, ROWS, MAIN), jnp.bfloat16),
            dma((GROUP,)),
            dma((GROUP,)),
            dma((GROUP,)),
            dma((GROUP,)),
            dma,
            dma,
            dma((3,)),
            dma((4,)),
            dma((4,)),
            dma((3,)),
            dma((3,)),
            dma((8,)),
            dma((8,)),
            dma((3 * CHUNKS,)),
            dma((3 * CHUNKS,)),
            dma((3 * CHUNKS,)),
            dma((3 * CHUNKS,)),
            dma((3 * CHUNKS,)),
            dma((3 * CHUNKS,)),
            dma((12 * CHUNKS,)),
            dma((12 * CHUNKS,)),
            dma((2 + CHUNKS,)),
        ],
        compiler_params=pltpu.CompilerParams(
            collective_id=0, has_side_effects=True, vmem_limit_bytes=VMEM_LIMIT
        ),
        name="rows_and_hidden",
    )(counts, column, dest, live, tok, cot, wts)


def grads_kernel(gexp, xg, qg, hg, out, xs, qs, hs, acc, source, rank, ends, in_sem, out_sem):
    loads = [
        pltpu.make_async_copy(ref, held, in_sem.at[i]) for i, (ref, held) in enumerate(((hg, hs), (xg, xs), (qg, qs)))
    ]
    for load in loads:
        load.start()

    def clear(at, carry):
        source[at] = -1
        return carry

    def count(g, carry):
        e = gexp[g]
        rank[g] = ends[e]
        ends[e] = ends[e] + 1
        return carry

    lax.fori_loop(0, MAX_TILES * PER_TILE, clear, 0)
    for e in range(EXPERTS + 1):
        ends[e] = 0
    lax.fori_loop(0, NGRAN, count, 0)
    end = 0
    for e in range(EXPERTS):
        end += (ends[e] + PER_TILE - 1) // PER_TILE
        ends[e] = end

    def fill(g, carry):
        e = gexp[g]

        @pl.when(e < EXPERTS)
        def _():
            start = jnp.where(e > 0, ends[jnp.maximum(e - 1, 0)], 0)
            source[start * PER_TILE + rank[g]] = g

        return carry

    lax.fori_loop(0, NGRAN, fill, 0)
    acc[...] = jnp.zeros_like(acc)
    for load in loads:
        load.wait()
    tail_rows = lax.broadcasted_iota(jnp.int32, (MAIN, DC), 0) % SIDE < 2 * TAIL
    side = lax.broadcasted_iota(jnp.int32, (ROWS, MAIN), 1) // SIDE

    def expert_step(e, start):
        def tile_step(t, carry):
            xt, qt, mains, tails = [], [], ([], [], []), []
            for j in range(PER_TILE):
                found = source[t * PER_TILE + j]
                g = jnp.maximum(found, 0)
                px, h, at = g // SLOT, (g % SLOT) // PART, g % PART
                xt.append(xs[g])
                qt.append(qs[g])
                for py in range(Y):
                    for m in range(3):
                        block = hs[px, py, h, 3 * at + m]
                        mains[m].append(jnp.where(found >= 0, block, jnp.zeros_like(block)))
                    block = hs[px, py, h, 3 * PART + at % PAIRS].astype(jnp.float32)
                    mine = side == jnp.where(found >= 0, at // PAIRS, 2)
                    tails.append(jnp.where(mine, block, 0.0).astype(jnp.bfloat16))
            xt, qt = jnp.concatenate(xt, axis=0), jnp.concatenate(qt, axis=0)
            for m, rows in ((0, xt), (1, xt), (2, qt)):
                acc[e, m * MAIN : (m + 1) * MAIN] += dot_tn(jnp.concatenate(mains[m], axis=0), rows)
            tail = jnp.concatenate(tails, axis=0)
            both = jnp.where(tail_rows, dot_tn(tail, xt), dot_tn(tail, qt))
            acc[e, 3 * MAIN : GROWS] += both[:SIDE] + both[SIDE:]
            return carry

        end = ends[e]
        lax.fori_loop(start, end, tile_step, 0)
        pltpu.make_async_copy(acc.at[e], out.at[e], out_sem.at[e]).start()
        return end

    lax.fori_loop(0, EXPERTS, expert_step, 0)

    def finish(e, carry):
        pltpu.make_async_copy(acc.at[e], out.at[e], out_sem.at[e]).wait()
        return carry

    lax.fori_loop(0, EXPERTS, finish, 0)


def gradients(gexp, xg, qg, hg):
    hbm = pl.BlockSpec(memory_space=pl.ANY)
    return pl.pallas_call(
        grads_kernel,
        out_shape=jax.ShapeDtypeStruct((EXPERTS, GROWS, DC), jnp.float32),
        in_specs=[pl.BlockSpec(memory_space=pltpu.SMEM), hbm, hbm, hbm],
        out_specs=hbm,
        scratch_shapes=[
            pltpu.VMEM(xg.shape, jnp.bfloat16),
            pltpu.VMEM(qg.shape, jnp.bfloat16),
            pltpu.VMEM(hg.shape, jnp.bfloat16),
            pltpu.VMEM((EXPERTS, GROWS, DC), jnp.float32),
            pltpu.SMEM((MAX_TILES * PER_TILE,), jnp.int32),
            pltpu.SMEM((NGRAN,), jnp.int32),
            pltpu.SMEM((EXPERTS + 1,), jnp.int32),
            pltpu.SemaphoreType.DMA((3,)),
            pltpu.SemaphoreType.DMA((EXPERTS,)),
        ],
        compiler_params=pltpu.CompilerParams(vmem_limit_bytes=VMEM_LIMIT),
        name="gradients",
    )(gexp, xg, qg, hg)


QUART = HALF // 2
PACK = 96
SHARE = 54
WINDOW = 256
OFFSETS = (4, 3, -3, 2, -2, 1, -1, 0)


def reduce_kernel(
    grads, out, own, sib, sbuf, rbuf, fin, win, wide, packf, pack, got, gotf, os_sem, ts_sem, tr_sem, cs_sem, cr_sem, swap_sem, send, recv,
    keep_sem,
):
    x, y, z, k = coords()
    zh, zl = z // 4, z % 4
    sibling = device(x, y, z, 1 - k)
    barrier = pltpu.get_barrier_semaphore()

    def target(share):
        return share // 2, (share % 2) * 4 + y

    def greet_share(share, carry):
        ty, tz = target(share)

        @pl.when((ty != y) | (tz != z))
        def _():
            signal(barrier, device(x, ty, tz, k))

        return carry

    def greet_source(pz, carry):
        @pl.when((zl != y) | (pz != z))
        def _():
            signal(barrier, device(x, zl, pz, k))

        return carry

    ahead = (device(x, y, (z + 1) % Z, k), device(x, y, (z + Z - 1) % Z, k))
    signal(barrier, sibling)
    signal(barrier, ahead[0])
    signal(barrier, ahead[1])
    lax.fori_loop(0, 8, greet_share, 0)
    lax.fori_loop(0, 8, greet_source, 0)
    self_here = jnp.where(zl == y, 1, 0)
    pl.semaphore_wait(barrier, 19 - 2 * self_here)

    def half(e, which):
        return grads.at[e, pl.ds(pl.multiple_of(which * HALF, HALF), HALF), :]

    trades, keeps = {}, {}
    for i, off in enumerate(OFFSETS):
        e = (z + off + Z) % Z
        trades[off] = remote(half(e, 1 - k), sib.at[e], ts_sem.at[i], tr_sem.at[i], sibling)
        keeps[off] = pltpu.make_async_copy(half(e, k), own.at[e], os_sem.at[i])
        trades[off].start()
        keeps[off].start()
    trades[-4], keeps[-4] = trades[4], keeps[4]
    ready = set()

    def ours(off, j):
        if abs(off) % 8 == 4:
            off = 4
        if off not in ready:
            trades[off].wait_recv()
            keeps[off].wait()
            ready.add(off)
        e = (z + off + Z) % Z
        cut = slice(j * QUART, (j + 1) * QUART)
        return own[e, cut] + sib[e, cut]

    chain = {}
    for dist in (4, 3, 2, 1):
        for way in range(2):
            for j in range(2):
                longest = 4 if way == j else 3
                if dist > longest:
                    continue
                value = ours(dist if way == 0 else -dist, j)
                if dist < longest:
                    chain[way, j, dist + 1].wait_recv()
                    value += rbuf[way, j, dist].astype(jnp.float32)
                sbuf[way, j, dist - 1] = value.astype(jnp.bfloat16)
                at = (way * 2 + j) * 4 + dist - 1
                go = remote(
                    sbuf.at[way, j, dist - 1], rbuf.at[way, j, dist - 1], cs_sem.at[at], cr_sem.at[at], ahead[way]
                )
                go.start()
                chain[way, j, dist] = go
    for j in range(2):
        value = ours(0, j)
        for way in range(2):
            chain[way, j, 1].wait_recv()
            value += rbuf[way, j, 0].astype(jnp.float32)
        fin[pl.ds(pl.multiple_of(k * HALF + j * QUART, 16), QUART)] = value
    mine = fin.at[pl.ds(pl.multiple_of(k * HALF, HALF), HALF)]
    swap = remote(mine, mine, swap_sem.at[0], swap_sem.at[1], sibling)
    swap.start()
    swap.wait()

    low = fin[:, 0:WINDOW]
    high = pltpu.roll(fin[:, DC - WINDOW : DC], DC // 2, 1)
    win[...] = jnp.where(k == 0, low, high)
    first_half = lax.broadcasted_iota(jnp.int32, (SHARE // 2, MAIN), 1) < SIDE
    for share in range(8):
        for m in range(3):
            if share < 7:
                lo = m * MAIN + 18 * share
                wide[share, 18 * m : 18 * m + 18] = win[lo : lo + 18]
            else:
                lo = m * MAIN + 126
                wide[share, 18 * m : 18 * m + 2] = win[lo : lo + 2]
                lo = 3 * MAIN + m * TAIL
                wide[share, 18 * m + 2 : 18 * m + 18] = win[lo : lo + TAIL]
        packf[share, 80:PACK] = jnp.zeros((PACK - 80, MAIN), jnp.float32)
        packf[share, 0:SHARE] = wide[share, 0:SHARE, :MAIN]
        packf[share, SHARE : SHARE + SHARE // 2] = jnp.where(
            first_half,
            wide[share, 0 : SHARE // 2, MAIN:],
            pltpu.roll(wide[share, SHARE // 2 : SHARE, MAIN:], SIDE, 1),
        )
        pack[share] = packf[share].astype(jnp.bfloat16)

    def share_copy(share):
        ty, tz = target(share)
        return remote(pack.at[share], got.at[z], send.at[share], recv.at[z], device(x, ty, tz, k))

    def start(share, carry):
        ty, tz = target(share)

        @pl.when((ty != y) | (tz != z))
        def _():
            share_copy(share).start()

        @pl.when((ty == y) & (tz == z))
        def _():
            pltpu.make_async_copy(pack.at[share], got.at[z], keep_sem).start()

        return carry

    def finish_send(share, carry):
        ty, tz = target(share)

        @pl.when((ty != y) | (tz != z))
        def _():
            share_copy(share).wait_send()

        @pl.when((ty == y) & (tz == z))
        def _():
            pltpu.make_async_copy(pack.at[share], got.at[z], keep_sem).wait()

        return carry

    def finish_recv(pz, carry):
        @pl.when((zl != y) | (pz != z))
        def _():
            pltpu.make_async_copy(got.at[pz], got.at[pz], recv.at[pz]).wait()

        return carry

    lax.fori_loop(0, 8, lambda i, carry: start((i + z) % 8, carry), 0)
    lax.fori_loop(0, 8, finish_send, 0)
    def unpack(e, carry):
        value = got[e].astype(jnp.float32)
        gotf[0:PACK, :MAIN] = value
        gotf[0 : SHARE // 2, MAIN:] = gotf[SHARE : SHARE + SHARE // 2, :MAIN]
        gotf[SHARE // 2 : SHARE, MAIN:] = pltpu.roll(gotf[SHARE : SHARE + SHARE // 2, :MAIN], SIDE, 1)
        for m in range(3):
            out[e, m] = gotf[18 * m : 18 * m + 18, : DC // 2].astype(jnp.bfloat16)
        return carry

    lax.fori_loop(0, 8, finish_recv, 0)
    lax.fori_loop(0, 8, unpack, 0)
    for off in OFFSETS:
        trades[off].wait_send()
    for go in chain.values():
        go.wait_send()


def reduce_grads(grads):
    dma = pltpu.SemaphoreType.DMA
    wide = pltpu.VMEM((EXPERTS, HALF, DC), jnp.float32)
    steps = pltpu.VMEM((2, 2, 4, QUART, DC), jnp.bfloat16)
    return pl.pallas_call(
        reduce_kernel,
        out_shape=jax.ShapeDtypeStruct((EXPERTS, 3, 18, DC // 2), jnp.bfloat16),
        in_specs=[pl.BlockSpec(memory_space=pl.ANY)],
        out_specs=pl.BlockSpec(memory_space=pltpu.VMEM),
        scratch_shapes=[
            wide,
            wide,
            steps,
            steps,
            pltpu.VMEM((GROWS, DC), jnp.float32),
            pltpu.VMEM((GROWS, WINDOW), jnp.float32),
            pltpu.VMEM((8, SHARE + 2, WINDOW), jnp.float32),
            pltpu.VMEM((8, PACK, MAIN), jnp.float32),
            pltpu.VMEM((8, PACK, MAIN), jnp.bfloat16),
            pltpu.VMEM((8, PACK, MAIN), jnp.bfloat16),
            pltpu.VMEM((PACK, WINDOW), jnp.float32),
            dma((8,)),
            dma((8,)),
            dma((8,)),
            dma((16,)),
            dma((16,)),
            dma((2,)),
            dma((8,)),
            dma((8,)),
            dma,
        ],
        compiler_params=pltpu.CompilerParams(
            collective_id=1, has_side_effects=True, vmem_limit_bytes=VMEM_LIMIT
        ),
        name="reduce_grads",
    )(grads)


def on_device(tok, cot, wts, counts, column, dest, live):
    xg, qg, hg, gexp = rows_and_hidden(counts, column, dest, live, tok, cot, wts)
    xg = xg.reshape(NGRAN, GRAN, DC)
    qg = qg.reshape(NGRAN, GRAN, DC)
    return reduce_grads(gradients(gexp, xg, qg, hg))


def solution(mesh):
    placed = (
        P("expert", "dp", None),
        P("expert", "dp", None),
        P("expert", None, None, None),
        P(),
        P(),
        P(),
        P(),
    )
    return jax.shard_map(
        on_device,
        mesh=mesh,
        in_specs=placed,
        out_specs=P(None, None, "dp", "expert"),
        check_vma=False,
    )
```
